128 devices in a mesh: dp: 64 (over x_hi, z, y, core), mp: 2 (over x_lo).
Axes of the slice: x: 4 (x_hi: 2, x_lo: 2; x = x_hi * 2 + x_lo), y: 4, z: 4, core: 2. Of those that a mesh axis runs over, the one named last changes fastest.
Arguments:
- hidden_in: bfloat16 [65536, 768], P('dp'), may hold values from -6 to 6
- buckets: int32 [64, 2], P('dp'), may hold values from 0 to 2, as said below
- lengths: int32 [64, 2, 4], P('dp'), may hold values from 0 to 512, as said below
- query_weight: bfloat16 [768, 768], P('dp', 'mp'), may hold values from -0.21875 to 0.21875
- key_weight: bfloat16 [768, 768], P('dp', 'mp'), may hold values from -0.21875 to 0.21875
- value_weight: bfloat16 [768, 768], P('dp', 'mp'), may hold values from -0.21875 to 0.21875
- query_bias: float32 [768], P('mp'), may hold values from -3 to 3
- value_bias: float32 [768], P('mp'), may hold values from -3 to 3
- output_weight: bfloat16 [768, 768], P('mp', 'dp'), may hold values from -1.75 to 1.75
- output_bias: float32 [768], replicated, may hold values from -3 to 3
- first_gain: float32 [768], replicated, may hold values from 0.5 to 1.5
- first_shift: float32 [768], replicated, may hold values from -3 to 3
- inner_weight: bfloat16 [768, 3072], P('dp', 'mp'), may hold values from -0.21875 to 0.21875
- inner_bias: float32 [3072], P('mp'), may hold values from -3 to 3
- outer_weight: bfloat16 [3072, 768], P('mp', 'dp'), may hold values from -0.15625 to 0.15625
- outer_bias: float32 [768], replicated, may hold values from -3 to 3
- second_gain: float32 [768], replicated, may hold values from 0.5 to 1.5
- second_shift: float32 [768], replicated, may hold values from -3 to 3
- cotangent: bfloat16 [65536, 768], P('dp'), may hold values from -6 to 6
Outputs:
- layer_out: bfloat16 [65536, 768], P('dp')
- input_grad: float32 [65536, 768], P('dp')
- grad_query_weight: float32 [768, 768], P('dp', 'mp')
- grad_key_weight: float32 [768, 768], P('dp', 'mp')
- grad_value_weight: float32 [768, 768], P('dp', 'mp')
- grad_query_bias: float32 [768], P('mp')
- grad_value_bias: float32 [768], P('mp')
- grad_output_weight: float32 [768, 768], P('mp', 'dp')
- grad_output_bias: float32 [768], replicated
- grad_first_gain: float32 [768], replicated
- grad_first_shift: float32 [768], replicated
- grad_inner_weight: float32 [768, 3072], P('dp', 'mp')
- grad_inner_bias: float32 [3072], P('mp')
- grad_outer_weight: float32 [3072, 768], P('mp', 'dp')
- grad_outer_bias: float32 [768], replicated
- grad_second_gain: float32 [768], replicated
- grad_second_shift: float32 [768], replicated
The draws below stay inside these ranges and needn't reach their ends.
Inputs may be any that keep to these rules, and one draw needn't show every extreme that they name: Rows of a block have 128 * 2**buckets tokens, so a block holds 4 >> buckets rows. `lengths`: entry r of a block is the live tokens of its row r: for rows that exist it lies between the row's length // 8 (at least 1) and the row's length, and one row of every block is full; entries for rows that don't exist are 0.
All inputs are finite; a program needn't handle non-finite values.
Results may differ from the reference program's by a relative error of at most 0.014.
The reference program's roundings to bfloat16 on the way count: a program that leaves them out, or rounds other values in their place, can miss the bound.
Values may be sent and summed in bfloat16 or wider, within the bound.
No kernel may reach another device: no remote copies, remote signals or barrier semaphores. Data moves between devices by JAX's collectives and lax.ppermute only.
A program may use at most 192 MiB of HBM per device.

```python
import jax
import jax.numpy as jnp
from jax import lax

D = 768
H = 12
DH = 64
FF = 3072
BASE_ROW_TOKENS = 128
MB = 2
MICRO_TOKENS = 512
TOKENS = 65536
N_DP = 64


def bucket_codes(key):
    return jax.random.randint(jax.random.fold_in(key, 17), (N_DP, MB), 0, 3).astype(jnp.int32)


def draw_buckets(key, part):
    return bucket_codes(key)


def draw_lengths(key, part):
    codes = bucket_codes(key)
    row_positions = MICRO_TOKENS // BASE_ROW_TOKENS
    length_multiple = jnp.where(codes == 0, 1, jnp.where(codes == 1, 2, 4)).astype(jnp.int32)
    single_row_length = BASE_ROW_TOKENS * length_multiple
    row_count = row_positions // length_multiple
    lowest = jnp.maximum(single_row_length // 8, 1)
    full_row = jax.random.randint(jax.random.fold_in(key, 23), (N_DP, MB), 0, row_count)
    drawn = jax.random.randint(jax.random.fold_in(key, 29), (N_DP, MB, row_positions), lowest[:, :, None], single_row_length[:, :, None] + 1)
    place = jnp.arange(row_positions, dtype=jnp.int32)[None, None, :]
    chosen = jnp.where(place == full_row[:, :, None], single_row_length[:, :, None], drawn)
    return jnp.where(place < row_count[:, :, None], chosen, 0).astype(jnp.int32)


def level_of(stream_key, extent, cuts, smallest, largest):
    level, own = 1.0, jax.random.fold_in(stream_key, 6)
    for position, blocks in cuts:
        steps = jnp.exp(jax.random.uniform(jax.random.fold_in(own, position), (blocks,), jnp.float32, smallest / len(cuts), largest / len(cuts)))
        level = level * jnp.repeat(steps, extent[position] // blocks).reshape([-1 if axis == position else 1 for axis in range(len(extent))])
    return level


def noise(key, extent, scale, bound, shards=(), held_as=jnp.bfloat16):
    values = scale * jax.random.normal(key, extent, jnp.float32)
    if shards:
        values = values * level_of(key, extent, shards, -0.22, 0.18)
    return jnp.clip(values, -bound, bound).astype(held_as)


def setup_inputs(seed: int = 0) -> dict:
    seeds = jax.random.split(jax.random.key(seed), 20)
    return {
        "hidden_in": noise(seeds[0], (TOKENS, D), 1.0, 6.0, ((0, 64),)),
        "buckets": draw_buckets(jax.random.fold_in(seeds[19], 71), 0),
        "lengths": draw_lengths(jax.random.fold_in(seeds[19], 71), 0),
        "query_weight": noise(seeds[3], (D, D), D ** -0.5, 0.21875, ((0, 64), (1, 2))),
        "key_weight": noise(seeds[4], (D, D), D ** -0.5, 0.21875, ((0, 64), (1, 2))),
        "value_weight": noise(seeds[5], (D, D), D ** -0.5, 0.21875, ((0, 64), (1, 2))),
        "query_bias": noise(seeds[6], (D,), 0.5, 3.0, ((0, 2),), jnp.float32),
        "value_bias": noise(seeds[7], (D,), 0.5, 3.0, ((0, 2),), jnp.float32),
        "output_weight": noise(seeds[8], (D, D), (D // 64) ** -0.5, 1.75, ((0, 2), (1, 64))),
        "output_bias": noise(seeds[9], (D,), 0.5, 3.0, (), jnp.float32),
        "first_gain": jnp.clip(1.0 + 0.1 * jax.random.normal(seeds[10], (D,), jnp.float32), 0.5, 1.5),
        "first_shift": noise(seeds[11], (D,), 0.5, 3.0, (), jnp.float32),
        "inner_weight": noise(seeds[12], (D, FF), D ** -0.5, 0.21875, ((0, 64), (1, 2))),
        "inner_bias": noise(seeds[13], (FF,), 0.5, 3.0, ((0, 2),), jnp.float32),
        "outer_weight": noise(seeds[14], (FF, D), (FF // 2) ** -0.5, 0.15625, ((0, 2), (1, 64))),
        "outer_bias": noise(seeds[15], (D,), 0.5, 3.0, (), jnp.float32),
        "second_gain": jnp.clip(1.0 + 0.1 * jax.random.normal(seeds[16], (D,), jnp.float32), 0.5, 1.5),
        "second_shift": noise(seeds[17], (D,), 0.5, 3.0, (), jnp.float32),
        "cotangent": noise(seeds[18], (TOKENS, D), 1.0, 6.0, ((0, 64),)),
    }


@jax.custom_vjp
def low(v):
    return lax.optimization_barrier(v.astype(jnp.bfloat16)).astype(jnp.float32)

@jax.custom_vjp
def low_back(v):
    return v

def low_keep(v):
    return (low(v), None)

def low_pass(kept, grad):
    return (grad,)

def back_keep(v):
    return (v, None)

def back_low(kept, grad):
    return (low(grad),)
low.defvjp(low_keep, low_pass)
low_back.defvjp(back_keep, back_low)
EPS = 1e-12
HIGHEST = lax.Precision.HIGHEST

def matmul(left, right):
    return jnp.dot(left, right, precision=HIGHEST)

def layer_norm(values, gain, shift):
    average = lax.optimization_barrier(jnp.mean(values, axis=-1, keepdims=True))
    centred = values - average
    variance = lax.optimization_barrier(jnp.mean(centred * centred, axis=-1, keepdims=True))
    return centred * lax.rsqrt(variance + EPS) * gain + shift

def permitted_pairs(bucket_label, per_row_lengths):
    place = jnp.arange(MICRO_TOKENS, dtype=jnp.int32)
    length_multiple = jnp.where(bucket_label == 0, 1, jnp.where(bucket_label == 1, 2, 4)).astype(jnp.int32)
    single_row_length = (BASE_ROW_TOKENS * length_multiple).astype(jnp.int32)
    row_index = (place // single_row_length).astype(jnp.int32)
    within = place - row_index * single_row_length
    row_positions = jnp.arange(MICRO_TOKENS // BASE_ROW_TOKENS, dtype=jnp.int32)
    live_count = lax.optimization_barrier(jnp.sum(jnp.where(row_index[:, None] == row_positions[None, :], per_row_lengths[None, :], 0), axis=1)).astype(jnp.int32)
    key_live = within < live_count
    return (row_index[:, None] == row_index[None, :]) & key_live[None, :]

def block_forward(weights, inputs, bucket_label, per_row_lengths):
    query_weight, key_weight, value_weight, query_bias, value_bias, output_weight, output_bias, first_gain, first_shift, inner_weight, inner_bias, outer_weight, outer_bias, second_gain, second_shift = weights
    permitted_set = permitted_pairs(bucket_label, per_row_lengths)
    queries = low_back(low(matmul(inputs, query_weight) + query_bias))
    keys = low_back(low(matmul(inputs, key_weight)))
    values = low_back(low(matmul(inputs, value_weight) + value_bias))
    query_heads = queries.reshape(MICRO_TOKENS, H, DH)
    key_heads = keys.reshape(MICRO_TOKENS, H, DH)
    value_heads = values.reshape(MICRO_TOKENS, H, DH)
    scores = low_back(jnp.einsum('qhd,khd->hqk', query_heads, key_heads, precision=HIGHEST) * DH ** (-0.5))
    masked = jnp.where(permitted_set[None], scores, -1e+30)
    probs = low(jax.nn.softmax(masked, axis=-1))
    context = low_back(low(jnp.einsum('hqk,khd->qhd', probs, value_heads, precision=HIGHEST).reshape(MICRO_TOKENS, D)))
    attended = low_back(matmul(context, output_weight) + output_bias)
    first_low = low(layer_norm(inputs + attended, first_gain, first_shift))
    inner = low_back(matmul(first_low, inner_weight) + inner_bias)
    activated = low(jax.nn.gelu(inner, approximate=False))
    outer = low_back(matmul(activated, outer_weight) + outer_bias)
    return layer_norm(first_low + outer, second_gain, second_shift)

def reference(hidden_in, buckets, lengths, query_weight, key_weight, value_weight, query_bias, value_bias, output_weight, output_bias, first_gain, first_shift, inner_weight, inner_bias, outer_weight, outer_bias, second_gain, second_shift, cotangent):
    weights = tuple((item.astype(jnp.float32) for item in (query_weight, key_weight, value_weight, query_bias, value_bias, output_weight, output_bias, first_gain, first_shift, inner_weight, inner_bias, outer_weight, outer_bias, second_gain, second_shift)))
    block_list = N_DP * MB
    inputs = hidden_in.astype(jnp.float32).reshape(block_list, MICRO_TOKENS, D)
    codes = buckets.reshape(block_list).astype(jnp.int32)
    token_ranges = lengths.reshape(block_list, MICRO_TOKENS // BASE_ROW_TOKENS).astype(jnp.int32)
    checked = jax.checkpoint(block_forward)

    def whole(weights, inputs):

        def advance(carry, item):
            block, code, span = item
            return (carry, checked(weights, block, code, span))
        start = jnp.zeros((), jnp.float32)
        ignored, outputs = lax.scan(advance, start, (inputs, codes, token_ranges))
        return outputs
    outputs, pullback = jax.vjp(whole, weights, inputs)
    grads, input_grads = pullback(cotangent.astype(jnp.float32).reshape(block_list, MICRO_TOKENS, D))
    layer_out = outputs.reshape(block_list * MICRO_TOKENS, D).astype(jnp.bfloat16)
    input_grad = input_grads.reshape(block_list * MICRO_TOKENS, D)
    return (layer_out, input_grad, grads[0], grads[1], grads[2], grads[3], grads[4], grads[5], grads[6], grads[7], grads[8], grads[9], grads[10], grads[11], grads[12], grads[13], grads[14])
```

```python
import jax
import jax.numpy as jnp
from jax import lax
from jax.experimental import pallas as pl
from jax.experimental.pallas import tpu as pltpu
from jax.sharding import Mesh
from jax.sharding import PartitionSpec as P

DP = ("dp_0", "dp_1", "dp_2", "dp_3")
AX = ("dp_0", "mp")
AZ, AY, AC = "dp_1", "dp_2", "dp_3"
D = 768
T = 512
DH = 64
FF = 3072
HALF = 384
FHALF = 1536
FQ = 768
CH = 2304
CQ = 1152
EPS = 1e-12
BF = jnp.bfloat16
F32 = jnp.float32
VMEM = pltpu.VMEM
INV_SQRT2 = 0.7071067811865476
INV_SQRT2PI = 0.3989422804014327


def nn(a, b):
    return lax.dot_general(a, b, (((1,), (0,)), ((), ())), preferred_element_type=F32)


def nt(a, b):
    return lax.dot_general(a, b, (((1,), (1,)), ((), ())), preferred_element_type=F32)


def tn(a, b):
    return lax.dot_general(a, b, (((0,), (0,)), ((), ())), preferred_element_type=F32)


def flip(a, axis, s):
    n = 4 if axis in (AX, AY, AZ) else 2
    return lax.ppermute(a, axis, [(i, i ^ s) for i in range(n)])


def joined(a, axis):
    return jnp.concatenate([a] + [flip(a, axis, s) for s in (1, 2, 3)], axis=1)


def spread(b, axis):
    own = [b] + [flip(b, axis, s) for s in (1, 2, 3)]
    return own + [flip(o, AC, 1) for o in own]


def halves(a, first, width):
    c = a.shape[2] // 2
    return jnp.concatenate([a[:, :, first : first + width], a[:, :, c + first : c + first + width]], axis=2)


def gather(shard):
    a = shard.reshape(3, 4, -1)
    p1, p2, p3 = (flip(a, AX, s) for s in (1, 2, 3))
    parts = []
    for first in (0, CH):
        cols = slice(first, first + CH)
        a0, a1, a2, a3 = (p[:, :, cols] for p in (a, p1, p2, p3))
        parts.append(
            jnp.concatenate(
                [jnp.concatenate([a0, a2], axis=1), jnp.concatenate([a1, a3], axis=1)], axis=2
            )
        )
    first = joined(parts[0], AY)
    second = joined(parts[1], AZ)
    attn = spread(halves(first, 0, 4 * HALF), AZ)
    late = spread(second, AY)
    inner, _ = lax.optimization_barrier((halves(first, 4 * HALF, FQ), attn[1]))
    return attn, spread(inner, AZ), late


def add(*parts):
    total = parts[0].astype(F32)
    for p in parts[1:]:
        total = total + p.astype(F32)
    return total


def reduce(own, other, first, second):
    c = own.shape[-1] // 2
    other = flip(other, AC, 1)
    r = [add(own[s], other[s]).astype(BF) for s in range(4)]
    r = [r[0]] + [flip(r[s], first, s) for s in (1, 2, 3)]
    m = []
    for t in range(4):
        rows = add(*(p[:96].reshape(3, 4, 8, 2 * c)[:, t] for p in r)).astype(BF)
        vecs = add(*(p[96:] for p in r)).astype(BF)
        m.append(jnp.concatenate([rows.reshape(24, 2 * c), vecs], axis=0))
    m = [m[0]] + [flip(m[t], second, t) for t in (1, 2, 3)]
    n = []
    for s in range(4):
        cols = slice((s & 1) * c, (s & 1) * c + c)
        rows = add(*(p[:24, cols].reshape(3, 2, 4, c)[:, s >> 1] for p in m)).astype(BF)
        vecs = add(*(p[24:, cols] for p in m)).astype(BF)
        n.append(jnp.concatenate([rows.reshape(12, c), vecs], axis=0))
    total = add(n[0], *(flip(n[s], AX, s) for s in (1, 2, 3)))
    return total[:12], total[12:]


def order_matrix(place, swap):
    r = lax.broadcasted_iota(jnp.int32, (1, D), 1)
    j = r & 3
    hi = ((r >> 2) & 1) ^ place[0]
    near, far = (r >> 3) & 3, (r >> 5) & 3
    y = (far if swap else near) ^ place[2]
    z = (near if swap else far) ^ place[1]
    block = r >> 7
    core = jnp.where(block >= 3, 1, 0)
    group = block - 3 * core
    core = core ^ place[3]
    source = (((hi * 4 + z) * 4 + y) * 2 + core) * 12 + group * 4 + j
    rows = lax.broadcasted_iota(jnp.int32, (D, D), 0)
    return jnp.where(rows == source, 1.0, 0.0)


def swap_matrix():
    r = lax.broadcasted_iota(jnp.int32, (1, D), 1)
    source = (r & ~0x78) | ((r & 0x18) << 2) | ((r & 0x60) >> 2)
    rows = lax.broadcasted_iota(jnp.int32, (D, D), 0)
    return jnp.where(rows == source, 1.0, 0.0)


def exact(a, b, dims):
    return lax.dot_general(
        a, b, (dims, ((), ())), preferred_element_type=F32, precision=lax.Precision.HIGHEST
    )


def order_kernel(place, x, y, v, order_a, order_b, swap, xr, yr, vr):
    m = order_matrix(place, False)
    order_a[...] = m.astype(BF)
    xr[...] = nn(x[...], order_a[...]).astype(BF)
    vr[0:8, :] = exact(v[0:8, :], m, ((1,), (0,)))
    m = order_matrix(place, True)
    order_b[...] = m.astype(BF)
    yr[...] = nn(y[...], order_b[...]).astype(BF)
    vr[8:16, :] = exact(v[8:16, :], m, ((1,), (0,)))
    swap[...] = swap_matrix().astype(BF)


def start_weight(pieces, first, width, stride, dst, at, step, sem):
    for core in range(2):
        for z in range(4):
            for g in range(3):
                for m in range(2):
                    pltpu.make_async_copy(
                        pieces[core * 4 + z].at[g, :, pl.ds(m * stride + first, width)],
                        dst.at[pl.ds(((core * 3 + g) * 4 + z) * 32, 32), pl.ds(at + m * step, width)],
                        sem,
                    ).start()


def wait_whole(dst, sem):
    pltpu.make_async_copy(dst, dst, sem).wait()


def row_starts(info, shape, axis):
    shift = 7 + info[0]
    pos = lax.broadcasted_iota(jnp.int32, shape, axis)
    seq = lax.shift_right_logical(pos, shift)
    within = pos & (lax.shift_left(1, shift) - 1)
    live = jnp.where(
        seq == 0, info[1], jnp.where(seq == 1, info[2], jnp.where(seq == 2, info[3], info[4]))
    )
    return seq, within < live


def mask_bias(info, key_axis):
    kshape = (T, 1) if key_axis == 0 else (1, T)
    qshape = (1, T) if key_axis == 0 else (T, 1)
    kseq, live = row_starts(info, kshape, key_axis)
    qseq, _ = row_starts(info, qshape, 1 - key_axis)
    kseq = jnp.where(live, kseq, -1)
    return jnp.where(kseq == qseq, 0.0, -1e30)


def attention_kernel(
    info, xr, bias, p0, p1, p2, p3, p4, p5, p6, p7, q, k, v, ctx, lse, w_out, w, mask, lcol, sem, sem2
):
    start_weight((p0, p1, p2, p3, p4, p5, p6, p7), 0, 3 * HALF, 4 * HALF, w, 0, 3 * HALF, sem)
    mask[...] = mask_bias(info, 1)
    wait_whole(w, sem)
    keep = pltpu.make_async_copy(w, w_out, sem2)
    keep.start()
    for m in range(2):
        for i, (out, scale) in enumerate(((q, 0.125), (k, None), (v, None))):
            at = (m * 3 + i) * HALF
            a = nn(xr[...], w[:, at : at + HALF])
            if i == 0:
                a = a + bias[0:1, m * HALF : (m + 1) * HALF]
            if i == 2:
                a = a + bias[1:2, m * HALF : (m + 1) * HALF]
            a = a.astype(BF)
            if scale is not None:
                a = a * BF(scale)
            out[:, m * HALF : (m + 1) * HALF] = a
    lcol[...] = jnp.zeros_like(lcol)
    lane = lax.broadcasted_iota(jnp.int32, (1, 128), 1)

    def pair(i, _):
        cols = pl.ds(pl.multiple_of(i * 128, 128), 128)
        q2, k2, v2 = q[:, cols], k[:, cols], v[:, cols]
        total = None
        for half in range(2):
            mine = (lane < 64) if half == 0 else (lane >= 64)
            s = nt(jnp.where(mine, q2, BF(0)), k2) + mask[...]
            peak = jnp.max(s, axis=1, keepdims=True)
            e = jnp.exp(s - peak)
            z = jnp.sum(e, axis=1, keepdims=True)
            p = (e / z).astype(BF)
            c = nn(p, jnp.where(mine, v2, BF(0)))
            total = c if total is None else total + c
            l = peak + jnp.log(z)
            lcol[...] = jnp.where(lane == i * 2 + half, l, lcol[...])
        ctx[:, cols] = total.astype(BF)
        return 0

    lax.fori_loop(0, 6, pair, 0)
    lse[...] = lcol[...].T[0:16, :]
    keep.wait()


def stats(a):
    mean = jnp.mean(a, axis=1, keepdims=True)
    a = a - mean
    r = lax.rsqrt(jnp.mean(a * a, axis=1, keepdims=True) + EPS)
    return a * r, r


def norm_back(dy, n, r, gain):
    a = dy * gain
    return r * (
        a - jnp.mean(a, axis=1, keepdims=True) - n * jnp.mean(a * n, axis=1, keepdims=True)
    )


def store_rows(own, other, value, cols):
    for core, dst in enumerate((own, other)):
        for g in range(3):
            for z in range(4):
                at = ((core * 3 + g) * 4 + z) * 32
                dst[z, g * 32 : (g + 1) * 32, cols] = value[at : at + 32]


def store_vectors(own, other, value):
    for dst in (own, other):
        for z in range(4):
            dst[z, 96:104, :] = value


def middle_kernel(
    ctx, xr, yr, vr, inb, order_a, order_b, swap,
    a0, a1, a2, a3, a4, a5, a6, a7, b0, b1, b2, b3, b4, b5, b6, b7, c0, c1, c2, c3, c4, c5, c6, c7,
    out, dc, dr, grads_a, grads_a1, grads_b, grads_b1,
    wo, wi, wt, h1, h1b, n1, gact, slope, big, lowt, h1t, h1bt, sems,
):
    ap, bp, cp = (
        (a0, a1, a2, a3, a4, a5, a6, a7),
        (b0, b1, b2, b3, b4, b5, b6, b7),
        (c0, c1, c2, c3, c4, c5, c6, c7),
    )
    start_weight(ap, 3 * HALF, HALF, 4 * HALF, wo, 0, HALF, sems.at[0])
    start_weight(bp, 0, FQ, FQ, wi, 0, FQ, sems.at[1])
    start_weight(cp, 2 * FQ, FQ, CH, wi, 2 * FQ, FQ, sems.at[1])
    start_weight(cp, 0, FQ, CH, wt, 0, FQ, sems.at[2])
    start_weight(cp, FQ, FQ, CH, wt, 2 * FQ, FQ, sems.at[2])
    wait_whole(wo, sems.at[0])
    ob, g1, s1 = (vr[i : i + 1, :] for i in range(3))
    fb, g2, s2 = (vr[i : i + 1, :] for i in range(8, 11))
    nrm, r1 = stats(nt(ctx[...], wo[...]) + ob + xr[...].astype(F32))
    n1[...] = nrm
    h1[...] = (nrm * g1 + s1).astype(BF)
    h1b[...] = nn(h1[...], swap[...]).astype(BF)
    wait_whole(wi, sems.at[1])
    wait_whole(wt, sems.at[2])
    big[...] = h1b[...].astype(F32) + fb

    for half, h in enumerate((h1, h1b)):

        def up(m, _, half=half, h=h):
            cols = pl.ds(pl.multiple_of((half * 2 + m) * FQ, FQ), FQ)
            u = nn(h[...], wi[:, cols]) + inb[:, cols]
            phi = 0.5 + 0.5 * lax.erf(u * INV_SQRT2)
            slope[:, cols] = phi + u * (jnp.exp(-0.5 * u * u) * INV_SQRT2PI)
            g = (u * phi).astype(BF)
            gact[:, cols] = g
            big[...] += nt(g, wt[:, cols])
            return 0

        lax.fori_loop(0, 2, up, 0)
    n2, r2 = stats(big[...])
    low = (n2 * g2 + s2).astype(BF)
    out[...] = nt(low, order_b[...]).astype(BF)
    y = yr[...].astype(F32)
    dg2 = jnp.sum(y * n2, axis=0, keepdims=True)
    ds2 = jnp.sum(y, axis=0, keepdims=True)
    db = norm_back(y, n2, r2, g2)
    big[...] = db
    df = db.astype(BF)
    dfb = jnp.sum(df.astype(F32), axis=0, keepdims=True)
    dc[...] = df
    lowt[...] = db.T.astype(BF)
    h1t[...] = h1[...].astype(F32).T.astype(BF)
    h1bt[...] = h1b[...].astype(F32).T.astype(BF)
    dinb = [None] * 4
    for f in (2, 3, 0, 1):
        half, m = f >> 1, f & 1
        cols = slice(f * FQ, (f + 1) * FQ)
        du = (nn(dc[...], wt[:, cols]) * slope[:, cols]).astype(BF)
        dinb[f] = jnp.sum(du.astype(F32), axis=0, keepdims=True)
        if f == 0:
            db = big[...]
            hi = db.astype(BF)
            lo = (db - hi.astype(F32)).astype(BF)
            big[...] = nt(hi, swap[...]) + nt(lo, swap[...])
        big[...] += nt(du, wi[:, cols])
        g = nn(lowt[...], gact[:, cols]).astype(BF)
        store_rows(grads_b, grads_b1, g, pl.ds(m * CH + half * FQ, FQ))
        g = nn((h1bt if half else h1t)[...], du).astype(BF)
        if half:
            store_rows(grads_b, grads_b1, g, pl.ds(m * CH + 2 * FQ, FQ))
        else:
            store_rows(grads_a, grads_a1, g, pl.ds(m * CQ + HALF, FQ))
    dh = big[...]
    nrm = n1[...]
    dg1 = jnp.sum(dh * nrm, axis=0, keepdims=True)
    ds1 = jnp.sum(dh, axis=0, keepdims=True)
    d = norm_back(dh, nrm, r1, g1)
    dr[...] = d
    da = d.astype(BF)
    dob = jnp.sum(da.astype(F32), axis=0, keepdims=True)
    dc[...] = nn(da, wo[...]).astype(BF)
    lowt[...] = d.T.astype(BF)
    g = nn(lowt[...], ctx[...]).astype(BF)
    for m in range(2):
        store_rows(grads_a, grads_a1, g[:, m * HALF : (m + 1) * HALF], pl.ds(m * CQ, HALF))
    sa = exact(
        jnp.concatenate([dob, dg1, ds1, dob, dob, dob, dob, dob], axis=0),
        order_a[...].astype(F32),
        ((1,), (1,)),
    )
    sb = exact(
        jnp.concatenate([dfb, dg2, ds2, dfb, dfb, dfb, dfb, dfb], axis=0),
        order_b[...].astype(F32),
        ((1,), (1,)),
    )
    sides = []
    for m in range(2):
        line = jnp.concatenate(
            [dinb[m], dinb[2 + m]] + [sa[i : i + 1] for i in range(3)] + [sb[i : i + 1] for i in range(3)],
            axis=1,
        )
        rows = [line[:, i * CQ : (i + 1) * CQ] for i in range(5)]
        rows.append(jnp.concatenate([line[:, 5 * CQ :], jnp.zeros((1, 6 * CQ - 8 * FQ), F32)], axis=1))
        sides.append(jnp.concatenate(rows + [jnp.zeros((2, CQ), F32)], axis=0))
    store_vectors(grads_a, grads_a1, jnp.concatenate(sides, axis=1).astype(BF))
    store_vectors(grads_b, grads_b1, jnp.zeros((8, 2 * CH), BF))


def back_kernel(
    info, q, k, v, dc, lse, xr, w, dr, order, grads, grads1, gin, mask, dq, dk, dv, big, dqb, dvb
):
    mask[...] = mask_bias(info, 0)
    lane = lax.broadcasted_iota(jnp.int32, (1, 128), 1)

    def pair(i, _):
        cols = pl.ds(pl.multiple_of(i * 128, 128), 128)
        q2, k2, v2, c2 = q[:, cols], k[:, cols], v[:, cols], dc[:, cols]
        outs = []
        for half in range(2):
            mine = (lane < 64) if half == 0 else (lane >= 64)
            s = nt(jnp.where(mine, k2, BF(0)), q2) + mask[...]
            p = jnp.exp(s - lse[pl.ds(i * 2 + half, 1), :])
            dp = nt(jnp.where(mine, v2, BF(0)), c2)
            delta = jnp.sum(dp * p, axis=0, keepdims=True)
            ds = (p * (dp - delta)).astype(BF)
            outs.append((tn(ds, k2), nn(ds, q2), nn(p.astype(BF), c2)))
        first = lane < 64
        dq2, dk2, dv2 = (jnp.where(first, a, b) for a, b in zip(*outs))
        dq2 = (dq2 * 0.125).astype(BF)
        dk2 = dk2.astype(BF)
        dv2 = dv2.astype(BF)
        dq[:, cols] = dq2
        dk[:, cols] = dk2
        dv[:, cols] = dv2
        dqb[:, cols] = jnp.sum(dq2.astype(F32), axis=0, keepdims=True)
        dvb[:, cols] = jnp.sum(dv2.astype(F32), axis=0, keepdims=True)
        return 0

    lax.fori_loop(0, 6, pair, 0)
    xt = xr[...].astype(F32).T.astype(BF)
    big[...] = dr[...]
    for m in range(2):
        for i, src in enumerate((dq, dk, dv)):
            at = (m * 3 + i) * HALF
            a = src[:, m * HALF : (m + 1) * HALF]
            store_rows(grads, grads1, nn(xt, a).astype(BF), pl.ds(at, HALF))
            big[...] += nt(a, w[:, at : at + HALF])
    gin[...] = nt(big[...].astype(BF), order[...]).astype(BF)
    blank = jnp.zeros((1, HALF), F32)
    line = jnp.concatenate(
        [dqb[:, :HALF], dvb[:, :HALF], blank, dqb[:, HALF:], dvb[:, HALF:], blank], axis=1
    )
    line = jnp.concatenate([line, jnp.zeros((7, 6 * HALF), F32)], axis=0)
    store_vectors(grads, grads1, line.astype(BF))


def call(kernel, outs, args, scratch=(), vmem=48, flops=0, smem=0, hbm=(), anyouts=()):
    specs = []
    for i in range(len(args)):
        if i < smem:
            specs.append(pl.BlockSpec(memory_space=pltpu.SMEM))
        elif i in hbm:
            specs.append(pl.BlockSpec(memory_space=pl.ANY))
        else:
            specs.append(pl.BlockSpec(memory_space=VMEM))
    return pl.pallas_call(
        kernel,
        out_shape=[jax.ShapeDtypeStruct(s, d) for s, d in outs],
        in_specs=specs,
        out_specs=[
            pl.BlockSpec(memory_space=pl.ANY if i in anyouts else VMEM) for i in range(len(outs))
        ],
        scratch_shapes=list(scratch),
        compiler_params=pltpu.CompilerParams(vmem_limit_bytes=vmem * 2**20),
        cost_estimate=pl.CostEstimate(flops=flops, bytes_accessed=10**7, transcendentals=0),
    )(*args)


def body(
    hidden_in, buckets, lengths, query_weight, key_weight, value_weight, query_bias, value_bias,
    output_weight, output_bias, first_gain, first_shift, inner_weight, inner_bias, outer_weight,
    outer_bias, second_gain, second_shift, cotangent,
):
    mp = lax.axis_index("mp")
    place = jnp.stack([lax.axis_index(a) for a in DP]).astype(jnp.int32)
    shard = jnp.concatenate(
        [
            query_weight,
            key_weight,
            value_weight,
            output_weight.T,
            inner_weight[:, :FQ],
            outer_weight.T,
            inner_weight[:, FQ:],
        ],
        axis=1,
    )
    pa, pb, pc = gather(shard)
    biases = jnp.concatenate([query_bias, value_bias, inner_bias])
    others = flip(biases, "mp", 1)
    qvb = jnp.stack(
        [
            jnp.concatenate([biases[:HALF], others[:HALF]]),
            jnp.concatenate([biases[HALF:D], others[HALF:D]]),
        ]
    )
    inb = jnp.concatenate(
        [biases[D : D + FQ], others[D : D + FQ], biases[D + FQ :], others[D + FQ :]]
    )[None]
    va = [output_bias, first_gain, first_shift] + [output_bias] * 5
    vb = [outer_bias, second_gain, second_shift] + [outer_bias] * 5
    x = lax.dynamic_slice_in_dim(hidden_in, mp * T, T, 0)
    cot = lax.dynamic_slice_in_dim(cotangent, mp * T, T, 0)
    info = jnp.concatenate(
        [lax.dynamic_slice_in_dim(buckets[0], mp, 1, 0), lax.dynamic_index_in_dim(lengths[0], mp, 0, False)]
    )
    square = ((D, D), BF)
    tokens = ((T, D), BF)
    order_a, order_b, swap, xr, yr, vr = call(
        order_kernel,
        [square, square, square, tokens, tokens, ((16, D), F32)],
        (place, x, cot, jnp.stack(va + vb)),
        smem=1,
        vmem=24,
        flops=2 * 10**9,
    )
    q, k, v, ctx, lse, w = call(
        attention_kernel,
        [tokens, tokens, tokens, tokens, ((16, T), F32), ((D, 6 * HALF), BF)],
        (info, xr, qvb, *pa),
        [
            VMEM((D, 6 * HALF), BF),
            VMEM((T, T), F32),
            VMEM((T, 128), F32),
            pltpu.SemaphoreType.DMA(()),
            pltpu.SemaphoreType.DMA(()),
        ],
        smem=1,
        hbm=range(3, 11),
        anyouts=(5,),
        vmem=32,
        flops=10 * 10**9,
    )
    ga, gb = ((4, 104, 2 * CQ), BF), ((4, 104, 2 * CH), BF)
    out, dc, dr, grads_a, grads_a1, grads_b, grads_b1 = call(
        middle_kernel,
        [tokens, tokens, ((T, D), F32), ga, ga, gb, gb],
        (ctx, xr, yr, vr, inb, order_a, order_b, swap, *pa, *pb, *pc),
        [
            VMEM((D, D), BF),
            VMEM((D, FF), BF),
            VMEM((D, FF), BF),
            VMEM((T, D), BF),
            VMEM((T, D), BF),
            VMEM((T, D), F32),
            VMEM((T, FF), BF),
            VMEM((T, FF), F32),
            VMEM((T, D), F32),
            VMEM((D, T), BF),
            VMEM((D, T), BF),
            VMEM((D, T), BF),
            pltpu.SemaphoreType.DMA((3,)),
        ],
        hbm=range(8, 32),
        vmem=58,
        flops=16 * 10**9,
    )
    grads_q, grads_q1, gin = call(
        back_kernel,
        [ga, ga, tokens],
        (info, q, k, v, dc, lse, xr, w, dr, order_a),
        [
            VMEM((T, T), F32),
            VMEM((T, D), BF),
            VMEM((T, D), BF),
            VMEM((T, D), BF),
            VMEM((T, D), F32),
            VMEM((1, D), F32),
            VMEM((1, D), F32),
        ],
        smem=1,
        vmem=40,
        flops=14 * 10**9,
    )
    rb, _ = reduce(grads_b, grads_b1, AY, AZ)
    ra, vec = reduce(grads_a, grads_a1, AZ, AY)
    rq, qv = reduce(grads_q, grads_q1, AZ, AY)

    def both(mine):
        other = flip(mine, "mp", 1)
        return jnp.where(
            mp == 0, jnp.concatenate([mine, other], axis=0), jnp.concatenate([other, mine], axis=0)
        )

    layer_out = both(out)
    input_grad = both(gin).astype(F32)
    vec = vec.reshape(-1)
    dob, dg1, ds1, dfb, dg2, ds2 = (vec[FHALF + i * D : FHALF + (i + 1) * D] for i in range(6))
    return (
        layer_out,
        input_grad,
        rq[:, :HALF],
        rq[:, HALF:D],
        rq[:, D:],
        qv[0, :HALF],
        qv[0, HALF:D],
        ra[:, :HALF].T,
        dob,
        dg1,
        ds1,
        jnp.concatenate([ra[:, HALF:], rb[:, FHALF:]], axis=1),
        vec[:FHALF],
        rb[:, :FHALF].T,
        dfb,
        dg2,
        ds2,
    )


def solution(mesh):
    torus = Mesh(
        mesh.devices.reshape(2, 4, 4, 2, mesh.shape["mp"]), ("dp_0", "dp_1", "dp_2", "dp_3", "mp")
    )
    row, col, half = P(DP, "mp"), P("mp", DP), P("mp")
    in_specs = (
        P(DP, None), P(DP, None), P(DP, None, None), row, row, row, half, half, col, P(), P(), P(),
        row, half, col, P(), P(), P(), P(DP, None),
    )
    out_specs = (
        P(DP, None), P(DP, None), row, row, row, half, half, col, P(), P(), P(), row, half, col,
        P(), P(), P(),
    )
    return jax.shard_map(body, mesh=torus, in_specs=in_specs, out_specs=out_specs, check_vma=False)
```

```python
import functools

import jax
import jax.numpy as jnp
from jax import lax
from jax.experimental import pallas as pl
from jax.experimental.pallas import tpu as pltpu
from jax.sharding import Mesh
from jax.sharding import PartitionSpec as P

DP = ("dp_0", "dp_1", "dp_2", "dp_3")
AX = ("dp_0", "mp")
AZ, AY, AC = "dp_1", "dp_2", "dp_3"
D = 768
T = 512
DH = 64
FF = 3072
HALF = 384
FHALF = 1536
FQ = 768
CH = 2304
CQ = 1152
CA = 1920
EPS = 1e-12
BF = jnp.bfloat16
F32 = jnp.float32
VMEM = pltpu.VMEM
INV_SQRT2 = 0.7071067811865476
INV_SQRT2PI = 0.3989422804014327


def nn(a, b):
    return lax.dot_general(a, b, (((1,), (0,)), ((), ())), preferred_element_type=F32)


def nt(a, b):
    return lax.dot_general(a, b, (((1,), (1,)), ((), ())), preferred_element_type=F32)


def tn(a, b):
    return lax.dot_general(a, b, (((0,), (0,)), ((), ())), preferred_element_type=F32)


def flip(a, axis, s):
    n = 4 if axis in (AX, AY, AZ) else 2
    return lax.ppermute(a, axis, [(i, i ^ s) for i in range(n)])


def joined(a, axis):
    return jnp.concatenate([a] + [flip(a, axis, s) for s in (1, 2, 3)], axis=1)


def gather(shard, ready):
    a = shard
    p1, p2, p3 = (flip(a, AX, s) for s in (1, 2, 3))
    parts = []
    for first in (0, CH):
        cols = slice(first, first + CH)
        a0, a1, a2, a3 = (p[:, :, cols] for p in (a, p1, p2, p3))
        parts.append(
            jnp.concatenate(
                [jnp.concatenate([a0, a2], axis=1), jnp.concatenate([a1, a3], axis=1)], axis=2
            )
        )
    parts = lax.optimization_barrier((joined(parts[0], AY), joined(parts[1], AZ)))
    near = [[flip(b, axis, s) for s in (1, 3)] for b, axis in zip(parts, (AZ, AY))]
    near, ready = lax.optimization_barrier((near, ready))
    out = []
    for b, axis, (n1, n3) in zip(parts, (AZ, AY), near):
        far = [flip(n1[:, :, :CH], axis, 3), flip(n3[:, :, CH:], axis, 1)]
        own = [b, n1, n3, *far]
        out.append(own + [flip(o, AC, 1) for o in own])
    return *out, ready


def add(*parts):
    total = parts[0].astype(F32)
    for p in parts[1:]:
        total = total + p.astype(F32)
    return total


def low_sum(*parts):
    return add(*parts).astype(BF)


def core_kernel(*refs):
    c0, c1, c3, left, right = refs[-5:]
    pairs = [refs[i : i + 2] for i in range(0, len(refs) - 5, 2)]
    at = 0
    for own, other in pairs:
        rows, n = own.shape[1:]
        for s, dst in ((0, c0), (1, c1), (3, c3), (2, None)):
            total = low_sum(own[s], other[s])
            if s == 2:
                left[:rows, at // 2 : (at + n) // 2] = total[:, : n // 2]
                right[:rows, at // 2 : (at + n) // 2] = total[:, n // 2 :]
                dsts = (left, right)
            else:
                dst[:rows, at : at + n] = total
                dsts = (dst,)
            for d in dsts:
                if rows < d.shape[0]:
                    lo, hi = (at // 2, (at + n) // 2) if s == 2 else (at, at + n)
                    d[rows:, lo:hi] = jnp.zeros((d.shape[0] - rows, hi - lo), BF)
        at += n


def core_sums(pairs, rows):
    n = sum(own.shape[2] for own, _ in pairs)
    whole, half = ((rows, n), BF), ((rows, n // 2), BF)
    return call(
        core_kernel, [whole, whole, whole, half, half], [a for p in pairs for a in p], vmem=32
    )


def relay_kernel(widths, c1, c3, left, right, out1, out3):
    at = 0
    for n in widths:
        h = n // 2
        part = slice(at // 2, at // 2 + h)
        out3[:, at : at + h] = low_sum(c3[:, at : at + h], left[:, part])
        out3[:, at + h : at + n] = c3[:, at + h : at + n]
        out1[:, at : at + h] = c1[:, at : at + h]
        out1[:, at + h : at + n] = low_sum(c1[:, at + h : at + n], right[:, part])
        at += n


def relayed(widths, c1, c3, left, right):
    whole = (c1.shape, BF)
    return call(
        functools.partial(relay_kernel, widths), [whole, whole], (c1, c3, left, right), vmem=24
    )


def chip_rows(total, near, hi):
    return [total[g * 32 + near * 8 + hi * 4 : g * 32 + near * 8 + hi * 4 + 4] for g in range(3)]


def attention_sums_kernel(index, a, a1, b, b1, out):
    (hi0, z0, y0, _), m0 = decoded(index[0])
    blank = jnp.zeros((2, HALF), F32)
    for m, (own, other) in enumerate(((a, a1), (b, b1))):
        for y in range(4):
            total = add(own[y], other[y])
            vec = jnp.concatenate([total[96:97, :HALF], total[96:97, HALF:D], blank], axis=0)
            for z in range(4):
                for hi in range(2):
                    r0, r1, r2 = chip_rows(total, z, hi)
                    c0, c1, c2 = (r2[:, i * HALF : (i + 1) * HALF] for i in range(3))
                    block = jnp.concatenate(
                        [
                            jnp.concatenate([r0, c0, c1], axis=1),
                            jnp.concatenate([r1, c2, vec], axis=1),
                        ],
                        axis=0,
                    )
                    chip = (((hi ^ hi0) * 2 + (m ^ m0)) * 4 + (z ^ z0)) * 4 + (y ^ y0)
                    out[chip] = block.astype(BF)


def sent(parts, axis):
    return [parts[0]] + [flip(parts[s], axis, s) for s in (1, 2, 3)]


def second_kernel(a0, a1, a3, *outs):
    total = add(a0[...], a1[...], a3[...]).astype(BF)
    for y in range(4):
        for g in range(3):
            at = g * 32 + y * 8
            outs[y][g * 8 : (g + 1) * 8, :] = total[at : at + 8]
        outs[y][24:, :] = total[96:]


def third_kernel(m0, m1, m2, m3, *outs):
    total = add(m0[...], m1[...], m2[...], m3[...])
    for m in range(2):
        at = 2 * CQ + m * FQ
        part = jnp.concatenate(
            [total[:, m * CQ : (m + 1) * CQ], total[:, at : at + FQ]], axis=1
        )
        for hi in range(2):
            rows = [part[g * 8 + hi * 4 : g * 8 + hi * 4 + 4] for g in range(3)]
            rows = jnp.concatenate(rows + [part[24:]], axis=0)
            outs[hi * 2 + m][...] = rows.astype(BF)


def outer_sums_kernel(index, b0, b1, b3, out):
    (hi0, z0, _, _), m0 = decoded(index[0])
    total = add(b0[...], b1[...], b3[...])
    for m in range(2):
        part = total[:, m * FHALF : (m + 1) * FHALF]
        for z in range(4):
            for hi in range(2):
                r0, r1, r2 = chip_rows(part, z, hi)
                block = jnp.concatenate(
                    [
                        jnp.concatenate([r0, r2[:, :FQ]], axis=1),
                        jnp.concatenate([r1, r2[:, FQ:]], axis=1),
                    ],
                    axis=0,
                )
                out[((hi ^ hi0) * 2 + (m ^ m0)) * 4 + (z ^ z0)] = block.astype(BF)


def exchanged(blocks, axes):
    return lax.all_to_all(blocks, axes, 0, 0, tiled=True)


def total_of(blocks):
    total = blocks[0].astype(F32)
    for i in range(1, blocks.shape[0]):
        total = total + blocks[i].astype(F32)
    return total


def final_kernel(n0, n1, n2, n3, fb_, fq, wq, wk, wv, wo, wi, wt, qb, vb, ib, ob, g1, s1, fb, g2, s2):
    total = add(n0[...], n1[...], n2[...], n3[...])
    wo[...] = total[:12, :HALF]
    wi[...] = total[:12, HALF:]
    vec = jnp.concatenate([total[12 + i : 13 + i, :CQ] for i in range(6)], axis=1)
    at = 0
    for dst in (ib, ob, g1, s1, fb, g2, s2):
        dst[...] = vec[0, at : at + dst.shape[0]]
        at += dst.shape[0]
    total = total_of(fb_)
    wt[:8] = total[:, :FHALF]
    wt[8:, :FQ] = total[:4, FHALF:]
    wt[8:, FQ:] = total[4:, FHALF:]
    total = total_of(fq)
    for i, dst in enumerate((wq, wk, wv)):
        dst[:8] = total[:, i * HALF : (i + 1) * HALF]
        at = (i >> 1) * 4
        dst[8:] = total[at : at + 4, CQ + (i & 1) * HALF : CQ + ((i & 1) + 1) * HALF]
    qb[...] = total[4, CQ + HALF :]
    vb[...] = total[5, CQ + HALF :]


def decoded(index):
    return (index >> 6, (index >> 4) & 3, (index >> 2) & 3, (index >> 1) & 1), index & 1


def row_of(vector):
    return vector[...].reshape(1, -1)


def order_matrix(place, swap):
    r = lax.broadcasted_iota(jnp.int32, (1, D), 1)
    j = r & 3
    hi = ((r >> 2) & 1) ^ place[0]
    near, far = (r >> 3) & 3, (r >> 5) & 3
    y = (far if swap else near) ^ place[2]
    z = (near if swap else far) ^ place[1]
    block = r >> 7
    core = jnp.where(block >= 3, 1, 0)
    group = block - 3 * core
    core = core ^ place[3]
    source = (((hi * 4 + z) * 4 + y) * 2 + core) * 12 + group * 4 + j
    rows = lax.broadcasted_iota(jnp.int32, (D, D), 0)
    return jnp.where(rows == source, 1.0, 0.0)


def swap_matrix():
    r = lax.broadcasted_iota(jnp.int32, (1, D), 1)
    source = (r & ~0x78) | ((r & 0x18) << 2) | ((r & 0x60) >> 2)
    rows = lax.broadcasted_iota(jnp.int32, (D, D), 0)
    return jnp.where(rows == source, 1.0, 0.0)


def exact(a, b, dims):
    return lax.dot_general(
        a, b, (dims, ((), ())), preferred_element_type=F32, precision=lax.Precision.HIGHEST
    )


def pack_kernel(wq, wk, wv, wo, wi, wt, out):
    at = 0
    for src, first, n in (
        (wq, 0, HALF),
        (wk, 0, HALF),
        (wv, 0, HALF),
        (wo, 0, HALF),
        (wi, 0, FQ),
        (wt, 0, FHALF),
        (wi, FQ, FQ),
    ):
        for g in range(3):
            out[g, :, at : at + n] = src[g * 4 : (g + 1) * 4, first : first + n]
        at += n


def decoded(index):
    return (index >> 6, (index >> 4) & 3, (index >> 2) & 3, (index >> 1) & 1), index & 1


def row_of(vector):
    return vector[...].reshape(1, -1)


def order_matrix(place, swap):
    r = lax.broadcasted_iota(jnp.int32, (1, D), 1)
    j = r & 3
    hi = ((r >> 2) & 1) ^ place[0]
    near, far = (r >> 3) & 3, (r >> 5) & 3
    y = (far if swap else near) ^ place[2]
    z = (near if swap else far) ^ place[1]
    block = r >> 7
    core = jnp.where(block >= 3, 1, 0)
    group = block - 3 * core
    core = core ^ place[3]
    source = (((hi * 4 + z) * 4 + y) * 2 + core) * 12 + group * 4 + j
    rows = lax.broadcasted_iota(jnp.int32, (D, D), 0)
    return jnp.where(rows == source, 1.0, 0.0)


def swap_matrix():
    r = lax.broadcasted_iota(jnp.int32, (1, D), 1)
    source = (r & ~0x78) | ((r & 0x18) << 2) | ((r & 0x60) >> 2)
    rows = lax.broadcasted_iota(jnp.int32, (D, D), 0)
    return jnp.where(rows == source, 1.0, 0.0)


def exact(a, b, dims):
    return lax.dot_general(
        a, b, (dims, ((), ())), preferred_element_type=F32, precision=lax.Precision.HIGHEST
    )


def order_kernel(
    index, x_all, y_all, ob, g1, s1, fb, g2, s2,
    order_a, order_b, swap, xr, xb, yr, vr, x, y, sems,
):
    place, mp = decoded(index[0])
    rows = pl.ds(pl.multiple_of(mp * T, T), T)
    copies = [
        pltpu.make_async_copy(src.at[rows, :], dst, sems.at[i])
        for i, (src, dst) in enumerate(((x_all, x), (y_all, y)))
    ]
    for c in copies:
        c.start()
    m = order_matrix(place, False)
    order_a[...] = m.astype(BF)
    blank = jnp.zeros((5, D), F32)
    vr[0:8, :] = exact(
        jnp.concatenate([row_of(ob), row_of(g1), row_of(s1), blank], axis=0), m, ((1,), (0,))
    )
    m = order_matrix(place, True)
    order_b[...] = m.astype(BF)
    vr[8:16, :] = exact(
        jnp.concatenate([row_of(fb), row_of(g2), row_of(s2), blank], axis=0), m, ((1,), (0,))
    )
    swap[...] = swap_matrix().astype(BF)
    for c in copies:
        c.wait()
    xr[...] = nn(x[...], order_a[...]).astype(BF)
    xb[...] = nn(x[...], order_b[...]).astype(BF)
    yr[...] = nn(y[...], order_b[...]).astype(BF)


def start_weight(pieces, first, width, dst, at, m, sem):
    for core in range(2):
        for i, z in enumerate((0, 1, 3, 2)):
            src = pieces[core * 5 + i + (m if z == 2 else 0)]
            col = first + (0 if z == 2 else m * CH)
            pltpu.make_async_copy(
                src.at[:, :, pl.ds(col, width)],
                dst.at[pl.ds(core * 3, 3), pl.ds(z * 32, 32), pl.ds(at, width)],
                sem,
            ).start()


def wait_weight(dst, at, width, sem):
    part = dst.at[:, :, pl.ds(at, width)]
    pltpu.make_async_copy(part, part, sem).wait()


def weight(w, at, width):
    return w[:, :, pl.ds(at, width)].reshape(D, width)


def row_starts(info, shape, axis):
    index, buckets, lengths = info
    mp = index[0] & 1
    shift = 7 + buckets[0, mp]
    pos = lax.broadcasted_iota(jnp.int32, shape, axis)
    seq = lax.shift_right_logical(pos, shift)
    within = pos & (lax.shift_left(1, shift) - 1)
    n0, n1, n2, n3 = (lengths[0, mp, i] for i in range(4))
    live = jnp.where(seq == 0, n0, jnp.where(seq == 1, n1, jnp.where(seq == 2, n2, n3)))
    return seq, within < live


def mask_bias(info, key_axis):
    kshape = (T, 1) if key_axis == 0 else (1, T)
    qshape = (1, T) if key_axis == 0 else (T, 1)
    kseq, live = row_starts(info, kshape, key_axis)
    qseq, _ = row_starts(info, qshape, 1 - key_axis)
    kseq = jnp.where(live, kseq, -1)
    return jnp.where(kseq == qseq, 0.0, -1e30)


def attention_kernel(
    index, buckets, lengths, xr, qb, vb, others, p0, p1, p2, p3, p4, p5, p6, p7, p8, p9,
    q, k, v, ctx, lse, w_out, w, mask, lcol, sem, sem2,
):
    pieces = (p0, p1, p2, p3, p4, p5, p6, p7, p8, p9)
    for m in range(2):
        start_weight(pieces, 0, 3 * HALF, w, m * 3 * HALF, m, sem)
    mask[...] = mask_bias((index, buckets, lengths), 1)
    wait_weight(w, 0, 6 * HALF, sem)
    keep = pltpu.make_async_copy(w, w_out, sem2)
    keep.start()
    for m in range(2):
        for i, (out, scale) in enumerate(((q, 0.125), (k, None), (v, None))):
            at = (m * 3 + i) * HALF
            a = nn(xr[...], weight(w, at, HALF))
            if i != 1:
                own = (qb, None, vb)[i]
                at = (0, None, HALF)[i]
                a = a + (row_of(own) if m == 0 else others[pl.ds(at, HALF)].reshape(1, HALF))
            a = a.astype(BF)
            if scale is not None:
                a = a * BF(scale)
            out[:, m * HALF : (m + 1) * HALF] = a
    lcol[...] = jnp.zeros_like(lcol)
    lane = lax.broadcasted_iota(jnp.int32, (1, 128), 1)

    def pair(i, _):
        cols = pl.ds(pl.multiple_of(i * 128, 128), 128)
        q2, k2, v2 = q[:, cols], k[:, cols], v[:, cols]
        total = None
        for half in range(2):
            mine = (lane < 64) if half == 0 else (lane >= 64)
            s = nt(jnp.where(mine, q2, BF(0)), k2) + mask[...]
            peak = jnp.max(s, axis=1, keepdims=True)
            e = jnp.exp(s - peak)
            z = jnp.sum(e, axis=1, keepdims=True)
            p = (e / z).astype(BF)
            c = nn(p, jnp.where(mine, v2, BF(0)))
            total = c if total is None else total + c
            l = peak + jnp.log(z)
            lcol[...] = jnp.where(lane == i * 2 + half, l, lcol[...])
        ctx[:, cols] = total.astype(BF)
        return 0

    lax.fori_loop(0, 6, pair, 0)
    lse[...] = lcol[...].T[0:16, :]
    keep.wait()


def stats(a):
    mean = jnp.mean(a, axis=1, keepdims=True)
    a = a - mean
    r = lax.rsqrt(jnp.mean(a * a, axis=1, keepdims=True) + EPS)
    return a * r, r


def norm_back(dy, n, r, gain):
    a = dy * gain
    return r * (
        a - jnp.mean(a, axis=1, keepdims=True) - n * jnp.mean(a * n, axis=1, keepdims=True)
    )


def store_rows(own, other, value, cols):
    for core, dst in enumerate((own, other)):
        for g in range(3):
            for z in range(4):
                at = ((core * 3 + g) * 4 + z) * 32
                dst[z, g * 32 : (g + 1) * 32, cols] = value[at : at + 32]


def store_vectors(own, other, value):
    for dst in (own, other):
        for z in range(4):
            dst[z, 96:104, :] = value


def unit_source(f):
    return f < 2, (4 * HALF if f < 2 else 2 * FQ), f & 1


def up_kernel(
    ctx, xr, yr, vr, inb, others, order_b, swap,
    a0, a1, a2, a3, a4, a5, a6, a7, a8, a9, b0, b1, b2, b3, b4, b5, b6, b7, b8, b9,
    out, h1, n1, r1, db, sums, slope_out, grads, grads1,
    wo, wi, wt, h1b, gact, slope, big, lowt, sems, keeps,
):
    ap = (a0, a1, a2, a3, a4, a5, a6, a7, a8, a9)
    bp = (b0, b1, b2, b3, b4, b5, b6, b7, b8, b9)
    for m in range(2):
        start_weight(ap, 3 * HALF, HALF, wo, m * HALF, m, sems.at[0])
    for f in range(4):
        first, col, m = unit_source(f)
        start_weight(ap if first else bp, col, FQ, wi, f * FQ, m, sems.at[1 + f])
        start_weight(bp, (f >> 1) * FQ, FQ, wt, f * FQ, m, sems.at[5 + f])
    wait_weight(wo, 0, D, sems.at[0])
    ob, g1, s1 = (vr[i : i + 1, :] for i in range(3))
    fb, g2, s2 = (vr[i : i + 1, :] for i in range(8, 11))
    nrm, r = stats(nt(ctx[...], weight(wo, 0, D)) + ob + xr[...].astype(F32))
    n1[...] = nrm
    r1[...] = jnp.broadcast_to(r, (T, 128))
    h1[...] = (nrm * g1 + s1).astype(BF)
    h1b[...] = nn(h1[...], swap[...]).astype(BF)
    big[...] = h1b[...].astype(F32) + fb
    keep = []
    for f in range(4):
        cols = slice(f * FQ, (f + 1) * FQ)
        wait_weight(wi, f * FQ, FQ, sems.at[1 + f])
        bias, at = (inb, 0) if f & 1 == 0 else (others, D)
        bias = bias[pl.ds(at + (f >> 1) * FQ, FQ)].reshape(1, FQ)
        u = nn((h1 if f < 2 else h1b)[...], weight(wi, f * FQ, FQ)) + bias
        phi = 0.5 + 0.5 * lax.erf(u * INV_SQRT2)
        slope[f] = phi + u * (jnp.exp(-0.5 * u * u) * INV_SQRT2PI)
        keep.append(pltpu.make_async_copy(slope.at[f], slope_out.at[f], keeps.at[f]))
        keep[-1].start()
        g = (u * phi).astype(BF)
        gact[:, cols] = g
        wait_weight(wt, f * FQ, FQ, sems.at[5 + f])
        big[...] += nt(g, weight(wt, f * FQ, FQ))
    n2, r2 = stats(big[...])
    low = (n2 * g2 + s2).astype(BF)
    out[...] = nt(low, order_b[...]).astype(BF)
    y = yr[...].astype(F32)
    sums[1:2, :] = jnp.sum(y * n2, axis=0, keepdims=True)
    sums[2:3, :] = jnp.sum(y, axis=0, keepdims=True)
    d = norm_back(y, n2, r2, g2)
    db[...] = d
    sums[0:1, :] = jnp.sum(d.astype(BF).astype(F32), axis=0, keepdims=True)
    sums[3:8, :] = jnp.zeros((5, D), F32)
    lowt[...] = d.T.astype(BF)
    for f in range(4):
        g = nn(lowt[...], gact[:, f * FQ : (f + 1) * FQ]).astype(BF)
        store_rows(grads, grads1, g, pl.ds((f & 1) * FHALF + (f >> 1) * FQ, FQ))
    for k in keep:
        k.wait()


def down_units(units, df, wi, wt, slope, big, h1t, swap, grads, grads1, step, sems, keep):
    sums = []
    for i, f in enumerate(units):
        wait_weight(wt, i * FQ, FQ, sems.at[2 * i])
        keep[i].wait()
        du = (nn(df, weight(wt, i * FQ, FQ)) * slope[i]).astype(BF)
        sums.append(jnp.sum(du.astype(F32), axis=0, keepdims=True))
        wait_weight(wi, i * FQ, FQ, sems.at[2 * i + 1])
        big[...] += nt(du, weight(wi, i * FQ, FQ))
        g = nn(h1t[...], du).astype(BF)
        store_rows(grads, grads1, g, pl.ds(i * step + step - FQ, FQ))
    return sums


def start_units(units, ap, bp, wi, wt, slope_in, slope, sems, keeps):
    keep = []
    for i, f in enumerate(units):
        first, col, m = unit_source(f)
        start_weight(bp, (f >> 1) * FQ, FQ, wt, i * FQ, m, sems.at[2 * i])
        keep.append(pltpu.make_async_copy(slope_in.at[f], slope.at[i], keeps.at[i]))
        keep[-1].start()
        start_weight(ap if first else bp, col, FQ, wi, i * FQ, m, sems.at[2 * i + 1])
    return keep


def down_kernel0(
    h1, db, swap, slope_in, b0, b1, b2, b3, b4, b5, b6, b7, b8, b9,
    h1t, df, da, dinb, grads, grads1, wi, wt, slope, big, sems, keeps,
):
    bp = (b0, b1, b2, b3, b4, b5, b6, b7, b8, b9)
    keep = start_units((2, 3), None, bp, wi, wt, slope_in, slope, sems, keeps)
    big[...] = db[...]
    df[...] = db[...].astype(BF)
    h1t[...] = h1[...].astype(F32).T.astype(BF)
    sums = down_units(
        (2, 3), df[...], wi, wt, slope, big, h1t, swap, grads, grads1, FQ, sems, keep
    )
    dinb[...] = jnp.concatenate(sums, axis=1)
    d = big[...]
    hi = d.astype(BF)
    lo = (d - hi.astype(F32)).astype(BF)
    da[...] = nt(hi, swap[...]) + nt(lo, swap[...])


def down_kernel1(
    ctx, h1t, n1, r1, df, da_in, dinb, sums, vr, order_a, order_b, slope_in,
    a0, a1, a2, a3, a4, a5, a6, a7, a8, a9, b0, b1, b2, b3, b4, b5, b6, b7, b8, b9,
    dc, dr, grads, grads1,
    wo, wi, wt, slope, big, lowt, sems, keeps,
):
    ap = (a0, a1, a2, a3, a4, a5, a6, a7, a8, a9)
    bp = (b0, b1, b2, b3, b4, b5, b6, b7, b8, b9)
    keep = start_units((0, 1), ap, bp, wi, wt, slope_in, slope, sems, keeps)
    for m in range(2):
        start_weight(ap, 3 * HALF, HALF, wo, m * HALF, m, sems.at[4])
    big[...] = da_in[...]
    inner = down_units(
        (0, 1), df[...], wi, wt, slope, big, h1t, None, grads, grads1, CQ, sems, keep
    )
    dh = big[...]
    nrm = n1[...]
    g1 = vr[1:2, :]
    dg1 = jnp.sum(dh * nrm, axis=0, keepdims=True)
    ds1 = jnp.sum(dh, axis=0, keepdims=True)
    d = norm_back(dh, nrm, r1[:, 0:1], g1)
    dr[...] = d
    da = d.astype(BF)
    dob = jnp.sum(da.astype(F32), axis=0, keepdims=True)
    wait_weight(wo, 0, D, sems.at[4])
    dc[...] = nn(da, weight(wo, 0, D)).astype(BF)
    lowt[...] = d.T.astype(BF)
    g = nn(lowt[...], ctx[...]).astype(BF)
    for m in range(2):
        store_rows(grads, grads1, g[:, m * HALF : (m + 1) * HALF], pl.ds(m * CQ, HALF))
    sa = exact(
        jnp.concatenate([dob, dg1, ds1, dob, dob, dob, dob, dob], axis=0),
        order_a[...].astype(F32),
        ((1,), (1,)),
    )
    sb = exact(sums[...], order_b[...].astype(F32), ((1,), (1,)))
    sides = []
    for m in range(2):
        line = jnp.concatenate(
            [inner[m], dinb[:, m * FQ : (m + 1) * FQ]]
            + [sa[i : i + 1] for i in range(3)]
            + [sb[i : i + 1] for i in range(3)]
            + [jnp.zeros((1, 6 * CQ - 8 * FQ), F32)],
            axis=1,
        )
        rows = [line[:, i * CQ : (i + 1) * CQ] for i in range(6)]
        sides.append(jnp.concatenate(rows + [jnp.zeros((2, CQ), F32)], axis=0))
    store_vectors(grads, grads1, jnp.concatenate(sides, axis=1).astype(BF))


def back_half(m, index, buckets, lengths, q, k, v, dc, lse, xb, w, grads, grads1, mask, dq, dk, dv, big, qb, vb):
    mask[...] = mask_bias((index, buckets, lengths), 0)
    lane = lax.broadcasted_iota(jnp.int32, (1, 128), 1)

    def pair(i, _):
        head = pl.ds(pl.multiple_of(m * HALF + i * 128, 128), 128)
        cols = pl.ds(pl.multiple_of(i * 128, 128), 128)
        q2, k2, v2, c2 = q[:, head], k[:, head], v[:, head], dc[:, head]
        outs = []
        for half in range(2):
            mine = (lane < 64) if half == 0 else (lane >= 64)
            s = nt(jnp.where(mine, k2, BF(0)), q2) + mask[...]
            p = jnp.exp(s - lse[pl.ds(m * 6 + i * 2 + half, 1), :])
            dp = nt(jnp.where(mine, v2, BF(0)), c2)
            delta = jnp.sum(dp * p, axis=0, keepdims=True)
            ds = (p * (dp - delta)).astype(BF)
            outs.append((tn(ds, k2), nn(ds, q2), nn(p.astype(BF), c2)))
        first = lane < 64
        dq2, dk2, dv2 = (jnp.where(first, a, b) for a, b in zip(*outs))
        dq2 = (dq2 * 0.125).astype(BF)
        dk2 = dk2.astype(BF)
        dv2 = dv2.astype(BF)
        dq[:, cols] = dq2
        dk[:, cols] = dk2
        dv[:, cols] = dv2
        qb[:, cols] = jnp.sum(dq2.astype(F32), axis=0, keepdims=True)
        vb[:, cols] = jnp.sum(dv2.astype(F32), axis=0, keepdims=True)
        return 0

    lax.fori_loop(0, 3, pair, 0)
    xt = xb[...].astype(F32).T.astype(BF)
    for i, src in enumerate((dq, dk, dv)):
        at = (m * 3 + i) * HALF
        a = src[...]
        store_rows(grads, grads1, nn(xt, a).astype(BF), pl.ds(i * HALF, HALF))
        big[...] += nt(a, weight(w, at, HALF))
    line = jnp.concatenate([qb[...], vb[...], jnp.zeros((1, HALF), F32)], axis=1)
    line = jnp.concatenate([line, jnp.zeros((7, CQ), F32)], axis=0)
    store_vectors(grads, grads1, line.astype(BF))


def back_kernel0(
    index, buckets, lengths, q, k, v, dc, lse, xb, w, dr, grads, grads1, big, mask, dq, dk, dv, qb, vb
):
    big[...] = dr[...]
    back_half(
        0, index, buckets, lengths, q, k, v, dc, lse, xb, w, grads, grads1, mask, dq, dk, dv, big, qb, vb
    )


def back_kernel1(
    index, buckets, lengths, q, k, v, dc, lse, xb, w, dr, order,
    grads, grads1, gin, mask, dq, dk, dv, big, qb, vb,
):
    big[...] = dr[...]
    back_half(
        1, index, buckets, lengths, q, k, v, dc, lse, xb, w, grads, grads1, mask, dq, dk, dv, big, qb, vb
    )
    gin[...] = big[...].astype(BF)


def last_kernel(gin, order, out):
    out[...] = nt(gin[...], order[...]).astype(BF)


def call(kernel, outs, args, scratch=(), vmem=48, flops=0, smem=0, hbm=(), anyouts=()):
    specs = []
    for i in range(len(args)):
        if i < smem:
            specs.append(pl.BlockSpec(memory_space=pltpu.SMEM))
        elif i in hbm:
            specs.append(pl.BlockSpec(memory_space=pl.ANY))
        else:
            specs.append(pl.BlockSpec(memory_space=VMEM))
    return pl.pallas_call(
        kernel,
        out_shape=[jax.ShapeDtypeStruct(s, d) for s, d in outs],
        in_specs=specs,
        out_specs=[
            pl.BlockSpec(memory_space=pl.ANY if i in anyouts else VMEM) for i in range(len(outs))
        ],
        scratch_shapes=list(scratch),
        compiler_params=pltpu.CompilerParams(vmem_limit_bytes=vmem * 2**20),
        cost_estimate=pl.CostEstimate(flops=flops // 1000, bytes_accessed=1000, transcendentals=0),
    )(*args)


def body(
    hidden_in, buckets, lengths, query_weight, key_weight, value_weight, query_bias, value_bias,
    output_weight, output_bias, first_gain, first_shift, inner_weight, inner_bias, outer_weight,
    outer_bias, second_gain, second_shift, cotangent,
):
    mp = lax.axis_index("mp")
    index = lax.axis_index((*DP, "mp")).astype(jnp.int32).reshape(1)
    info = (index, buckets, lengths)
    (shard,) = call(
        pack_kernel,
        [((3, 4, 2 * CH), BF)],
        (query_weight, key_weight, value_weight, output_weight.T, inner_weight, outer_weight.T),
        vmem=60,
    )
    biases = jnp.concatenate([query_bias, value_bias, inner_bias])
    others = flip(biases, "mp", 1)
    def sides(mine, other):
        return jnp.where(
            mp == 0, jnp.concatenate([mine, other], axis=0), jnp.concatenate([other, mine], axis=0)
        )

    square = ((D, D), BF)
    tokens = ((T, D), BF)
    order_a, order_b, swap, xr, xb, yr, vr = call(
        order_kernel,
        [square, square, square, tokens, tokens, tokens, ((16, D), F32)],
        (
            index,
            hidden_in,
            cotangent,
            output_bias,
            first_gain,
            first_shift,
            outer_bias,
            second_gain,
            second_shift,
        ),
        [VMEM((T, D), BF), VMEM((T, D), BF), pltpu.SemaphoreType.DMA((2,))],
        smem=1,
        hbm=(1, 2),
        vmem=60,
        flops=2 * 10**9,
    )
    pa, pb, (xr, xb, yr, others) = gather(shard, (xr, xb, yr, others))
    q, k, v, ctx, lse, w = call(
        attention_kernel,
        [tokens, tokens, tokens, tokens, ((16, T), F32), ((6, 128, 6 * HALF), BF)],
        (*info, xr, query_bias, value_bias, others, *pa),
        [
            VMEM((6, 128, 6 * HALF), BF),
            VMEM((T, T), F32),
            VMEM((T, 128), F32),
            pltpu.SemaphoreType.DMA(()),
            pltpu.SemaphoreType.DMA(()),
        ],
        smem=3,
        hbm=range(7, 17),
        anyouts=(5,),
        vmem=60,
        flops=10 * 10**9,
    )
    gb, gc, ga = ((4, 96, 2 * FHALF), BF), ((4, 96, 2 * FQ), BF), ((4, 104, 2 * CQ), BF)
    wide, chunks = ((T, D), F32), ((4, T, FQ), F32)
    weights = [VMEM((6, 128, D), BF), VMEM((6, 128, FF), BF), VMEM((6, 128, FF), BF)]
    out, h1, n1, r1, db, sums, slope, grads_b, grads_b1 = call(
        up_kernel,
        [tokens, tokens, wide, ((T, 128), F32), wide, ((8, D), F32), chunks, gb, gb],
        (ctx, xr, yr, vr, inner_bias, others, order_b, swap, *pa, *pb),
        weights
        + [
            VMEM((T, D), BF),
            VMEM((T, FF), BF),
            VMEM((4, T, FQ), F32),
            VMEM((T, D), F32),
            VMEM((D, T), BF),
            pltpu.SemaphoreType.DMA((9,)),
            pltpu.SemaphoreType.DMA((4,)),
        ],
        hbm=range(8, 28),
        anyouts=(6,),
        vmem=60,
        flops=8 * 10**9,
    )
    grads_b1 = flip(grads_b1, AC, 1)
    out_own, out = out, flip(out, "mp", 1)
    half = [VMEM((6, 128, 2 * FQ), BF)] * 2 + [VMEM((2, T, FQ), F32), VMEM((T, D), F32)]
    h1t, df, da, dinb, grads_c, grads_c1 = call(
        down_kernel0,
        [((D, T), BF), tokens, wide, ((1, 2 * FQ), F32), gc, gc],
        (h1, db, swap, slope, *pb),
        half + [pltpu.SemaphoreType.DMA((4,)), pltpu.SemaphoreType.DMA((2,))],
        hbm=range(3, 14),
        vmem=60,
        flops=4 * 10**9,
    )
    b0, b1, b3, bl, br = core_sums([(grads_b, grads_b1)], 96)
    da, b0, b1, b3, bl, br = lax.optimization_barrier((da, b0, b1, b3, bl, br))
    bl, br = flip(bl, AY, 1), flip(br, AY, 3)
    grads_c1 = flip(grads_c1, AC, 1)
    dc, dr, grads_a, grads_a1 = call(
        down_kernel1,
        [tokens, wide, ga, ga],
        (ctx, h1t, n1, r1, df, da, dinb, sums, vr, order_a, order_b, slope, *pa, *pb),
        [VMEM((6, 128, D), BF)]
        + half
        + [VMEM((D, T), BF), pltpu.SemaphoreType.DMA((5,)), pltpu.SemaphoreType.DMA((2,))],
        hbm=range(11, 32),
        vmem=60,
        flops=4 * 10**9,
    )
    b1, b3 = relayed((2 * FHALF,), b1, b3, bl, br)
    dc, b1, b3 = lax.optimization_barrier((dc, b1, b3))
    b1, b3 = flip(b1, AY, 1), flip(b3, AY, 3)
    grads_a1 = flip(grads_a1, AC, 1)
    gq = ((4, 104, CQ), BF)
    scratch = [VMEM((T, T), F32)] + [VMEM((T, HALF), BF)] * 3
    lines = [VMEM((1, HALF), F32)] * 2
    q00, q01, big = call(
        back_kernel0,
        [gq, gq, ((T, D), F32)],
        (*info, q, k, v, dc, lse, xb, w, dr),
        scratch + lines,
        smem=3,
        vmem=60,
        flops=7 * 10**9,
    )
    a0, a1, a3, al, ar = core_sums([(grads_a, grads_a1), (grads_c, grads_c1)], 104)
    (fb,) = call(
        outer_sums_kernel, [((16, 8, 3 * FQ), BF)], (index, b0, b1, b3), smem=1, vmem=24
    )
    big, a0, a1, a3, al, ar, fb, out = lax.optimization_barrier((big, a0, a1, a3, al, ar, fb, out))
    fb = exchanged(fb, (*AX, AZ))
    al, ar = flip(al, AZ, 1), flip(ar, AZ, 3)
    q10, q11, gin = call(
        back_kernel1,
        [gq, gq, tokens],
        (*info, q, k, v, dc, lse, xb, w, big, order_a),
        scratch + [VMEM((T, D), F32)] + lines,
        smem=3,
        vmem=60,
        flops=7 * 10**9,
    )
    q01, q11, al, ar, fb = lax.optimization_barrier((q01, q11, al, ar, fb))
    q01, q11 = flip(q01, AC, 1), flip(q11, AC, 1)
    a1, a3 = relayed((2 * CQ, 2 * FQ), a1, a3, al, ar)
    a1, a3 = flip(a1, AZ, 1), flip(a3, AZ, 3)
    (fq,) = call(
        attention_sums_kernel,
        [((64, 8, CA), BF)],
        (index, q00, q01, q10, q11),
        smem=1,
        vmem=32,
    )
    fq = exchanged(fq, (*AX, AZ, AY))
    (gin,) = call(last_kernel, [tokens], (gin, order_a), vmem=16)
    fa = sent(call(second_kernel, [((32, 2 * CA), BF)] * 4, (a0, a1, a3), vmem=24), AY)
    fa = sent(call(third_kernel, [((20, CA), BF)] * 4, fa, vmem=24), AX)
    small, inner, vector = ((12, HALF), F32), ((12, FHALF), F32), ((D,), F32)
    half = ((HALF,), F32)
    wq, wk, wv, wo, wi, wt, qb, vb, ib, *vecs = call(
        final_kernel,
        [small] * 4 + [inner] * 2 + [half] * 2 + [((FHALF,), F32)] + [vector] * 6,
        (*fa, fb, fq),
        vmem=24,
    )
    layer_out = sides(out_own, out)
    input_grad = sides(gin, flip(gin, "mp", 1)).astype(F32)
    dob, dg1, ds1, dfb, dg2, ds2 = vecs
    return (
        layer_out, input_grad, wq, wk, wv, qb, vb, wo.T, dob, dg1, ds1, wi, ib, wt.T, dfb, dg2, ds2
    )


def solution(mesh):
    torus = Mesh(
        mesh.devices.reshape(2, 4, 4, 2, mesh.shape["mp"]), ("dp_0", "dp_1", "dp_2", "dp_3", "mp")
    )
    row, col, half = P(DP, "mp"), P("mp", DP), P("mp")
    in_specs = (
        P(DP, None), P(DP, None), P(DP, None, None), row, row, row, half, half, col, P(), P(), P(),
        row, half, col, P(), P(), P(), P(DP, None),
    )
    out_specs = (
        P(DP, None), P(DP, None), row, row, row, half, half, col, P(), P(), P(), row, half, col,
        P(), P(), P(),
    )
    return jax.shard_map(body, mesh=torus, in_specs=in_specs, out_specs=out_specs, check_vma=False)
```

```python
import functools

import jax
import jax.numpy as jnp
from jax import lax
from jax.experimental import pallas as pl
from jax.experimental.pallas import tpu as pltpu
from jax.sharding import Mesh
from jax.sharding import PartitionSpec as P

DP = ("dp_0", "dp_1", "dp_2", "dp_3")
AX = ("dp_0", "mp")
AZ, AY, AC = "dp_1", "dp_2", "dp_3"
D = 768
T = 512
DH = 64
FF = 3072
HALF = 384
FHALF = 1536
FQ = 768
CH = 2304
CQ = 1152
CA = 1920
EPS = 1e-12
BF = jnp.bfloat16
F32 = jnp.float32
VMEM = pltpu.VMEM
INV_SQRT2 = 0.7071067811865476
INV_SQRT2PI = 0.3989422804014327


def nn(a, b):
    return lax.dot_general(a, b, (((1,), (0,)), ((), ())), preferred_element_type=F32)


def nt(a, b):
    return lax.dot_general(a, b, (((1,), (1,)), ((), ())), preferred_element_type=F32)


def tn(a, b):
    return lax.dot_general(a, b, (((0,), (0,)), ((), ())), preferred_element_type=F32)


def flip(a, axis, s):
    n = 4 if axis in (AX, AY, AZ) else 2
    return lax.ppermute(a, axis, [(i, i ^ s) for i in range(n)])


def joined(a, axis):
    return jnp.concatenate([a] + [flip(a, axis, s) for s in (1, 2, 3)], axis=1)


def gather(shard, ready):
    a = shard
    p1, p2, p3 = (flip(a, AX, s) for s in (1, 2, 3))
    parts = []
    for first in (0, CH):
        cols = slice(first, first + CH)
        a0, a1, a2, a3 = (p[:, :, cols] for p in (a, p1, p2, p3))
        parts.append(
            jnp.concatenate(
                [jnp.concatenate([a0, a2], axis=1), jnp.concatenate([a1, a3], axis=1)], axis=2
            )
        )
    parts = lax.optimization_barrier((joined(parts[0], AY), joined(parts[1], AZ)))
    near = [[flip(b, axis, s) for s in (1, 3)] for b, axis in zip(parts, (AZ, AY))]
    near, ready = lax.optimization_barrier((near, ready))
    out = []
    for b, axis, (n1, n3) in zip(parts, (AZ, AY), near):
        far = [flip(n1[:, :, :CH], axis, 3), flip(n3[:, :, CH:], axis, 1)]
        own = [b, n1, n3, *far]
        out.append(own + [flip(o, AC, 1) for o in own])
    return *out, ready


def add(*parts):
    total = parts[0].astype(F32)
    for p in parts[1:]:
        total = total + p.astype(F32)
    return total


def low_sum(*parts):
    return add(*parts).astype(BF)


def core_kernel(*refs):
    c0, c1, c3, left, right = refs[-5:]
    pairs = [refs[i : i + 2] for i in range(0, len(refs) - 5, 2)]
    at = 0
    for own, other in pairs:
        rows, n = own.shape[1:]
        for s, dst in ((0, c0), (1, c1), (3, c3), (2, None)):
            total = low_sum(own[s], other[s])
            if s == 2:
                left[:rows, at // 2 : (at + n) // 2] = total[:, : n // 2]
                right[:rows, at // 2 : (at + n) // 2] = total[:, n // 2 :]
                dsts = (left, right)
            else:
                dst[:rows, at : at + n] = total
                dsts = (dst,)
            for d in dsts:
                if rows < d.shape[0]:
                    lo, hi = (at // 2, (at + n) // 2) if s == 2 else (at, at + n)
                    d[rows:, lo:hi] = jnp.zeros((d.shape[0] - rows, hi - lo), BF)
        at += n


def core_sums(pairs, rows):
    n = sum(own.shape[2] for own, _ in pairs)
    whole, half = ((rows, n), BF), ((rows, n // 2), BF)
    return call(
        core_kernel, [whole, whole, whole, half, half], [a for p in pairs for a in p], vmem=32
    )


def relay_kernel(widths, c1, c3, left, right, out1, out3):
    at = 0
    for n in widths:
        h = n // 2
        part = slice(at // 2, at // 2 + h)
        out3[:, at : at + h] = low_sum(c3[:, at : at + h], left[:, part])
        out3[:, at + h : at + n] = c3[:, at + h : at + n]
        out1[:, at : at + h] = c1[:, at : at + h]
        out1[:, at + h : at + n] = low_sum(c1[:, at + h : at + n], right[:, part])
        at += n


def relayed(widths, c1, c3, left, right):
    whole = (c1.shape, BF)
    return call(
        functools.partial(relay_kernel, widths), [whole, whole], (c1, c3, left, right), vmem=24
    )


def pair_kernel(a, a1, b, b1, *outs):
    n = a.shape[2]
    for s in range(4):
        outs[s][:, :n] = low_sum(a[s], a1[s])
        outs[s][:, n:] = low_sum(b[s], b1[s])


def sent(parts, axis):
    return [parts[0]] + [flip(parts[s], axis, s) for s in (1, 2, 3)]


def second_kernel(a0, a1, a3, *outs):
    total = add(a0[...], a1[...], a3[...]).astype(BF)
    for y in range(4):
        for g in range(3):
            at = g * 32 + y * 8
            outs[y][g * 8 : (g + 1) * 8, :] = total[at : at + 8]
        outs[y][24:, :] = total[96:]


def third_kernel(m0, m1, m2, m3, *outs):
    total = add(m0[...], m1[...], m2[...], m3[...])
    for m in range(2):
        part = total[:, m * CQ : (m + 1) * CQ]
        for hi in range(2):
            rows = [part[g * 8 + hi * 4 : g * 8 + hi * 4 + 4] for g in range(3)]
            rows = jnp.concatenate(rows + [part[24:]], axis=0)
            outs[hi * 2 + m][...] = rows.astype(BF)


def last_sums_kernel(index, b0, b1, b3, q0, q1, q2, q3, out):
    (hi0, z0, _, _), m0 = decoded(index[0])
    outer = add(b0[...], b1[...], b3[...])
    attn = add(q0[...], q1[...], q2[...], q3[...])
    blank = jnp.zeros((2, HALF), F32)
    for m in range(2):
        part = jnp.concatenate(
            [outer[:, m * CH : (m + 1) * CH], attn[:96, m * CQ : (m + 1) * CQ]], axis=1
        )
        n = CH + CQ
        vec = [attn[96:97, m * CQ + i * HALF : m * CQ + (i + 1) * HALF] for i in range(2)]
        vec = jnp.concatenate(vec + [blank], axis=0)
        for z in range(4):
            for hi in range(2):
                r0, r1, r2 = (
                    part[g * 32 + z * 8 + hi * 4 : g * 32 + z * 8 + hi * 4 + 4] for g in range(3)
                )
                block = jnp.concatenate(
                    [
                        jnp.concatenate([r0, r2[:, : 5 * HALF]], axis=1),
                        jnp.concatenate([r1, r2[:, 5 * HALF :], vec], axis=1),
                    ],
                    axis=0,
                )
                out[((hi ^ hi0) * 2 + (m ^ m0)) * 4 + (z ^ z0)] = block.astype(BF)


def exchanged(blocks, axes):
    return lax.all_to_all(blocks, axes, 0, 0, tiled=True)


def total_of(blocks):
    total = blocks[0].astype(F32)
    for i in range(1, blocks.shape[0]):
        total = total + blocks[i].astype(F32)
    return total


def final_kernel(n0, n1, n2, n3, blocks, wq, wk, wv, wo, wi, wt, qb, vb, ib, ob, g1, s1, fb, g2, s2):
    total = add(n0[...], n1[...], n2[...], n3[...])
    wo[...] = total[:12, :HALF]
    wi[:, :FQ] = total[:12, HALF:]
    vec = jnp.concatenate([total[12 + i : 13 + i, :CQ] for i in range(6)], axis=1)
    at = 0
    for dst in (ib, ob, g1, s1, fb, g2, s2):
        dst[...] = vec[0, at : at + dst.shape[0]]
        at += dst.shape[0]
    total = total_of(blocks)
    n = CH + CQ
    tail = jnp.concatenate([total[:4, n:], total[4:, n : n + 4 * HALF]], axis=1)
    at = 0
    for dst, first, width in (
        (wt, 0, FHALF), (wi, FQ, FQ), (wq, 0, HALF), (wk, 0, HALF), (wv, 0, HALF)
    ):
        dst[:8, first : first + width] = total[:, at : at + width]
        dst[8:, first : first + width] = tail[:, at : at + width]
        at += width
    qb[...] = total[4, n + 4 * HALF :]
    vb[...] = total[5, n + 4 * HALF :]


def decoded(index):
    return (index >> 6, (index >> 4) & 3, (index >> 2) & 3, (index >> 1) & 1), index & 1


def row_of(vector):
    return vector[...].reshape(1, -1)


def order_matrix(place, swap):
    r = lax.broadcasted_iota(jnp.int32, (1, D), 1)
    j = r & 3
    hi = ((r >> 2) & 1) ^ place[0]
    near, far = (r >> 3) & 3, (r >> 5) & 3
    y = (far if swap else near) ^ place[2]
    z = (near if swap else far) ^ place[1]
    block = r >> 7
    core = jnp.where(block >= 3, 1, 0)
    group = block - 3 * core
    core = core ^ place[3]
    source = (((hi * 4 + z) * 4 + y) * 2 + core) * 12 + group * 4 + j
    rows = lax.broadcasted_iota(jnp.int32, (D, D), 0)
    return jnp.where(rows == source, 1.0, 0.0)


def swap_matrix():
    r = lax.broadcasted_iota(jnp.int32, (1, D), 1)
    source = (r & ~0x78) | ((r & 0x18) << 2) | ((r & 0x60) >> 2)
    rows = lax.broadcasted_iota(jnp.int32, (D, D), 0)
    return jnp.where(rows == source, 1.0, 0.0)


def exact(a, b, dims):
    return lax.dot_general(
        a, b, (dims, ((), ())), preferred_element_type=F32, precision=lax.Precision.HIGHEST
    )


def pack_kernel(wq, wk, wv, wo, wi, wt, out):
    at = 0
    for src, first, n in (
        (wq, 0, HALF),
        (wk, 0, HALF),
        (wv, 0, HALF),
        (wo, 0, HALF),
        (wi, 0, FQ),
        (wt, 0, FHALF),
        (wi, FQ, FQ),
    ):
        for g in range(3):
            out[g, :, at : at + n] = src[g * 4 : (g + 1) * 4, first : first + n]
        at += n


def decoded(index):
    return (index >> 6, (index >> 4) & 3, (index >> 2) & 3, (index >> 1) & 1), index & 1


def row_of(vector):
    return vector[...].reshape(1, -1)


def order_matrix(place, swap):
    r = lax.broadcasted_iota(jnp.int32, (1, D), 1)
    j = r & 3
    hi = ((r >> 2) & 1) ^ place[0]
    near, far = (r >> 3) & 3, (r >> 5) & 3
    y = (far if swap else near) ^ place[2]
    z = (near if swap else far) ^ place[1]
    block = r >> 7
    core = jnp.where(block >= 3, 1, 0)
    group = block - 3 * core
    core = core ^ place[3]
    source = (((hi * 4 + z) * 4 + y) * 2 + core) * 12 + group * 4 + j
    rows = lax.broadcasted_iota(jnp.int32, (D, D), 0)
    return jnp.where(rows == source, 1.0, 0.0)


def swap_matrix():
    r = lax.broadcasted_iota(jnp.int32, (1, D), 1)
    source = (r & ~0x78) | ((r & 0x18) << 2) | ((r & 0x60) >> 2)
    rows = lax.broadcasted_iota(jnp.int32, (D, D), 0)
    return jnp.where(rows == source, 1.0, 0.0)


def exact(a, b, dims):
    return lax.dot_general(
        a, b, (dims, ((), ())), preferred_element_type=F32, precision=lax.Precision.HIGHEST
    )


def order_kernel(
    index, x_all, y_all, ob, g1, s1, fb, g2, s2,
    order_a, order_b, swap, xr, xb, yr, vr, x, y, sems,
):
    place, mp = decoded(index[0])
    rows = pl.ds(pl.multiple_of(mp * T, T), T)
    copies = [
        pltpu.make_async_copy(src.at[rows, :], dst, sems.at[i])
        for i, (src, dst) in enumerate(((x_all, x), (y_all, y)))
    ]
    for c in copies:
        c.start()
    m = order_matrix(place, False)
    order_a[...] = m.astype(BF)
    blank = jnp.zeros((5, D), F32)
    vr[0:8, :] = exact(
        jnp.concatenate([row_of(ob), row_of(g1), row_of(s1), blank], axis=0), m, ((1,), (0,))
    )
    m = order_matrix(place, True)
    order_b[...] = m.astype(BF)
    vr[8:16, :] = exact(
        jnp.concatenate([row_of(fb), row_of(g2), row_of(s2), blank], axis=0), m, ((1,), (0,))
    )
    swap[...] = swap_matrix().astype(BF)
    for c in copies:
        c.wait()
    xr[...] = nn(x[...], order_a[...]).astype(BF)
    xb[...] = nn(x[...], order_b[...]).astype(BF)
    yr[...] = nn(y[...], order_b[...]).astype(BF)


def start_weight(pieces, first, width, dst, at, m, sem):
    for core in range(2):
        for i, z in enumerate((0, 1, 3, 2)):
            src = pieces[core * 5 + i + (m if z == 2 else 0)]
            col = first + (0 if z == 2 else m * CH)
            pltpu.make_async_copy(
                src.at[:, :, pl.ds(col, width)],
                dst.at[pl.ds(core * 3, 3), pl.ds(z * 32, 32), pl.ds(at, width)],
                sem,
            ).start()


def wait_weight(dst, at, width, sem):
    part = dst.at[:, :, pl.ds(at, width)]
    pltpu.make_async_copy(part, part, sem).wait()


def weight(w, at, width):
    return w[:, :, pl.ds(at, width)].reshape(D, width)


def row_starts(info, shape, axis):
    index, buckets, lengths = info
    mp = index[0] & 1
    shift = 7 + buckets[0, mp]
    pos = lax.broadcasted_iota(jnp.int32, shape, axis)
    seq = lax.shift_right_logical(pos, shift)
    within = pos & (lax.shift_left(1, shift) - 1)
    n0, n1, n2, n3 = (lengths[0, mp, i] for i in range(4))
    live = jnp.where(seq == 0, n0, jnp.where(seq == 1, n1, jnp.where(seq == 2, n2, n3)))
    return seq, within < live


def mask_bias(info, key_axis):
    kshape = (T, 1) if key_axis == 0 else (1, T)
    qshape = (1, T) if key_axis == 0 else (T, 1)
    kseq, live = row_starts(info, kshape, key_axis)
    qseq, _ = row_starts(info, qshape, 1 - key_axis)
    kseq = jnp.where(live, kseq, -1)
    return jnp.where(kseq == qseq, 0.0, -1e30)


def attention_kernel(
    index, buckets, lengths, xr, qb, vb, others, p0, p1, p2, p3, p4, p5, p6, p7, p8, p9,
    q, k, v, ctx, lse, w_out, w, qkv, biases, mask, lcol, sem, sem2,
):
    pieces = (p0, p1, p2, p3, p4, p5, p6, p7, p8, p9)
    for m in range(2):
        start_weight(pieces, 0, 3 * HALF, w, m * 3 * HALF, m, sem)
    mask[...] = mask_bias((index, buckets, lengths), 1)
    wait_weight(w, 0, 6 * HALF, sem)
    keep = pltpu.make_async_copy(w, w_out, sem2)
    keep.start()
    zero = jnp.zeros((1, HALF), F32)
    for m in range(2):
        for i, own in enumerate((qb, None, vb)):
            if i == 1:
                b = zero
            elif m == 0:
                b = row_of(own)
            else:
                b = others[pl.ds((i >> 1) * HALF, HALF)].reshape(1, HALF)
            biases[m * 3 + i : m * 3 + i + 1, :] = b

    def project(i, _):
        a = nn(xr[...], weight(w, pl.multiple_of(i * HALF, HALF), HALF)) + biases[pl.ds(i, 1), :]
        scale = jnp.where((i == 0) | (i == 3), 0.125, 1.0)
        qkv[i] = (a.astype(BF).astype(F32) * scale).astype(BF)
        return 0

    lax.fori_loop(0, 6, project, 0)
    for i in range(6):
        (q, k, v)[i % 3][:, (i // 3) * HALF : (i // 3 + 1) * HALF] = qkv[i]
    lcol[...] = jnp.zeros_like(lcol)
    lane = lax.broadcasted_iota(jnp.int32, (1, 128), 1)

    def pair(i, _):
        cols = pl.ds(pl.multiple_of(i * 128, 128), 128)
        q2, k2, v2 = q[:, cols], k[:, cols], v[:, cols]
        total = None
        for half in range(2):
            mine = (lane < 64) if half == 0 else (lane >= 64)
            s = nt(jnp.where(mine, q2, BF(0)), k2) + mask[...]
            peak = jnp.max(s, axis=1, keepdims=True)
            e = jnp.exp(s - peak)
            z = jnp.sum(e, axis=1, keepdims=True)
            p = (e / z).astype(BF)
            c = nn(p, jnp.where(mine, v2, BF(0)))
            total = c if total is None else total + c
            l = peak + jnp.log(z)
            lcol[...] = jnp.where(lane == i * 2 + half, l, lcol[...])
        ctx[:, cols] = total.astype(BF)
        return 0

    lax.fori_loop(0, 6, pair, 0)
    lse[...] = lcol[...].T[0:16, :]
    keep.wait()


def stats(a):
    mean = jnp.mean(a, axis=1, keepdims=True)
    a = a - mean
    r = lax.rsqrt(jnp.mean(a * a, axis=1, keepdims=True) + EPS)
    return a * r, r


def norm_back(dy, n, r, gain):
    a = dy * gain
    return r * (
        a - jnp.mean(a, axis=1, keepdims=True) - n * jnp.mean(a * n, axis=1, keepdims=True)
    )


def store_rows(own, other, value, cols):
    for core, dst in enumerate((own, other)):
        for g in range(3):
            for z in range(4):
                at = ((core * 3 + g) * 4 + z) * 32
                dst[z, g * 32 : (g + 1) * 32, cols] = value[at : at + 32]


def store_vectors(own, other, value):
    for dst in (own, other):
        for z in range(4):
            dst[z, 96:104, :] = value


def unit_source(f):
    return f < 2, (4 * HALF if f < 2 else 2 * FQ), f & 1


def up_kernel(
    ctx, xr, yr, vr, inb, others, order_b, swap,
    a0, a1, a2, a3, a4, a5, a6, a7, a8, a9, b0, b1, b2, b3, b4, b5, b6, b7, b8, b9,
    out, h1t_out, n1_out, r1, df, da, dinb, sums, slope_out, grads_out, grads1_out,
    wo, wi, wt, hs, hts, biases, n1, gact, slope, big, lowt, grads, grads1, sems, keeps, goes,
):
    ap = (a0, a1, a2, a3, a4, a5, a6, a7, a8, a9)
    bp = (b0, b1, b2, b3, b4, b5, b6, b7, b8, b9)
    for m in range(2):
        start_weight(ap, 3 * HALF, HALF, wo, m * HALF, m, sems.at[0])
    for f in range(4):
        first, col, m = unit_source(f)
        start_weight(ap if first else bp, col, FQ, wi, f * FQ, m, sems.at[1 + f])
        start_weight(bp, (f >> 1) * FQ, FQ, wt, f * FQ, m, sems.at[5 + f])
    wait_weight(wo, 0, D, sems.at[0])
    ob, g1, s1 = (vr[i : i + 1, :] for i in range(3))
    fb, g2, s2 = (vr[i : i + 1, :] for i in range(8, 11))
    nrm, r = stats(nt(ctx[...], weight(wo, 0, D)) + ob + xr[...].astype(F32))
    n1[...] = nrm
    keep = []

    def send(src, dst, sem):
        keep.append(pltpu.make_async_copy(src, dst, sem))
        keep[-1].start()

    send(n1, n1_out, keeps.at[2])
    r1[...] = jnp.broadcast_to(r, (T, 128))
    low = nrm * g1 + s1
    hs[0] = low.astype(BF)
    hts[0] = low.T.astype(BF)
    send(hts.at[0], h1t_out, keeps.at[3])
    low = nn(hs[0], swap[...])
    hs[1] = low.astype(BF)
    hts[1] = low.T.astype(BF)
    big[...] = hs[1].astype(F32) + fb
    for f in range(4):
        bias, at = (inb, 0) if f & 1 == 0 else (others, D)
        biases[f : f + 1, :] = bias[pl.ds(at + (f >> 1) * FQ, FQ)].reshape(1, FQ)

    def up(f, _):
        at = pl.multiple_of(f * FQ, FQ)
        wait_weight(wi, at, FQ, sems.at[1 + f])
        u = nn(hs[f >> 1], weight(wi, at, FQ)) + biases[pl.ds(f, 1), :]
        phi = 0.5 + 0.5 * lax.erf(u * INV_SQRT2)
        slope[f] = phi + u * (jnp.exp(-0.5 * u * u) * INV_SQRT2PI)

        @pl.when(f < 2)
        def _():
            pltpu.make_async_copy(slope.at[f], slope_out.at[f], keeps.at[f]).start()

        g = (u * phi).astype(BF)
        gact[:, pl.ds(at, FQ)] = g
        wait_weight(wt, at, FQ, sems.at[5 + f])
        big[...] += nt(g, weight(wt, at, FQ))
        return 0

    lax.fori_loop(0, 4, up, 0)
    keep += [pltpu.make_async_copy(slope.at[f], slope_out.at[f], keeps.at[f]) for f in range(2)]
    n2, r2 = stats(big[...])
    low = (n2 * g2 + s2).astype(BF)
    out[...] = nt(low, order_b[...]).astype(BF)
    y = yr[...].astype(F32)
    sums[1:2, :] = jnp.sum(y * n2, axis=0, keepdims=True)
    sums[2:3, :] = jnp.sum(y, axis=0, keepdims=True)
    d = norm_back(y, n2, r2, g2)
    big[...] = d
    low = d.astype(BF)
    df[...] = low
    sums[0:1, :] = jnp.sum(low.astype(F32), axis=0, keepdims=True)
    sums[3:8, :] = jnp.zeros((5, D), F32)
    lowt[...] = d.T.astype(BF)

    def go(first, width, sem):
        for k, (src, dst) in enumerate(((grads, grads_out), (grads1, grads1_out))):
            cols = pl.ds(first, width)
            yield pltpu.make_async_copy(src.at[:, :, cols], dst.at[:, :, cols], sem(k))

    def outer(f, _):
        g = nn(lowt[...], gact[:, pl.ds(pl.multiple_of(f * FQ, FQ), FQ)]).astype(BF)
        at = pl.multiple_of((f & 1) * CH + (f >> 1) * FQ, FQ)
        store_rows(grads, grads1, g, pl.ds(at, FQ))

        @pl.when(f >= 2)
        def _():
            for c in go(pl.multiple_of((f & 1) * CH, CH), FHALF, lambda k: goes.at[k, f & 1]):
                c.start()

        return 0

    lax.fori_loop(0, 4, outer, 0)

    def inner(m, _):
        f = m + 2
        at = pl.multiple_of(f * FQ, FQ)
        du = (nn(df[...], weight(wt, at, FQ)) * slope[f]).astype(BF)
        dinb[:, pl.ds(pl.multiple_of(m * FQ, FQ), FQ)] = jnp.sum(
            du.astype(F32), axis=0, keepdims=True
        )
        big[...] += nt(du, weight(wi, at, FQ))
        g = nn(hts[1], du).astype(BF)
        to = pl.multiple_of(m * CH + FHALF, FQ)
        store_rows(grads, grads1, g, pl.ds(to, FQ))
        for c in go(to, FQ, lambda k: goes.at[2 + k, m]):
            c.start()
        return 0

    lax.fori_loop(0, 2, inner, 0)
    for m in range(2):
        keep += list(go(m * CH, FHALF, lambda k, m=m: goes.at[k, m]))
        keep += list(go(m * CH + FHALF, FQ, lambda k, m=m: goes.at[2 + k, m]))
    d = big[...]
    hi = d.astype(BF)
    lo = (d - hi.astype(F32)).astype(BF)
    da[...] = nt(hi, swap[...]) + nt(lo, swap[...])
    for k in keep:
        k.wait()


def down_units(df, wi, wt, slope, big, h1t, dinb, grads, grads1, sems, keeps, slope_in):
    def down(f, _):
        at = pl.multiple_of(f * FQ, FQ)
        wait_weight(wt, at, FQ, sems.at[2 * f])
        pltpu.make_async_copy(slope_in.at[f], slope.at[f], keeps.at[f]).wait()
        du = (nn(df[...], weight(wt, at, FQ)) * slope[f]).astype(BF)
        dinb[pl.ds(f, 1), :] = jnp.sum(du.astype(F32), axis=0, keepdims=True)
        wait_weight(wi, at, FQ, sems.at[2 * f + 1])
        big[...] += nt(du, weight(wi, at, FQ))
        g = nn(h1t[...], du).astype(BF)
        store_rows(grads, grads1, g, pl.ds(pl.multiple_of(f * CQ + HALF, HALF), FQ))
        return 0

    lax.fori_loop(0, 2, down, 0)


def start_units(units, ap, bp, wi, wt, slope_in, slope, sems, keeps):
    for i, f in enumerate(units):
        first, col, m = unit_source(f)
        start_weight(bp, (f >> 1) * FQ, FQ, wt, i * FQ, m, sems.at[2 * i])
        pltpu.make_async_copy(slope_in.at[f], slope.at[i], keeps.at[i]).start()
        start_weight(ap if first else bp, col, FQ, wi, i * FQ, m, sems.at[2 * i + 1])


def down_kernel1(
    ctx, h1t, n1, r1, df, da_in, dinb, sums, vr, order_a, order_b, slope_in,
    a0, a1, a2, a3, a4, a5, a6, a7, a8, a9, b0, b1, b2, b3, b4, b5, b6, b7, b8, b9,
    dc, dr, grads, grads1,
    wo, wi, wt, slope, big, lowt, inner, sems, keeps,
):
    ap = (a0, a1, a2, a3, a4, a5, a6, a7, a8, a9)
    bp = (b0, b1, b2, b3, b4, b5, b6, b7, b8, b9)
    start_units((0, 1), ap, bp, wi, wt, slope_in, slope, sems, keeps)
    for m in range(2):
        start_weight(ap, 3 * HALF, HALF, wo, m * HALF, m, sems.at[4])
    big[...] = da_in[...]
    down_units(df, wi, wt, slope, big, h1t, inner, grads, grads1, sems, keeps, slope_in)
    dh = big[...]
    nrm = n1[...]
    g1 = vr[1:2, :]
    dg1 = jnp.sum(dh * nrm, axis=0, keepdims=True)
    ds1 = jnp.sum(dh, axis=0, keepdims=True)
    d = norm_back(dh, nrm, r1[:, 0:1], g1)
    dr[...] = d
    da = d.astype(BF)
    dob = jnp.sum(da.astype(F32), axis=0, keepdims=True)
    wait_weight(wo, 0, D, sems.at[4])
    dc[...] = nn(da, weight(wo, 0, D)).astype(BF)
    lowt[...] = d.T.astype(BF)
    g = nn(lowt[...], ctx[...]).astype(BF)
    for m in range(2):
        store_rows(grads, grads1, g[:, m * HALF : (m + 1) * HALF], pl.ds(m * CQ, HALF))
    sa = exact(
        jnp.concatenate([dob, dg1, ds1, dob, dob, dob, dob, dob], axis=0),
        order_a[...].astype(F32),
        ((1,), (1,)),
    )
    sb = exact(sums[...], order_b[...].astype(F32), ((1,), (1,)))
    sides = []
    for m in range(2):
        line = jnp.concatenate(
            [inner[m : m + 1, :], dinb[:, m * FQ : (m + 1) * FQ]]
            + [sa[i : i + 1] for i in range(3)]
            + [sb[i : i + 1] for i in range(3)]
            + [jnp.zeros((1, 6 * CQ - 8 * FQ), F32)],
            axis=1,
        )
        rows = [line[:, i * CQ : (i + 1) * CQ] for i in range(6)]
        sides.append(jnp.concatenate(rows + [jnp.zeros((2, CQ), F32)], axis=0))
    store_vectors(grads, grads1, jnp.concatenate(sides, axis=1).astype(BF))


def back_half(m, index, buckets, lengths, q, k, v, dc, lse, xb, w, grads, grads1, mask, dqkv, big, qb, vb, xt_ref):
    mask[...] = mask_bias((index, buckets, lengths), 0)
    lane = lax.broadcasted_iota(jnp.int32, (1, 128), 1)

    def pair(i, _):
        head = pl.ds(pl.multiple_of(m * HALF + i * 128, 128), 128)
        cols = pl.ds(pl.multiple_of(i * 128, 128), 128)
        q2, k2, v2, c2 = q[:, head], k[:, head], v[:, head], dc[:, head]
        outs = []
        for half in range(2):
            mine = (lane < 64) if half == 0 else (lane >= 64)
            s = nt(jnp.where(mine, k2, BF(0)), q2) + mask[...]
            p = jnp.exp(s - lse[pl.ds(m * 6 + i * 2 + half, 1), :])
            dp = nt(jnp.where(mine, v2, BF(0)), c2)
            delta = jnp.sum(dp * p, axis=0, keepdims=True)
            ds = (p * (dp - delta)).astype(BF)
            outs.append((tn(ds, k2), nn(ds, q2), nn(p.astype(BF), c2)))
        first = lane < 64
        dq2, dk2, dv2 = (jnp.where(first, a, b) for a, b in zip(*outs))
        dq2 = (dq2 * 0.125).astype(BF)
        dk2 = dk2.astype(BF)
        dv2 = dv2.astype(BF)
        dqkv[0, :, cols] = dq2
        dqkv[1, :, cols] = dk2
        dqkv[2, :, cols] = dv2
        qb[:, cols] = jnp.sum(dq2.astype(F32), axis=0, keepdims=True)
        vb[:, cols] = jnp.sum(dv2.astype(F32), axis=0, keepdims=True)
        return 0

    lax.fori_loop(0, 3, pair, 0)
    xt = xb[...].astype(F32).T.astype(BF)
    xt_ref[...] = xt

    def weights(i, _):
        to = pl.multiple_of(i * HALF, HALF)
        a = dqkv[i]
        store_rows(grads, grads1, nn(xt_ref[...], a).astype(BF), pl.ds(to, HALF))
        big[...] += nt(a, weight(w, pl.multiple_of(m * 3 * HALF + i * HALF, HALF), HALF))
        return 0

    lax.fori_loop(0, 3, weights, 0)
    line = jnp.concatenate([qb[...], vb[...], jnp.zeros((1, HALF), F32)], axis=1)
    line = jnp.concatenate([line, jnp.zeros((7, CQ), F32)], axis=0)
    store_vectors(grads, grads1, line.astype(BF))


def back_kernel0(
    index, buckets, lengths, q, k, v, dc, lse, xb, w, dr, grads, grads1, big, mask, dqkv, qb, vb, xt
):
    big[...] = dr[...]
    back_half(
        0, index, buckets, lengths, q, k, v, dc, lse, xb, w, grads, grads1, mask, dqkv, big, qb, vb, xt
    )


def back_kernel1(
    index, buckets, lengths, q, k, v, dc, lse, xb, w, dr, order,
    grads, grads1, gin, mask, dqkv, big, qb, vb, xt,
):
    big[...] = dr[...]
    back_half(
        1, index, buckets, lengths, q, k, v, dc, lse, xb, w, grads, grads1, mask, dqkv, big, qb, vb, xt
    )
    gin[...] = big[...].astype(BF)


def last_kernel(gin, order, out):
    out[...] = nt(gin[...], order[...]).astype(BF)


def call(kernel, outs, args, scratch=(), vmem=48, flops=0, smem=0, hbm=(), anyouts=()):
    specs = []
    for i in range(len(args)):
        if i < smem:
            specs.append(pl.BlockSpec(memory_space=pltpu.SMEM))
        elif i in hbm:
            specs.append(pl.BlockSpec(memory_space=pl.ANY))
        else:
            specs.append(pl.BlockSpec(memory_space=VMEM))
    return pl.pallas_call(
        kernel,
        out_shape=[jax.ShapeDtypeStruct(s, d) for s, d in outs],
        in_specs=specs,
        out_specs=[
            pl.BlockSpec(memory_space=pl.ANY if i in anyouts else VMEM) for i in range(len(outs))
        ],
        scratch_shapes=list(scratch),
        compiler_params=pltpu.CompilerParams(vmem_limit_bytes=vmem * 2**20),
        cost_estimate=pl.CostEstimate(flops=flops // 1000, bytes_accessed=1000, transcendentals=0),
    )(*args)


def body(
    hidden_in, buckets, lengths, query_weight, key_weight, value_weight, query_bias, value_bias,
    output_weight, output_bias, first_gain, first_shift, inner_weight, inner_bias, outer_weight,
    outer_bias, second_gain, second_shift, cotangent,
):
    mp = lax.axis_index("mp")
    index = lax.axis_index((*DP, "mp")).astype(jnp.int32).reshape(1)
    info = (index, buckets, lengths)
    (shard,) = call(
        pack_kernel,
        [((3, 4, 2 * CH), BF)],
        (query_weight, key_weight, value_weight, output_weight.T, inner_weight, outer_weight.T),
        vmem=60,
    )
    biases = jnp.concatenate([query_bias, value_bias, inner_bias])
    others = flip(biases, "mp", 1)
    def sides(mine, other):
        return jnp.where(
            mp == 0, jnp.concatenate([mine, other], axis=0), jnp.concatenate([other, mine], axis=0)
        )

    square = ((D, D), BF)
    tokens = ((T, D), BF)
    order_a, order_b, swap, xr, xb, yr, vr = call(
        order_kernel,
        [square, square, square, tokens, tokens, tokens, ((16, D), F32)],
        (
            index,
            hidden_in,
            cotangent,
            output_bias,
            first_gain,
            first_shift,
            outer_bias,
            second_gain,
            second_shift,
        ),
        [VMEM((T, D), BF), VMEM((T, D), BF), pltpu.SemaphoreType.DMA((2,))],
        smem=1,
        hbm=(1, 2),
        vmem=60,
        flops=2 * 10**9,
    )
    pa, pb, (xr, xb, yr, others) = gather(shard, (xr, xb, yr, others))
    q, k, v, ctx, lse, w = call(
        attention_kernel,
        [tokens, tokens, tokens, tokens, ((16, T), F32), ((6, 128, 6 * HALF), BF)],
        (*info, xr, query_bias, value_bias, others, *pa),
        [
            VMEM((6, 128, 6 * HALF), BF),
            VMEM((6, T, HALF), BF),
            VMEM((8, HALF), F32),
            VMEM((T, T), F32),
            VMEM((T, 128), F32),
            pltpu.SemaphoreType.DMA(()),
            pltpu.SemaphoreType.DMA(()),
        ],
        smem=3,
        hbm=range(7, 17),
        anyouts=(5,),
        vmem=60,
        flops=10 * 10**9,
    )
    gb, ga = ((4, 96, 2 * CH), BF), ((4, 104, 2 * CQ), BF)
    wide = ((T, D), F32)
    out, h1t, n1, r1, df, da, dinb, sums, slope, grads_b, grads_b1 = call(
        up_kernel,
        [
            tokens,
            ((D, T), BF),
            wide,
            ((T, 128), F32),
            tokens,
            wide,
            ((1, 2 * FQ), F32),
            ((8, D), F32),
            ((2, T, FQ), F32),
            gb,
            gb,
        ],
        (ctx, xr, yr, vr, inner_bias, others, order_b, swap, *pa, *pb),
        [
            VMEM((6, 128, D), BF),
            VMEM((6, 128, FF), BF),
            VMEM((6, 128, FF), BF),
            VMEM((2, T, D), BF),
            VMEM((2, D, T), BF),
            VMEM((8, FQ), F32),
            VMEM((T, D), F32),
            VMEM((T, FF), BF),
            VMEM((4, T, FQ), F32),
            VMEM((T, D), F32),
            VMEM((D, T), BF),
            VMEM(*gb),
            VMEM(*gb),
            pltpu.SemaphoreType.DMA((9,)),
            pltpu.SemaphoreType.DMA((4,)),
            pltpu.SemaphoreType.DMA((4, 2)),
        ],
        hbm=range(8, 28),
        anyouts=(1, 2, 8, 9, 10),
        vmem=56,
        flops=8 * 10**9,
    )
    grads_b1 = flip(grads_b1, AC, 1)
    out_own, out = out, flip(out, "mp", 1)
    half = [VMEM((6, 128, 2 * FQ), BF)] * 2 + [VMEM((2, T, FQ), F32), VMEM((T, D), F32)]
    dc, dr, grads_a, grads_a1 = call(
        down_kernel1,
        [tokens, wide, ga, ga],
        (ctx, h1t, n1, r1, df, da, dinb, sums, vr, order_a, order_b, slope, *pa, *pb),
        [VMEM((6, 128, D), BF)]
        + half
        + [VMEM((D, T), BF), VMEM((8, FQ), F32), pltpu.SemaphoreType.DMA((5,)), pltpu.SemaphoreType.DMA((2,))],
        hbm=range(11, 32),
        vmem=60,
        flops=4 * 10**9,
    )
    b0, b1, b3, bl, br = core_sums([(grads_b, grads_b1)], 96)
    dc, b0, b1, b3, bl, br = lax.optimization_barrier((dc, b0, b1, b3, bl, br))
    bl, br = flip(bl, AY, 1), flip(br, AY, 3)
    grads_a1 = flip(grads_a1, AC, 1)
    gq = ((4, 104, CQ), BF)
    scratch = [VMEM((T, T), F32), VMEM((3, T, HALF), BF)]
    lines = [VMEM((1, HALF), F32)] * 2 + [VMEM((D, T), BF)]
    q00, q01, big = call(
        back_kernel0,
        [gq, gq, ((T, D), F32)],
        (*info, q, k, v, dc, lse, xb, w, dr),
        scratch + lines,
        smem=3,
        vmem=60,
        flops=7 * 10**9,
    )
    b1, b3 = relayed((2 * CH,), b1, b3, bl, br)
    a0, a1, a3, al, ar = core_sums([(grads_a, grads_a1)], 104)
    big, b1, b3, a0, a1, a3, al, ar, out = lax.optimization_barrier(
        (big, b1, b3, a0, a1, a3, al, ar, out)
    )
    b1, b3 = flip(b1, AY, 1), flip(b3, AY, 3)
    al, ar = flip(al, AZ, 1), flip(ar, AZ, 3)
    q10, q11, gin = call(
        back_kernel1,
        [gq, gq, tokens],
        (*info, q, k, v, dc, lse, xb, w, big, order_a),
        scratch + [VMEM((T, D), F32)] + lines,
        smem=3,
        vmem=60,
        flops=7 * 10**9,
    )
    q01, q11, al, ar, b1, b3 = lax.optimization_barrier((q01, q11, al, ar, b1, b3))
    q01, q11 = flip(q01, AC, 1), flip(q11, AC, 1)
    rq = call(pair_kernel, [((104, 2 * CQ), BF)] * 4, (q00, q01, q10, q11), vmem=24)
    rq, al, ar = lax.optimization_barrier((rq, al, ar))
    a1, a3 = relayed((2 * CQ,), a1, a3, al, ar)
    a1, a3 = flip(a1, AZ, 1), flip(a3, AZ, 3)
    rq = sent(rq, AY)
    gin, rq[1] = lax.optimization_barrier((gin, rq[1]))
    (gin,) = call(last_kernel, [tokens], (gin, order_a), vmem=16)
    theirs = flip(gin, "mp", 1)
    rq, a1, a3, theirs = lax.optimization_barrier((rq, a1, a3, theirs))
    fa = sent(call(second_kernel, [((32, 2 * CQ), BF)] * 4, (a0, a1, a3), vmem=24), AY)
    fa = sent(call(third_kernel, [((20, CQ), BF)] * 4, fa, vmem=24), AX)
    (blocks,) = call(
        last_sums_kernel,
        [((16, 8, 14 * HALF), BF)],
        (index, b0, b1, b3, *rq),
        smem=1,
        vmem=32,
    )
    blocks = exchanged(blocks, (*AX, AZ))
    small, inner, vector = ((12, HALF), F32), ((12, FHALF), F32), ((D,), F32)
    half = ((HALF,), F32)
    wq, wk, wv, wo, wi, wt, qb, vb, ib, *vecs = call(
        final_kernel,
        [small] * 4 + [inner] * 2 + [half] * 2 + [((FHALF,), F32)] + [vector] * 6,
        (*fa, blocks),
        vmem=24,
    )
    layer_out = sides(out_own, out)
    input_grad = sides(gin, theirs).astype(F32)
    dob, dg1, ds1, dfb, dg2, ds2 = vecs
    return (
        layer_out, input_grad, wq, wk, wv, qb, vb, wo.T, dob, dg1, ds1, wi, ib, wt.T, dfb, dg2, ds2
    )


def solution(mesh):
    torus = Mesh(
        mesh.devices.reshape(2, 4, 4, 2, mesh.shape["mp"]), ("dp_0", "dp_1", "dp_2", "dp_3", "mp")
    )
    row, col, half = P(DP, "mp"), P("mp", DP), P("mp")
    in_specs = (
        P(DP, None), P(DP, None), P(DP, None, None), row, row, row, half, half, col, P(), P(), P(),
        row, half, col, P(), P(), P(), P(DP, None),
    )
    out_specs = (
        P(DP, None), P(DP, None), row, row, row, half, half, col, P(), P(), P(), row, half, col,
        P(), P(), P(),
    )
    return jax.shard_map(body, mesh=torus, in_specs=in_specs, out_specs=out_specs, check_vma=False)
```

```python
import functools

import jax
import jax.numpy as jnp
from jax import lax
from jax.experimental import pallas as pl
from jax.experimental.pallas import tpu as pltpu
from jax.sharding import Mesh
from jax.sharding import PartitionSpec as P

DP = ("dp_0", "dp_1", "dp_2", "dp_3")
AX = ("dp_0", "mp")
AZ, AY, AC = "dp_1", "dp_2", "dp_3"
D = 768
T = 512
DH = 64
FF = 3072
HALF = 384
FHALF = 1536
FQ = 768
CH = 2304
CQ = 1152
CA = 1920
EPS = 1e-12
BF = jnp.bfloat16
F32 = jnp.float32
VMEM = pltpu.VMEM
INV_SQRT2 = 0.7071067811865476
INV_SQRT2PI = 0.3989422804014327


def nn(a, b):
    return lax.dot_general(a, b, (((1,), (0,)), ((), ())), preferred_element_type=F32)


def nt(a, b):
    return lax.dot_general(a, b, (((1,), (1,)), ((), ())), preferred_element_type=F32)


def tn(a, b):
    return lax.dot_general(a, b, (((0,), (0,)), ((), ())), preferred_element_type=F32)


def flip(a, axis, s):
    n = 4 if axis in (AX, AY, AZ) else 2
    return lax.ppermute(a, axis, [(i, i ^ s) for i in range(n)])


def joined(a, axis):
    return jnp.concatenate([a] + [flip(a, axis, s) for s in (1, 2, 3)], axis=1)


def gather(shard, ready):
    a = shard
    p1, p2, p3 = (flip(a, AX, s) for s in (1, 2, 3))
    parts = []
    for first in (0, CH):
        cols = slice(first, first + CH)
        a0, a1, a2, a3 = (p[:, :, cols] for p in (a, p1, p2, p3))
        parts.append(
            jnp.concatenate(
                [jnp.concatenate([a0, a2], axis=1), jnp.concatenate([a1, a3], axis=1)], axis=2
            )
        )
    parts = lax.optimization_barrier((joined(parts[0], AY), joined(parts[1], AZ)))
    near = [[flip(b, axis, s) for s in (1, 3)] for b, axis in zip(parts, (AZ, AY))]
    near, ready = lax.optimization_barrier((near, ready))
    out = []
    for b, axis, (n1, n3) in zip(parts, (AZ, AY), near):
        far = [flip(n1[:, :, :CH], axis, 3), flip(n3[:, :, CH:], axis, 1)]
        own = [b, n1, n3, *far]
        out.append(own + [flip(o, AC, 1) for o in own])
    return *out, ready


def add(*parts):
    total = parts[0].astype(F32)
    for p in parts[1:]:
        total = total + p.astype(F32)
    return total


def low_sum(*parts):
    return add(*parts).astype(BF)


def core_kernel(*refs):
    c0, c1, c3, left, right = refs[-5:]
    pairs = [refs[i : i + 2] for i in range(0, len(refs) - 5, 2)]
    at = 0
    for own, other in pairs:
        rows, n = own.shape[1:]
        for s, dst in ((0, c0), (1, c1), (3, c3), (2, None)):
            total = low_sum(own[s], other[s])
            if s == 2:
                left[:rows, at // 2 : (at + n) // 2] = total[:, : n // 2]
                right[:rows, at // 2 : (at + n) // 2] = total[:, n // 2 :]
                dsts = (left, right)
            else:
                dst[:rows, at : at + n] = total
                dsts = (dst,)
            for d in dsts:
                if rows < d.shape[0]:
                    lo, hi = (at // 2, (at + n) // 2) if s == 2 else (at, at + n)
                    d[rows:, lo:hi] = jnp.zeros((d.shape[0] - rows, hi - lo), BF)
        at += n


def core_sums(pairs, rows):
    n = sum(own.shape[2] for own, _ in pairs)
    whole, half = ((rows, n), BF), ((rows, n // 2), BF)
    return call(
        core_kernel, [whole, whole, whole, half, half], [a for p in pairs for a in p], vmem=32
    )


def relay_kernel(widths, c1, c3, left, right, out1, out3):
    at = 0
    for n in widths:
        h = n // 2
        part = slice(at // 2, at // 2 + h)
        out3[:, at : at + h] = low_sum(c3[:, at : at + h], left[:, part])
        out3[:, at + h : at + n] = c3[:, at + h : at + n]
        out1[:, at : at + h] = c1[:, at : at + h]
        out1[:, at + h : at + n] = low_sum(c1[:, at + h : at + n], right[:, part])
        at += n


def relayed(widths, c1, c3, left, right):
    whole = (c1.shape, BF)
    return call(
        functools.partial(relay_kernel, widths), [whole, whole], (c1, c3, left, right), vmem=24
    )


def pair_kernel(a, a1, b, b1, *outs):
    n = a.shape[2]
    for s in range(4):
        outs[s][:, :n] = low_sum(a[s], a1[s])
        outs[s][:, n:] = low_sum(b[s], b1[s])


def sent(parts, axis):
    return [parts[0]] + [flip(parts[s], axis, s) for s in (1, 2, 3)]


def second_kernel(a0, a1, a3, *outs):
    total = add(a0[...], a1[...], a3[...]).astype(BF)
    for y in range(4):
        for g in range(3):
            at = g * 32 + y * 8
            outs[y][g * 8 : (g + 1) * 8, :] = total[at : at + 8]
        outs[y][24:, :] = total[96:]


def third_kernel(m0, m1, m2, m3, *outs):
    total = add(m0[...], m1[...], m2[...], m3[...])
    for m in range(2):
        part = total[:, m * CQ : (m + 1) * CQ]
        for hi in range(2):
            rows = [part[g * 8 + hi * 4 : g * 8 + hi * 4 + 4] for g in range(3)]
            rows = jnp.concatenate(rows + [part[24:]], axis=0)
            outs[hi * 2 + m][...] = rows.astype(BF)


def last_sums_kernel(index, b0, b1, b3, q0, q1, q2, q3, out):
    (hi0, z0, _, _), m0 = decoded(index[0])
    outer = add(b0[...], b1[...], b3[...])
    attn = add(q0[...], q1[...], q2[...], q3[...])
    blank = jnp.zeros((2, HALF), F32)
    for m in range(2):
        part = jnp.concatenate(
            [outer[:, m * CH : (m + 1) * CH], attn[:96, m * CQ : (m + 1) * CQ]], axis=1
        )
        n = CH + CQ
        vec = [attn[96:97, m * CQ + i * HALF : m * CQ + (i + 1) * HALF] for i in range(2)]
        vec = jnp.concatenate(vec + [blank], axis=0)
        for z in range(4):
            for hi in range(2):
                r0, r1, r2 = (
                    part[g * 32 + z * 8 + hi * 4 : g * 32 + z * 8 + hi * 4 + 4] for g in range(3)
                )
                block = jnp.concatenate(
                    [
                        jnp.concatenate([r0, r2[:, : 5 * HALF]], axis=1),
                        jnp.concatenate([r1, r2[:, 5 * HALF :], vec], axis=1),
                    ],
                    axis=0,
                )
                out[((hi ^ hi0) * 2 + (m ^ m0)) * 4 + (z ^ z0)] = block.astype(BF)


def exchanged(blocks, axes):
    return lax.all_to_all(blocks, axes, 0, 0, tiled=True)


def total_of(blocks):
    total = blocks[0].astype(F32)
    for i in range(1, blocks.shape[0]):
        total = total + blocks[i].astype(F32)
    return total


def final_kernel(n0, n1, n2, n3, blocks, wq, wk, wv, wo, wi, wt, qb, vb, ib, ob, g1, s1, fb, g2, s2):
    total = add(n0[...], n1[...], n2[...], n3[...])
    wo[...] = total[:12, :HALF]
    wi[:, :FQ] = total[:12, HALF:]
    vec = jnp.concatenate([total[12 + i : 13 + i, :CQ] for i in range(6)], axis=1)
    at = 0
    for dst in (ib, ob, g1, s1, fb, g2, s2):
        dst[...] = vec[0, at : at + dst.shape[0]]
        at += dst.shape[0]
    total = total_of(blocks)
    n = CH + CQ
    tail = jnp.concatenate([total[:4, n:], total[4:, n : n + 4 * HALF]], axis=1)
    at = 0
    for dst, first, width in (
        (wt, 0, FHALF), (wi, FQ, FQ), (wq, 0, HALF), (wk, 0, HALF), (wv, 0, HALF)
    ):
        dst[:8, first : first + width] = total[:, at : at + width]
        dst[8:, first : first + width] = tail[:, at : at + width]
        at += width
    qb[...] = total[4, n + 4 * HALF :]
    vb[...] = total[5, n + 4 * HALF :]


def decoded(index):
    return (index >> 6, (index >> 4) & 3, (index >> 2) & 3, (index >> 1) & 1), index & 1


def row_of(vector):
    return vector[...].reshape(1, -1)


def order_matrix(place, swap):
    r = lax.broadcasted_iota(jnp.int32, (1, D), 1)
    j = r & 3
    hi = ((r >> 2) & 1) ^ place[0]
    near, far = (r >> 3) & 3, (r >> 5) & 3
    y = (far if swap else near) ^ place[2]
    z = (near if swap else far) ^ place[1]
    block = r >> 7
    core = jnp.where(block >= 3, 1, 0)
    group = block - 3 * core
    core = core ^ place[3]
    source = (((hi * 4 + z) * 4 + y) * 2 + core) * 12 + group * 4 + j
    rows = lax.broadcasted_iota(jnp.int32, (D, D), 0)
    return jnp.where(rows == source, 1.0, 0.0)


def swap_matrix():
    r = lax.broadcasted_iota(jnp.int32, (1, D), 1)
    source = (r & ~0x78) | ((r & 0x18) << 2) | ((r & 0x60) >> 2)
    rows = lax.broadcasted_iota(jnp.int32, (D, D), 0)
    return jnp.where(rows == source, 1.0, 0.0)


def exact(a, b, dims):
    return lax.dot_general(
        a, b, (dims, ((), ())), preferred_element_type=F32, precision=lax.Precision.HIGHEST
    )


def pack_kernel(wq, wk, wv, wo, wi, wt, out):
    at = 0
    for src, first, n in (
        (wq, 0, HALF),
        (wk, 0, HALF),
        (wv, 0, HALF),
        (wo, 0, HALF),
        (wi, 0, FQ),
        (wt, 0, FHALF),
        (wi, FQ, FQ),
    ):
        for g in range(3):
            out[g, :, at : at + n] = src[g * 4 : (g + 1) * 4, first : first + n]
        at += n


def decoded(index):
    return (index >> 6, (index >> 4) & 3, (index >> 2) & 3, (index >> 1) & 1), index & 1


def row_of(vector):
    return vector[...].reshape(1, -1)


def order_matrix(place, swap):
    r = lax.broadcasted_iota(jnp.int32, (1, D), 1)
    j = r & 3
    hi = ((r >> 2) & 1) ^ place[0]
    near, far = (r >> 3) & 3, (r >> 5) & 3
    y = (far if swap else near) ^ place[2]
    z = (near if swap else far) ^ place[1]
    block = r >> 7
    core = jnp.where(block >= 3, 1, 0)
    group = block - 3 * core
    core = core ^ place[3]
    source = (((hi * 4 + z) * 4 + y) * 2 + core) * 12 + group * 4 + j
    rows = lax.broadcasted_iota(jnp.int32, (D, D), 0)
    return jnp.where(rows == source, 1.0, 0.0)


def swap_matrix():
    r = lax.broadcasted_iota(jnp.int32, (1, D), 1)
    source = (r & ~0x78) | ((r & 0x18) << 2) | ((r & 0x60) >> 2)
    rows = lax.broadcasted_iota(jnp.int32, (D, D), 0)
    return jnp.where(rows == source, 1.0, 0.0)


def exact(a, b, dims):
    return lax.dot_general(
        a, b, (dims, ((), ())), preferred_element_type=F32, precision=lax.Precision.HIGHEST
    )


def order_kernel(
    index, x_all, y_all, ob, g1, s1, fb, g2, s2,
    order_a, order_b, swap, xr, xb, yr, vr, x, y, sems,
):
    place, mp = decoded(index[0])
    rows = pl.ds(pl.multiple_of(mp * T, T), T)
    copies = [
        pltpu.make_async_copy(src.at[rows, :], dst, sems.at[i])
        for i, (src, dst) in enumerate(((x_all, x), (y_all, y)))
    ]
    for c in copies:
        c.start()
    m = order_matrix(place, False)
    order_a[...] = m.astype(BF)
    blank = jnp.zeros((5, D), F32)
    vr[0:8, :] = exact(
        jnp.concatenate([row_of(ob), row_of(g1), row_of(s1), blank], axis=0), m, ((1,), (0,))
    )
    m = order_matrix(place, True)
    order_b[...] = m.astype(BF)
    vr[8:16, :] = exact(
        jnp.concatenate([row_of(fb), row_of(g2), row_of(s2), blank], axis=0), m, ((1,), (0,))
    )
    swap[...] = swap_matrix().astype(BF)
    for c in copies:
        c.wait()
    xr[...] = nn(x[...], order_a[...]).astype(BF)
    xb[...] = nn(x[...], order_b[...]).astype(BF)
    yr[...] = nn(y[...], order_b[...]).astype(BF)


def start_weight(pieces, first, width, dst, at, m, sem):
    for core in range(2):
        for i, z in enumerate((0, 1, 3, 2)):
            src = pieces[core * 5 + i + (m if z == 2 else 0)]
            col = first + (0 if z == 2 else m * CH)
            pltpu.make_async_copy(
                src.at[:, :, pl.ds(col, width)],
                dst.at[pl.ds(core * 3, 3), pl.ds(z * 32, 32), pl.ds(at, width)],
                sem,
            ).start()


def wait_weight(dst, at, width, sem):
    part = dst.at[:, :, pl.ds(at, width)]
    pltpu.make_async_copy(part, part, sem).wait()


def weight(w, at, width):
    return w[:, :, pl.ds(at, width)].reshape(D, width)


def row_starts(info, shape, axis):
    index, buckets, lengths = info
    mp = index[0] & 1
    shift = 7 + buckets[0, mp]
    pos = lax.broadcasted_iota(jnp.int32, shape, axis)
    seq = lax.shift_right_logical(pos, shift)
    within = pos & (lax.shift_left(1, shift) - 1)
    n0, n1, n2, n3 = (lengths[0, mp, i] for i in range(4))
    live = jnp.where(seq == 0, n0, jnp.where(seq == 1, n1, jnp.where(seq == 2, n2, n3)))
    return seq, within < live


def mask_bias(info, key_axis):
    kshape = (T, 1) if key_axis == 0 else (1, T)
    qshape = (1, T) if key_axis == 0 else (T, 1)
    kseq, live = row_starts(info, kshape, key_axis)
    qseq, _ = row_starts(info, qshape, 1 - key_axis)
    kseq = jnp.where(live, kseq, -1)
    return jnp.where(kseq == qseq, 0.0, -1e30)


def attention_kernel(
    index, buckets, lengths, xr, qb, vb, others, p0, p1, p2, p3, p4, p5, p6, p7, p8, p9,
    q, k, v, ctx, lse, w_out, w, qkv, biases, mask, lcol, sem, sem2,
):
    pieces = (p0, p1, p2, p3, p4, p5, p6, p7, p8, p9)
    for m in range(2):
        start_weight(pieces, 0, 3 * HALF, w, m * 3 * HALF, m, sem)
    mask[...] = mask_bias((index, buckets, lengths), 1)
    wait_weight(w, 0, 6 * HALF, sem)
    keep = pltpu.make_async_copy(w, w_out, sem2)
    keep.start()
    zero = jnp.zeros((1, HALF), F32)
    for m in range(2):
        for i, own in enumerate((qb, None, vb)):
            if i == 1:
                b = zero
            elif m == 0:
                b = row_of(own)
            else:
                b = others[pl.ds((i >> 1) * HALF, HALF)].reshape(1, HALF)
            biases[m * 3 + i : m * 3 + i + 1, :] = b

    def project(i, _):
        a = nn(xr[...], weight(w, pl.multiple_of(i * HALF, HALF), HALF)) + biases[pl.ds(i, 1), :]
        scale = jnp.where((i == 0) | (i == 3), 0.125, 1.0)
        qkv[i] = (a.astype(BF).astype(F32) * scale).astype(BF)
        return 0

    lax.fori_loop(0, 6, project, 0)
    for i in range(6):
        (q, k, v)[i % 3][:, (i // 3) * HALF : (i // 3 + 1) * HALF] = qkv[i]
    lcol[...] = jnp.zeros_like(lcol)
    lane = lax.broadcasted_iota(jnp.int32, (1, 128), 1)

    def pair(i, _):
        cols = pl.ds(pl.multiple_of(i * 128, 128), 128)
        q2, k2, v2 = q[:, cols], k[:, cols], v[:, cols]
        total = None
        for half in range(2):
            mine = (lane < 64) if half == 0 else (lane >= 64)
            s = nt(jnp.where(mine, q2, BF(0)), k2) + mask[...]
            peak = jnp.max(s, axis=1, keepdims=True)
            e = jnp.exp(s - peak)
            z = jnp.sum(e, axis=1, keepdims=True)
            p = (e / z).astype(BF)
            c = nn(p, jnp.where(mine, v2, BF(0)))
            total = c if total is None else total + c
            l = peak + jnp.log(z)
            lcol[...] = jnp.where(lane == i * 2 + half, l, lcol[...])
        ctx[:, cols] = total.astype(BF)
        return 0

    lax.fori_loop(0, 6, pair, 0)
    lse[...] = lcol[...].T[0:16, :]
    keep.wait()


def stats(a):
    mean = jnp.mean(a, axis=1, keepdims=True)
    a = a - mean
    r = lax.rsqrt(jnp.mean(a * a, axis=1, keepdims=True) + EPS)
    return a * r, r


def norm_back(dy, n, r, gain):
    a = dy * gain
    return r * (
        a - jnp.mean(a, axis=1, keepdims=True) - n * jnp.mean(a * n, axis=1, keepdims=True)
    )


def store_rows(own, other, value, cols):
    for core, dst in enumerate((own, other)):
        for g in range(3):
            for z in range(4):
                at = ((core * 3 + g) * 4 + z) * 32
                dst[z, g * 32 : (g + 1) * 32, cols] = value[at : at + 32]


def store_vectors(own, other, value):
    for dst in (own, other):
        for z in range(4):
            dst[z, 96:104, :] = value


def unit_source(f):
    return f < 2, (4 * HALF if f < 2 else 2 * FQ), f & 1


def up_kernel(
    ctx, xr, yr, vr, inb, others, order_b, swap,
    a0, a1, a2, a3, a4, a5, a6, a7, a8, a9, b0, b1, b2, b3, b4, b5, b6, b7, b8, b9,
    out, h1t_out, n1_out, r1, df, da, dinb, sums, slope_out, grads_out, grads1_out,
    wo, wi, wt, hs, hts, biases, n1, gact, slope, big, lowt, grads, grads1, sems, keeps, goes,
):
    ap = (a0, a1, a2, a3, a4, a5, a6, a7, a8, a9)
    bp = (b0, b1, b2, b3, b4, b5, b6, b7, b8, b9)
    for m in range(2):
        start_weight(ap, 3 * HALF, HALF, wo, m * HALF, m, sems.at[0])
    for f in range(4):
        first, col, m = unit_source(f)
        start_weight(ap if first else bp, col, FQ, wi, f * FQ, m, sems.at[1 + f])
        start_weight(bp, (f >> 1) * FQ, FQ, wt, f * FQ, m, sems.at[5 + f])
    wait_weight(wo, 0, D, sems.at[0])
    ob, g1, s1 = (vr[i : i + 1, :] for i in range(3))
    fb, g2, s2 = (vr[i : i + 1, :] for i in range(8, 11))
    nrm, r = stats(nt(ctx[...], weight(wo, 0, D)) + ob + xr[...].astype(F32))
    n1[...] = nrm
    keep = []

    def send(src, dst, sem):
        keep.append(pltpu.make_async_copy(src, dst, sem))
        keep[-1].start()

    send(n1, n1_out, keeps.at[2])
    r1[...] = jnp.broadcast_to(r, (T, 128))
    low = nrm * g1 + s1
    hs[0] = low.astype(BF)
    hts[0] = low.T.astype(BF)
    send(hts.at[0], h1t_out, keeps.at[3])
    low = nn(hs[0], swap[...])
    hs[1] = low.astype(BF)
    hts[1] = low.T.astype(BF)
    big[...] = hs[1].astype(F32) + fb
    for f in range(4):
        bias, at = (inb, 0) if f & 1 == 0 else (others, D)
        biases[f : f + 1, :] = bias[pl.ds(at + (f >> 1) * FQ, FQ)].reshape(1, FQ)

    def up(f, _):
        at = pl.multiple_of(f * FQ, FQ)
        wait_weight(wi, at, FQ, sems.at[1 + f])
        u = nn(hs[f >> 1], weight(wi, at, FQ)) + biases[pl.ds(f, 1), :]
        phi = 0.5 + 0.5 * lax.erf(u * INV_SQRT2)
        slope[f] = phi + u * (jnp.exp(-0.5 * u * u) * INV_SQRT2PI)

        @pl.when(f < 2)
        def _():
            pltpu.make_async_copy(slope.at[f], slope_out.at[f], keeps.at[f]).start()

        g = (u * phi).astype(BF)
        gact[:, pl.ds(at, FQ)] = g
        wait_weight(wt, at, FQ, sems.at[5 + f])
        big[...] += nt(g, weight(wt, at, FQ))
        return 0

    lax.fori_loop(0, 4, up, 0)
    keep += [pltpu.make_async_copy(slope.at[f], slope_out.at[f], keeps.at[f]) for f in range(2)]
    n2, r2 = stats(big[...])
    low = (n2 * g2 + s2).astype(BF)
    out[...] = nt(low, order_b[...]).astype(BF)
    y = yr[...].astype(F32)
    sums[1:2, :] = jnp.sum(y * n2, axis=0, keepdims=True)
    sums[2:3, :] = jnp.sum(y, axis=0, keepdims=True)
    d = norm_back(y, n2, r2, g2)
    big[...] = d
    low = d.astype(BF)
    df[...] = low
    sums[0:1, :] = jnp.sum(low.astype(F32), axis=0, keepdims=True)
    sums[3:8, :] = jnp.zeros((5, D), F32)
    lowt[...] = d.T.astype(BF)

    def go(first, width, sem):
        for k, (src, dst) in enumerate(((grads, grads_out), (grads1, grads1_out))):
            cols = pl.ds(first, width)
            yield pltpu.make_async_copy(src.at[:, :, cols], dst.at[:, :, cols], sem(k))

    def outer(f, _):
        g = nn(lowt[...], gact[:, pl.ds(pl.multiple_of(f * FQ, FQ), FQ)]).astype(BF)
        at = pl.multiple_of((f & 1) * CH + (f >> 1) * FQ, FQ)
        store_rows(grads, grads1, g, pl.ds(at, FQ))

        @pl.when(f >= 2)
        def _():
            for c in go(pl.multiple_of((f & 1) * CH, CH), FHALF, lambda k: goes.at[k, f & 1]):
                c.start()

        return 0

    lax.fori_loop(0, 4, outer, 0)

    def inner(m, _):
        f = m + 2
        at = pl.multiple_of(f * FQ, FQ)
        du = (nn(df[...], weight(wt, at, FQ)) * slope[f]).astype(BF)
        dinb[:, pl.ds(pl.multiple_of(m * FQ, FQ), FQ)] = jnp.sum(
            du.astype(F32), axis=0, keepdims=True
        )
        big[...] += nt(du, weight(wi, at, FQ))
        g = nn(hts[1], du).astype(BF)
        to = pl.multiple_of(m * CH + FHALF, FQ)
        store_rows(grads, grads1, g, pl.ds(to, FQ))
        for c in go(to, FQ, lambda k: goes.at[2 + k, m]):
            c.start()
        return 0

    lax.fori_loop(0, 2, inner, 0)
    for m in range(2):
        keep += list(go(m * CH, FHALF, lambda k, m=m: goes.at[k, m]))
        keep += list(go(m * CH + FHALF, FQ, lambda k, m=m: goes.at[2 + k, m]))
    d = big[...]
    hi = d.astype(BF)
    lo = (d - hi.astype(F32)).astype(BF)
    da[...] = nt(hi, swap[...]) + nt(lo, swap[...])
    for k in keep:
        k.wait()


def down_units(df, wi, wt, slope, big, h1t, dinb, grads, grads1, sems, keeps, slope_in):
    def down(f, _):
        at = pl.multiple_of(f * FQ, FQ)
        wait_weight(wt, at, FQ, sems.at[2 * f])
        pltpu.make_async_copy(slope_in.at[f], slope.at[f], keeps.at[f]).wait()
        du = (nn(df[...], weight(wt, at, FQ)) * slope[f]).astype(BF)
        dinb[pl.ds(f, 1), :] = jnp.sum(du.astype(F32), axis=0, keepdims=True)
        wait_weight(wi, at, FQ, sems.at[2 * f + 1])
        big[...] += nt(du, weight(wi, at, FQ))
        g = nn(h1t[...], du).astype(BF)
        store_rows(grads, grads1, g, pl.ds(pl.multiple_of(f * CQ + HALF, HALF), FQ))
        return 0

    lax.fori_loop(0, 2, down, 0)


def start_units(units, ap, bp, wi, wt, slope_in, slope, sems, keeps):
    for i, f in enumerate(units):
        first, col, m = unit_source(f)
        start_weight(bp, (f >> 1) * FQ, FQ, wt, i * FQ, m, sems.at[2 * i])
        pltpu.make_async_copy(slope_in.at[f], slope.at[i], keeps.at[i]).start()
        start_weight(ap if first else bp, col, FQ, wi, i * FQ, m, sems.at[2 * i + 1])


def down_kernel1(
    h1t, r1, df, dinb, sums, vr, ctx_all, n1_all, da_in, order_a_all, order_b_all, slope_in,
    a0, a1, a2, a3, a4, a5, a6, a7, a8, a9, b0, b1, b2, b3, b4, b5, b6, b7, b8, b9,
    dc, dr, grads, grads1,
    wo, wi, wt, slope, big, lowt, inner, ctx, n1, order_a, order_b, sems, keeps, loads,
):
    ap = (a0, a1, a2, a3, a4, a5, a6, a7, a8, a9)
    bp = (b0, b1, b2, b3, b4, b5, b6, b7, b8, b9)
    start_units((0, 1), ap, bp, wi, wt, slope_in, slope, sems, keeps)
    for m in range(2):
        start_weight(ap, 3 * HALF, HALF, wo, m * HALF, m, sems.at[4])
    copies = [
        pltpu.make_async_copy(src, dst, loads.at[i])
        for i, (src, dst) in enumerate(
            (
                (da_in, big),
                (n1_all, n1),
                (ctx_all, ctx),
                (order_a_all, order_a),
                (order_b_all, order_b),
            )
        )
    ]
    for c in copies:
        c.start()
    copies[0].wait()
    down_units(df, wi, wt, slope, big, h1t, inner, grads, grads1, sems, keeps, slope_in)
    for c in copies[1:]:
        c.wait()
    dh = big[...]
    nrm = n1[...]
    g1 = vr[1:2, :]
    dg1 = jnp.sum(dh * nrm, axis=0, keepdims=True)
    ds1 = jnp.sum(dh, axis=0, keepdims=True)
    d = norm_back(dh, nrm, r1[:, 0:1], g1)
    dr[...] = d
    da = d.astype(BF)
    dob = jnp.sum(da.astype(F32), axis=0, keepdims=True)
    wait_weight(wo, 0, D, sems.at[4])
    dc[...] = nn(da, weight(wo, 0, D)).astype(BF)
    lowt[...] = d.T.astype(BF)
    g = nn(lowt[...], ctx[...]).astype(BF)
    for m in range(2):
        store_rows(grads, grads1, g[:, m * HALF : (m + 1) * HALF], pl.ds(m * CQ, HALF))
    sa = exact(
        jnp.concatenate([dob, dg1, ds1, dob, dob, dob, dob, dob], axis=0),
        order_a[...].astype(F32),
        ((1,), (1,)),
    )
    sb = exact(sums[...], order_b[...].astype(F32), ((1,), (1,)))
    sides = []
    for m in range(2):
        line = jnp.concatenate(
            [inner[m : m + 1, :], dinb[:, m * FQ : (m + 1) * FQ]]
            + [sa[i : i + 1] for i in range(3)]
            + [sb[i : i + 1] for i in range(3)]
            + [jnp.zeros((1, 6 * CQ - 8 * FQ), F32)],
            axis=1,
        )
        rows = [line[:, i * CQ : (i + 1) * CQ] for i in range(6)]
        sides.append(jnp.concatenate(rows + [jnp.zeros((2, CQ), F32)], axis=0))
    store_vectors(grads, grads1, jnp.concatenate(sides, axis=1).astype(BF))


def back_half(
    m, index, buckets, lengths, q, k, v, dc, lse, xb_all, w_all, dr,
    grads, grads1, mask, dqkv, big, qb, vb, xt_ref, w, xb, sems,
):
    copies = [
        pltpu.make_async_copy(w_all.at[:, :, pl.ds(m * 3 * HALF, 3 * HALF)], w, sems.at[0]),
        pltpu.make_async_copy(xb_all, xb, sems.at[1]),
        pltpu.make_async_copy(dr, big, sems.at[2]),
    ]
    for c in copies:
        c.start()
    mask[...] = mask_bias((index, buckets, lengths), 0)
    lane = lax.broadcasted_iota(jnp.int32, (1, 128), 1)

    def pair(i, _):
        head = pl.ds(pl.multiple_of(m * HALF + i * 128, 128), 128)
        cols = pl.ds(pl.multiple_of(i * 128, 128), 128)
        q2, k2, v2, c2 = q[:, head], k[:, head], v[:, head], dc[:, head]
        outs = []
        for half in range(2):
            mine = (lane < 64) if half == 0 else (lane >= 64)
            s = nt(jnp.where(mine, k2, BF(0)), q2) + mask[...]
            p = jnp.exp(s - lse[pl.ds(m * 6 + i * 2 + half, 1), :])
            dp = nt(jnp.where(mine, v2, BF(0)), c2)
            delta = jnp.sum(dp * p, axis=0, keepdims=True)
            ds = (p * (dp - delta)).astype(BF)
            outs.append((tn(ds, k2), nn(ds, q2), nn(p.astype(BF), c2)))
        first = lane < 64
        dq2, dk2, dv2 = (jnp.where(first, a, b) for a, b in zip(*outs))
        dq2 = (dq2 * 0.125).astype(BF)
        dk2 = dk2.astype(BF)
        dv2 = dv2.astype(BF)
        dqkv[0, :, cols] = dq2
        dqkv[1, :, cols] = dk2
        dqkv[2, :, cols] = dv2
        qb[:, cols] = jnp.sum(dq2.astype(F32), axis=0, keepdims=True)
        vb[:, cols] = jnp.sum(dv2.astype(F32), axis=0, keepdims=True)
        return 0

    lax.fori_loop(0, 3, pair, 0)
    for c in copies:
        c.wait()
    xt_ref[...] = xb[...].astype(F32).T.astype(BF)

    def weights(i, _):
        to = pl.multiple_of(i * HALF, HALF)
        a = dqkv[i]
        store_rows(grads, grads1, nn(xt_ref[...], a).astype(BF), pl.ds(to, HALF))
        big[...] += nt(a, weight(w, to, HALF))
        return 0

    lax.fori_loop(0, 3, weights, 0)
    line = jnp.concatenate([qb[...], vb[...], jnp.zeros((1, HALF), F32)], axis=1)
    line = jnp.concatenate([line, jnp.zeros((7, CQ), F32)], axis=0)
    store_vectors(grads, grads1, line.astype(BF))


def back_kernel0(
    index, buckets, lengths, q, k, v, dc, lse, xb, w, dr,
    grads, grads1, out, mask, dqkv, *scratch,
):
    ins = (index, buckets, lengths, q, k, v, dc, lse, xb, w, dr)
    big = scratch[0]
    back_half(0, *ins, grads, grads1, mask, dqkv, *scratch)
    out[...] = big[...]


def back_kernel1(
    index, buckets, lengths, q, k, v, dc, lse, xb, w, dr,
    grads, grads1, gin, mask, dqkv, *scratch,
):
    ins = (index, buckets, lengths, q, k, v, dc, lse, xb, w, dr)
    big = scratch[0]
    back_half(1, *ins, grads, grads1, mask, dqkv, *scratch)
    gin[...] = big[...].astype(BF)


def last_kernel(gin, order, out):
    out[...] = nt(gin[...], order[...]).astype(BF)


def call(kernel, outs, args, scratch=(), vmem=48, flops=0, smem=0, hbm=(), anyouts=()):
    specs = []
    for i in range(len(args)):
        if i < smem:
            specs.append(pl.BlockSpec(memory_space=pltpu.SMEM))
        elif i in hbm:
            specs.append(pl.BlockSpec(memory_space=pl.ANY))
        else:
            specs.append(pl.BlockSpec(memory_space=VMEM))
    return pl.pallas_call(
        kernel,
        out_shape=[jax.ShapeDtypeStruct(s, d) for s, d in outs],
        in_specs=specs,
        out_specs=[
            pl.BlockSpec(memory_space=pl.ANY if i in anyouts else VMEM) for i in range(len(outs))
        ],
        scratch_shapes=list(scratch),
        compiler_params=pltpu.CompilerParams(vmem_limit_bytes=vmem * 2**20),
        cost_estimate=pl.CostEstimate(flops=flops // 1000, bytes_accessed=1000, transcendentals=0),
    )(*args)


def body(
    hidden_in, buckets, lengths, query_weight, key_weight, value_weight, query_bias, value_bias,
    output_weight, output_bias, first_gain, first_shift, inner_weight, inner_bias, outer_weight,
    outer_bias, second_gain, second_shift, cotangent,
):
    mp = lax.axis_index("mp")
    index = lax.axis_index((*DP, "mp")).astype(jnp.int32).reshape(1)
    info = (index, buckets, lengths)
    (shard,) = call(
        pack_kernel,
        [((3, 4, 2 * CH), BF)],
        (query_weight, key_weight, value_weight, output_weight.T, inner_weight, outer_weight.T),
        vmem=60,
    )
    biases = jnp.concatenate([query_bias, value_bias, inner_bias])
    others = flip(biases, "mp", 1)
    def sides(mine, other):
        return jnp.where(
            mp == 0, jnp.concatenate([mine, other], axis=0), jnp.concatenate([other, mine], axis=0)
        )

    square = ((D, D), BF)
    tokens = ((T, D), BF)
    order_a, order_b, swap, xr, xb, yr, vr = call(
        order_kernel,
        [square, square, square, tokens, tokens, tokens, ((16, D), F32)],
        (
            index,
            hidden_in,
            cotangent,
            output_bias,
            first_gain,
            first_shift,
            outer_bias,
            second_gain,
            second_shift,
        ),
        [VMEM((T, D), BF), VMEM((T, D), BF), pltpu.SemaphoreType.DMA((2,))],
        smem=1,
        hbm=(1, 2),
        vmem=60,
        flops=2 * 10**9,
    )
    pa, pb, (xr, xb, yr, others) = gather(shard, (xr, xb, yr, others))
    q, k, v, ctx, lse, w = call(
        attention_kernel,
        [tokens, tokens, tokens, tokens, ((16, T), F32), ((6, 128, 6 * HALF), BF)],
        (*info, xr, query_bias, value_bias, others, *pa),
        [
            VMEM((6, 128, 6 * HALF), BF),
            VMEM((6, T, HALF), BF),
            VMEM((8, HALF), F32),
            VMEM((T, T), F32),
            VMEM((T, 128), F32),
            pltpu.SemaphoreType.DMA(()),
            pltpu.SemaphoreType.DMA(()),
        ],
        smem=3,
        hbm=range(7, 17),
        anyouts=(5,),
        vmem=60,
        flops=10 * 10**9,
    )
    gb, ga = ((4, 96, 2 * CH), BF), ((4, 104, 2 * CQ), BF)
    wide = ((T, D), F32)
    out, h1t, n1, r1, df, da, dinb, sums, slope, grads_b, grads_b1 = call(
        up_kernel,
        [
            tokens,
            ((D, T), BF),
            wide,
            ((T, 128), F32),
            tokens,
            wide,
            ((1, 2 * FQ), F32),
            ((8, D), F32),
            ((2, T, FQ), F32),
            gb,
            gb,
        ],
        (ctx, xr, yr, vr, inner_bias, others, order_b, swap, *pa, *pb),
        [
            VMEM((6, 128, D), BF),
            VMEM((6, 128, FF), BF),
            VMEM((6, 128, FF), BF),
            VMEM((2, T, D), BF),
            VMEM((2, D, T), BF),
            VMEM((8, FQ), F32),
            VMEM((T, D), F32),
            VMEM((T, FF), BF),
            VMEM((4, T, FQ), F32),
            VMEM((T, D), F32),
            VMEM((D, T), BF),
            VMEM(*gb),
            VMEM(*gb),
            pltpu.SemaphoreType.DMA((9,)),
            pltpu.SemaphoreType.DMA((4,)),
            pltpu.SemaphoreType.DMA((4, 2)),
        ],
        hbm=range(8, 28),
        anyouts=(1, 2, 8, 9, 10),
        vmem=56,
        flops=8 * 10**9,
    )
    grads_b1 = flip(grads_b1, AC, 1)
    out_own, out = out, flip(out, "mp", 1)
    half = [VMEM((6, 128, 2 * FQ), BF)] * 2 + [VMEM((2, T, FQ), F32), VMEM((T, D), F32)]
    dc, dr, grads_a, grads_a1 = call(
        down_kernel1,
        [tokens, wide, ga, ga],
        (h1t, r1, df, dinb, sums, vr, ctx, n1, da, order_a, order_b, slope, *pa, *pb),
        [VMEM((6, 128, D), BF)]
        + half
        + [
            VMEM((D, T), BF),
            VMEM((8, FQ), F32),
            VMEM((T, D), BF),
            VMEM((T, D), F32),
            VMEM((D, D), BF),
            VMEM((D, D), BF),
            pltpu.SemaphoreType.DMA((5,)),
            pltpu.SemaphoreType.DMA((2,)),
            pltpu.SemaphoreType.DMA((5,)),
        ],
        hbm=range(6, 32),
        vmem=60,
        flops=4 * 10**9,
    )
    b0, b1, b3, bl, br = core_sums([(grads_b, grads_b1)], 96)
    grads_a1 = flip(grads_a1, AC, 1)
    a0, a1, a3, al, ar = core_sums([(grads_a, grads_a1)], 104)
    dc, b0, b1, b3, bl, br, a0, a1, a3, al, ar = lax.optimization_barrier(
        (dc, b0, b1, b3, bl, br, a0, a1, a3, al, ar)
    )
    bl, br = flip(bl, AY, 1), flip(br, AY, 3)
    al, ar = flip(al, AZ, 1), flip(ar, AZ, 3)
    gq = ((4, 104, CQ), BF)
    scratch = [
        VMEM((T, T), F32),
        VMEM((3, T, HALF), BF),
        VMEM((T, D), F32),
        VMEM((1, HALF), F32),
        VMEM((1, HALF), F32),
        VMEM((D, T), BF),
        VMEM((6, 128, 3 * HALF), BF),
        VMEM((T, D), BF),
        pltpu.SemaphoreType.DMA((3,)),
    ]
    q00, q01, big = call(
        back_kernel0,
        [gq, gq, wide],
        (*info, q, k, v, dc, lse, xb, w, dr),
        scratch,
        smem=3,
        hbm=(8, 9, 10),
        vmem=60,
        flops=7 * 10**9,
    )
    b1, b3 = relayed((2 * CH,), b1, b3, bl, br)
    a1, a3 = relayed((2 * CQ,), a1, a3, al, ar)
    big, b1, b3, a1, a3, out = lax.optimization_barrier((big, b1, b3, a1, a3, out))
    b1, b3 = flip(b1, AY, 1), flip(b3, AY, 3)
    a1, a3 = flip(a1, AZ, 1), flip(a3, AZ, 3)
    q10, q11, gin = call(
        back_kernel1,
        [gq, gq, tokens],
        (*info, q, k, v, dc, lse, xb, w, big),
        scratch,
        smem=3,
        hbm=(8, 9, 10),
        vmem=60,
        flops=7 * 10**9,
    )
    q01, q11, b1, b3, a1, a3 = lax.optimization_barrier((q01, q11, b1, b3, a1, a3))
    q01, q11 = flip(q01, AC, 1), flip(q11, AC, 1)
    rq = call(pair_kernel, [((104, 2 * CQ), BF)] * 4, (q00, q01, q10, q11), vmem=24)
    rq = sent(rq, AY)
    (gin,) = call(last_kernel, [tokens], (gin, order_a), vmem=16)
    theirs = flip(gin, "mp", 1)
    rq, theirs = lax.optimization_barrier((rq, theirs))
    fa = sent(call(second_kernel, [((32, 2 * CQ), BF)] * 4, (a0, a1, a3), vmem=24), AY)
    fa = sent(call(third_kernel, [((20, CQ), BF)] * 4, fa, vmem=24), AX)
    (blocks,) = call(
        last_sums_kernel,
        [((16, 8, 14 * HALF), BF)],
        (index, b0, b1, b3, *rq),
        smem=1,
        vmem=32,
    )
    blocks = exchanged(blocks, (*AX, AZ))
    small, inner, vector = ((12, HALF), F32), ((12, FHALF), F32), ((D,), F32)
    half = ((HALF,), F32)
    wq, wk, wv, wo, wi, wt, qb, vb, ib, *vecs = call(
        final_kernel,
        [small] * 4 + [inner] * 2 + [half] * 2 + [((FHALF,), F32)] + [vector] * 6,
        (*fa, blocks),
        vmem=24,
    )
    layer_out = sides(out_own, out)
    input_grad = sides(gin, theirs).astype(F32)
    dob, dg1, ds1, dfb, dg2, ds2 = vecs
    return (
        layer_out, input_grad, wq, wk, wv, qb, vb, wo.T, dob, dg1, ds1, wi, ib, wt.T, dfb, dg2, ds2
    )


def solution(mesh):
    torus = Mesh(
        mesh.devices.reshape(2, 4, 4, 2, mesh.shape["mp"]), ("dp_0", "dp_1", "dp_2", "dp_3", "mp")
    )
    row, col, half = P(DP, "mp"), P("mp", DP), P("mp")
    in_specs = (
        P(DP, None), P(DP, None), P(DP, None, None), row, row, row, half, half, col, P(), P(), P(),
        row, half, col, P(), P(), P(), P(DP, None),
    )
    out_specs = (
        P(DP, None), P(DP, None), row, row, row, half, half, col, P(), P(), P(), row, half, col,
        P(), P(), P(),
    )
    return jax.shard_map(body, mesh=torus, in_specs=in_specs, out_specs=out_specs, check_vma=False)
```

```python
import functools

import jax
import jax.numpy as jnp
from jax import lax
from jax.experimental import pallas as pl
from jax.experimental.pallas import tpu as pltpu
from jax.sharding import Mesh
from jax.sharding import PartitionSpec as P

DP = ("dp_0", "dp_1", "dp_2", "dp_3")
AX = ("dp_0", "mp")
AZ, AY, AC = "dp_1", "dp_2", "dp_3"
D = 768
T = 512
DH = 64
FF = 3072
HALF = 384
FHALF = 1536
FQ = 768
CH = 2304
CQ = 1152
CA = 1920
EPS = 1e-12
BF = jnp.bfloat16
F32 = jnp.float32
VMEM = pltpu.VMEM
INV_SQRT2 = 0.7071067811865476
INV_SQRT2PI = 0.3989422804014327


def nn(a, b):
    return lax.dot_general(a, b, (((1,), (0,)), ((), ())), preferred_element_type=F32)


def nt(a, b):
    return lax.dot_general(a, b, (((1,), (1,)), ((), ())), preferred_element_type=F32)


def tn(a, b):
    return lax.dot_general(a, b, (((0,), (0,)), ((), ())), preferred_element_type=F32)


def flip(a, axis, s):
    n = 4 if axis in (AX, AY, AZ) else 2
    return lax.ppermute(a, axis, [(i, i ^ s) for i in range(n)])


def joined(a, axis):
    return jnp.concatenate([a] + [flip(a, axis, s) for s in (1, 2, 3)], axis=1)


def gather(shard, ready):
    a = shard
    p1, p2, p3 = (flip(a, AX, s) for s in (1, 2, 3))
    parts = []
    for first in (0, CH):
        cols = slice(first, first + CH)
        a0, a1, a2, a3 = (p[:, :, cols] for p in (a, p1, p2, p3))
        parts.append(
            jnp.concatenate(
                [jnp.concatenate([a0, a2], axis=1), jnp.concatenate([a1, a3], axis=1)], axis=2
            )
        )
    parts = lax.optimization_barrier((joined(parts[0], AY), joined(parts[1], AZ)))
    near = [[flip(b, axis, s) for s in (1, 3)] for b, axis in zip(parts, (AZ, AY))]
    near, ready = lax.optimization_barrier((near, ready))
    out = []
    for b, axis, (n1, n3) in zip(parts, (AZ, AY), near):
        far = [flip(n1[:, :, :CH], axis, 3), flip(n3[:, :, CH:], axis, 1)]
        out.append([b, n1, n3, *far])
    return *out, ready


def with_other_core(own):
    return own + [flip(o, AC, 1) for o in own]


def add(*parts):
    total = parts[0].astype(F32)
    for p in parts[1:]:
        total = total + p.astype(F32)
    return total


def low_sum(*parts):
    return add(*parts).astype(BF)


def core_kernel(*refs):
    c0, c1, c3, left, right = refs[-5:]
    pairs = [refs[i : i + 2] for i in range(0, len(refs) - 5, 2)]
    at = 0
    for own, other in pairs:
        rows, n = own.shape[1:]
        for s, dst in ((0, c0), (1, c1), (3, c3), (2, None)):
            total = low_sum(own[s], other[s])
            if s == 2:
                left[:rows, at // 2 : (at + n) // 2] = total[:, : n // 2]
                right[:rows, at // 2 : (at + n) // 2] = total[:, n // 2 :]
                dsts = (left, right)
            else:
                dst[:rows, at : at + n] = total
                dsts = (dst,)
            for d in dsts:
                if rows < d.shape[0]:
                    lo, hi = (at // 2, (at + n) // 2) if s == 2 else (at, at + n)
                    d[rows:, lo:hi] = jnp.zeros((d.shape[0] - rows, hi - lo), BF)
        at += n


def core_sums(pairs, rows):
    n = sum(own.shape[2] for own, _ in pairs)
    whole, half = ((rows, n), BF), ((rows, n // 2), BF)
    return call(
        core_kernel, [whole, whole, whole, half, half], [a for p in pairs for a in p], vmem=32
    )


def relay_kernel(widths, c1, c3, left, right, out1, out3):
    at = 0
    for n in widths:
        h = n // 2
        part = slice(at // 2, at // 2 + h)
        out3[:, at : at + h] = low_sum(c3[:, at : at + h], left[:, part])
        out3[:, at + h : at + n] = c3[:, at + h : at + n]
        out1[:, at : at + h] = c1[:, at : at + h]
        out1[:, at + h : at + n] = low_sum(c1[:, at + h : at + n], right[:, part])
        at += n


def relayed(widths, c1, c3, left, right):
    whole = (c1.shape, BF)
    return call(
        functools.partial(relay_kernel, widths), [whole, whole], (c1, c3, left, right), vmem=24
    )


def pair_kernel(a, a1, b, b1, c0, c1, c3, left, right):
    n = a.shape[2]
    for s, dst in ((0, c0), (1, c1), (3, c3)):
        dst[:, :n] = low_sum(a[s], a1[s])
        dst[:, n:] = low_sum(b[s], b1[s])
    left[...] = low_sum(a[2], a1[2])
    right[...] = low_sum(b[2], b1[2])


def sent(parts, axis):
    return [parts[0]] + [flip(parts[s], axis, s) for s in (1, 2, 3)]


def second_kernel(a0, a1, a3, *outs):
    total = add(a0[...], a1[...], a3[...]).astype(BF)
    for y in range(4):
        for g in range(3):
            at = g * 32 + y * 8
            outs[y][g * 8 : (g + 1) * 8, :] = total[at : at + 8]
        outs[y][24:, :] = total[96:]


def third_kernel(m0, m1, m2, m3, *outs):
    total = add(m0[...], m1[...], m2[...], m3[...])
    for m in range(2):
        part = total[:, m * CQ : (m + 1) * CQ]
        for hi in range(2):
            rows = [part[g * 8 + hi * 4 : g * 8 + hi * 4 + 4] for g in range(3)]
            rows = jnp.concatenate(rows + [part[24:]], axis=0)
            outs[hi * 2 + m][...] = rows.astype(BF)


def last_sums_kernel(index, b0, b1, b3, q0, q1, q3, out):
    (hi0, z0, _, _), m0 = decoded(index[0])
    outer = add(b0[...], b1[...], b3[...])
    attn = add(q0[...], q1[...], q3[...])
    blank = jnp.zeros((2, HALF), F32)
    for m in range(2):
        part = jnp.concatenate(
            [outer[:, m * CH : (m + 1) * CH], attn[:96, m * CQ : (m + 1) * CQ]], axis=1
        )
        n = CH + CQ
        vec = [attn[96:97, m * CQ + i * HALF : m * CQ + (i + 1) * HALF] for i in range(2)]
        vec = jnp.concatenate(vec + [blank], axis=0)
        for z in range(4):
            for hi in range(2):
                r0, r1, r2 = (
                    part[g * 32 + z * 8 + hi * 4 : g * 32 + z * 8 + hi * 4 + 4] for g in range(3)
                )
                block = jnp.concatenate(
                    [
                        jnp.concatenate([r0, r2[:, : 5 * HALF]], axis=1),
                        jnp.concatenate([r1, r2[:, 5 * HALF :], vec], axis=1),
                    ],
                    axis=0,
                )
                out[((hi ^ hi0) * 2 + (m ^ m0)) * 4 + (z ^ z0)] = block.astype(BF)


def exchanged(blocks, axes):
    return lax.all_to_all(blocks, axes, 0, 0, tiled=True)


def total_of(blocks):
    total = blocks[0].astype(F32)
    for i in range(1, blocks.shape[0]):
        total = total + blocks[i].astype(F32)
    return total


def final_kernel(n0, n1, n2, n3, blocks, wq, wk, wv, wo, wi, wt, qb, vb, ib, ob, g1, s1, fb, g2, s2):
    total = add(n0[...], n1[...], n2[...], n3[...])
    wo[...] = total[:12, :HALF]
    wi[:, :FQ] = total[:12, HALF:]
    vec = jnp.concatenate([total[12 + i : 13 + i, :CQ] for i in range(6)], axis=1)
    at = 0
    for dst in (ib, ob, g1, s1, fb, g2, s2):
        dst[...] = vec[0, at : at + dst.shape[0]]
        at += dst.shape[0]
    total = total_of(blocks)
    n = CH + CQ
    tail = jnp.concatenate([total[:4, n:], total[4:, n : n + 4 * HALF]], axis=1)
    at = 0
    for dst, first, width in (
        (wt, 0, FHALF), (wi, FQ, FQ), (wq, 0, HALF), (wk, 0, HALF), (wv, 0, HALF)
    ):
        dst[:8, first : first + width] = total[:, at : at + width]
        dst[8:, first : first + width] = tail[:, at : at + width]
        at += width
    qb[...] = total[4, n + 4 * HALF :]
    vb[...] = total[5, n + 4 * HALF :]


def decoded(index):
    return (index >> 6, (index >> 4) & 3, (index >> 2) & 3, (index >> 1) & 1), index & 1


def row_of(vector):
    return vector[...].reshape(1, -1)


def order_matrix(place, swap):
    r = lax.broadcasted_iota(jnp.int32, (1, D), 1)
    j = r & 3
    hi = ((r >> 2) & 1) ^ place[0]
    near, far = (r >> 3) & 3, (r >> 5) & 3
    y = (far if swap else near) ^ place[2]
    z = (near if swap else far) ^ place[1]
    block = r >> 7
    core = jnp.where(block >= 3, 1, 0)
    group = block - 3 * core
    core = core ^ place[3]
    source = (((hi * 4 + z) * 4 + y) * 2 + core) * 12 + group * 4 + j
    rows = lax.broadcasted_iota(jnp.int32, (D, D), 0)
    return jnp.where(rows == source, 1.0, 0.0)


def swap_matrix():
    r = lax.broadcasted_iota(jnp.int32, (1, D), 1)
    source = (r & ~0x78) | ((r & 0x18) << 2) | ((r & 0x60) >> 2)
    rows = lax.broadcasted_iota(jnp.int32, (D, D), 0)
    return jnp.where(rows == source, 1.0, 0.0)


def exact(a, b, dims):
    return lax.dot_general(
        a, b, (dims, ((), ())), preferred_element_type=F32, precision=lax.Precision.HIGHEST
    )


def pack_kernel(wq, wk, wv, wo, wi, wt, out):
    at = 0
    for src, first, n in (
        (wq, 0, HALF),
        (wk, 0, HALF),
        (wv, 0, HALF),
        (wo, 0, HALF),
        (wi, 0, FQ),
        (wt, 0, FHALF),
        (wi, FQ, FQ),
    ):
        for g in range(3):
            out[g, :, at : at + n] = src[g * 4 : (g + 1) * 4, first : first + n]
        at += n


def decoded(index):
    return (index >> 6, (index >> 4) & 3, (index >> 2) & 3, (index >> 1) & 1), index & 1


def row_of(vector):
    return vector[...].reshape(1, -1)


def order_matrix(place, swap):
    r = lax.broadcasted_iota(jnp.int32, (1, D), 1)
    j = r & 3
    hi = ((r >> 2) & 1) ^ place[0]
    near, far = (r >> 3) & 3, (r >> 5) & 3
    y = (far if swap else near) ^ place[2]
    z = (near if swap else far) ^ place[1]
    block = r >> 7
    core = jnp.where(block >= 3, 1, 0)
    group = block - 3 * core
    core = core ^ place[3]
    source = (((hi * 4 + z) * 4 + y) * 2 + core) * 12 + group * 4 + j
    rows = lax.broadcasted_iota(jnp.int32, (D, D), 0)
    return jnp.where(rows == source, 1.0, 0.0)


def swap_matrix():
    r = lax.broadcasted_iota(jnp.int32, (1, D), 1)
    source = (r & ~0x78) | ((r & 0x18) << 2) | ((r & 0x60) >> 2)
    rows = lax.broadcasted_iota(jnp.int32, (D, D), 0)
    return jnp.where(rows == source, 1.0, 0.0)


def exact(a, b, dims):
    return lax.dot_general(
        a, b, (dims, ((), ())), preferred_element_type=F32, precision=lax.Precision.HIGHEST
    )


def order_kernel(
    index, x_all, y_all, ob, g1, s1, fb, g2, s2,
    order_a, order_b, swap, xr, xb, yr, vr, x, y, sems,
):
    place, mp = decoded(index[0])
    rows = pl.ds(pl.multiple_of(mp * T, T), T)
    copies = [
        pltpu.make_async_copy(src.at[rows, :], dst, sems.at[i])
        for i, (src, dst) in enumerate(((x_all, x), (y_all, y)))
    ]
    for c in copies:
        c.start()
    m = order_matrix(place, False)
    order_a[...] = m.astype(BF)
    blank = jnp.zeros((5, D), F32)
    vr[0:8, :] = exact(
        jnp.concatenate([row_of(ob), row_of(g1), row_of(s1), blank], axis=0), m, ((1,), (0,))
    )
    m = order_matrix(place, True)
    order_b[...] = m.astype(BF)
    vr[8:16, :] = exact(
        jnp.concatenate([row_of(fb), row_of(g2), row_of(s2), blank], axis=0), m, ((1,), (0,))
    )
    swap[...] = swap_matrix().astype(BF)
    for c in copies:
        c.wait()
    xr[...] = nn(x[...], order_a[...]).astype(BF)
    xb[...] = nn(x[...], order_b[...]).astype(BF)
    yr[...] = nn(y[...], order_b[...]).astype(BF)


def start_weight(pieces, first, width, dst, at, m, sem):
    for core in range(2):
        for i, z in enumerate((0, 1, 3, 2)):
            src = pieces[core * 5 + i + (m if z == 2 else 0)]
            col = first + (0 if z == 2 else m * CH)
            pltpu.make_async_copy(
                src.at[:, :, pl.ds(col, width)],
                dst.at[pl.ds(core * 3, 3), pl.ds(z * 32, 32), pl.ds(at, width)],
                sem,
            ).start()


def wait_weight(dst, at, width, sem):
    part = dst.at[:, :, pl.ds(at, width)]
    pltpu.make_async_copy(part, part, sem).wait()


def weight(w, at, width):
    return w[:, :, pl.ds(at, width)].reshape(D, width)


def row_starts(info, shape, axis):
    index, buckets, lengths = info
    mp = index[0] & 1
    shift = 7 + buckets[0, mp]
    pos = lax.broadcasted_iota(jnp.int32, shape, axis)
    seq = lax.shift_right_logical(pos, shift)
    within = pos & (lax.shift_left(1, shift) - 1)
    n0, n1, n2, n3 = (lengths[0, mp, i] for i in range(4))
    live = jnp.where(seq == 0, n0, jnp.where(seq == 1, n1, jnp.where(seq == 2, n2, n3)))
    return seq, within < live


def mask_bias(info, key_axis):
    kshape = (T, 1) if key_axis == 0 else (1, T)
    qshape = (1, T) if key_axis == 0 else (T, 1)
    kseq, live = row_starts(info, kshape, key_axis)
    qseq, _ = row_starts(info, qshape, 1 - key_axis)
    kseq = jnp.where(live, kseq, -1)
    return jnp.where(kseq == qseq, 0.0, -1e30)


def attention_kernel(
    index, buckets, lengths, xr, qb, vb, others, p0, p1, p2, p3, p4, p5, p6, p7, p8, p9,
    q, k, v, ctx, lse, w_out, w, qkv, biases, mask, lcol, sem, sem2,
):
    pieces = (p0, p1, p2, p3, p4, p5, p6, p7, p8, p9)
    for m in range(2):
        start_weight(pieces, 0, 3 * HALF, w, m * 3 * HALF, m, sem)
    mask[...] = mask_bias((index, buckets, lengths), 1)
    wait_weight(w, 0, 6 * HALF, sem)
    keep = pltpu.make_async_copy(w, w_out, sem2)
    keep.start()
    zero = jnp.zeros((1, HALF), F32)
    for m in range(2):
        for i, own in enumerate((qb, None, vb)):
            if i == 1:
                b = zero
            elif m == 0:
                b = row_of(own)
            else:
                b = others[pl.ds((i >> 1) * HALF, HALF)].reshape(1, HALF)
            biases[m * 3 + i : m * 3 + i + 1, :] = b

    def project(i, _):
        a = nn(xr[...], weight(w, pl.multiple_of(i * HALF, HALF), HALF)) + biases[pl.ds(i, 1), :]
        scale = jnp.where((i == 0) | (i == 3), 0.125, 1.0)
        qkv[i] = (a.astype(BF).astype(F32) * scale).astype(BF)
        return 0

    lax.fori_loop(0, 6, project, 0)
    for i in range(6):
        (q, k, v)[i % 3][:, (i // 3) * HALF : (i // 3 + 1) * HALF] = qkv[i]
    lcol[...] = jnp.zeros_like(lcol)
    lane = lax.broadcasted_iota(jnp.int32, (1, 128), 1)

    def pair(i, _):
        cols = pl.ds(pl.multiple_of(i * 128, 128), 128)
        q2, k2, v2 = q[:, cols], k[:, cols], v[:, cols]
        total = None
        for half in range(2):
            mine = (lane < 64) if half == 0 else (lane >= 64)
            s = nt(jnp.where(mine, q2, BF(0)), k2) + mask[...]
            peak = jnp.max(s, axis=1, keepdims=True)
            e = jnp.exp(s - peak)
            z = jnp.sum(e, axis=1, keepdims=True)
            p = (e / z).astype(BF)
            c = nn(p, jnp.where(mine, v2, BF(0)))
            total = c if total is None else total + c
            l = peak + jnp.log(z)
            lcol[...] = jnp.where(lane == i * 2 + half, l, lcol[...])
        ctx[:, cols] = total.astype(BF)
        return 0

    lax.fori_loop(0, 6, pair, 0)
    lse[...] = lcol[...].T[0:16, :]
    keep.wait()


def stats(a):
    mean = jnp.mean(a, axis=1, keepdims=True)
    a = a - mean
    r = lax.rsqrt(jnp.mean(a * a, axis=1, keepdims=True) + EPS)
    return a * r, r


def norm_back(dy, n, r, gain):
    a = dy * gain
    return r * (
        a - jnp.mean(a, axis=1, keepdims=True) - n * jnp.mean(a * n, axis=1, keepdims=True)
    )


def store_rows(own, other, value, cols):
    for core, dst in enumerate((own, other)):
        for g in range(3):
            for z in range(4):
                at = ((core * 3 + g) * 4 + z) * 32
                dst[z, g * 32 : (g + 1) * 32, cols] = value[at : at + 32]


def store_vectors(own, other, value):
    for dst in (own, other):
        for z in range(4):
            dst[z, 96:104, :] = value


def unit_source(f):
    return f < 2, (4 * HALF if f < 2 else 2 * FQ), f & 1


def up_kernel(
    ctx, xr, yr, vr, inb, others, order_b, swap,
    a0, a1, a2, a3, a4, a5, a6, a7, a8, a9, b0, b1, b2, b3, b4, b5, b6, b7, b8, b9,
    out, h1t_out, n1_out, r1, df, da, dinb, sums, slope_out, grads_out, grads1_out,
    wo, wi, wt, hs, hts, biases, n1, gact, slope, big, lowt, grads, grads1, sems, keeps, goes,
):
    ap = (a0, a1, a2, a3, a4, a5, a6, a7, a8, a9)
    bp = (b0, b1, b2, b3, b4, b5, b6, b7, b8, b9)
    for m in range(2):
        start_weight(ap, 3 * HALF, HALF, wo, m * HALF, m, sems.at[0])
    for f in range(4):
        first, col, m = unit_source(f)
        start_weight(ap if first else bp, col, FQ, wi, f * FQ, m, sems.at[1 + f])
        start_weight(bp, (f >> 1) * FQ, FQ, wt, f * FQ, m, sems.at[5 + f])
    wait_weight(wo, 0, D, sems.at[0])
    ob, g1, s1 = (vr[i : i + 1, :] for i in range(3))
    fb, g2, s2 = (vr[i : i + 1, :] for i in range(8, 11))
    nrm, r = stats(nt(ctx[...], weight(wo, 0, D)) + ob + xr[...].astype(F32))
    n1[...] = nrm
    keep = []

    def send(src, dst, sem):
        keep.append(pltpu.make_async_copy(src, dst, sem))
        keep[-1].start()

    send(n1, n1_out, keeps.at[2])
    r1[...] = jnp.broadcast_to(r, (T, 128))
    low = nrm * g1 + s1
    hs[0] = low.astype(BF)
    hts[0] = low.T.astype(BF)
    send(hts.at[0], h1t_out, keeps.at[3])
    low = nn(hs[0], swap[...])
    hs[1] = low.astype(BF)
    hts[1] = low.T.astype(BF)
    big[...] = hs[1].astype(F32) + fb
    for f in range(4):
        bias, at = (inb, 0) if f & 1 == 0 else (others, D)
        biases[f : f + 1, :] = bias[pl.ds(at + (f >> 1) * FQ, FQ)].reshape(1, FQ)

    def up(f, _):
        at = pl.multiple_of(f * FQ, FQ)
        wait_weight(wi, at, FQ, sems.at[1 + f])
        u = nn(hs[f >> 1], weight(wi, at, FQ)) + biases[pl.ds(f, 1), :]
        phi = 0.5 + 0.5 * lax.erf(u * INV_SQRT2)
        slope[f] = phi + u * (jnp.exp(-0.5 * u * u) * INV_SQRT2PI)

        @pl.when(f < 2)
        def _():
            pltpu.make_async_copy(slope.at[f], slope_out.at[f], keeps.at[f]).start()

        g = (u * phi).astype(BF)
        gact[:, pl.ds(at, FQ)] = g
        wait_weight(wt, at, FQ, sems.at[5 + f])
        big[...] += nt(g, weight(wt, at, FQ))
        return 0

    lax.fori_loop(0, 4, up, 0)
    keep += [pltpu.make_async_copy(slope.at[f], slope_out.at[f], keeps.at[f]) for f in range(2)]
    n2, r2 = stats(big[...])
    low = (n2 * g2 + s2).astype(BF)
    out[...] = nt(low, order_b[...]).astype(BF)
    y = yr[...].astype(F32)
    sums[1:2, :] = jnp.sum(y * n2, axis=0, keepdims=True)
    sums[2:3, :] = jnp.sum(y, axis=0, keepdims=True)
    d = norm_back(y, n2, r2, g2)
    big[...] = d
    low = d.astype(BF)
    df[...] = low
    sums[0:1, :] = jnp.sum(low.astype(F32), axis=0, keepdims=True)
    sums[3:8, :] = jnp.zeros((5, D), F32)
    lowt[...] = d.T.astype(BF)

    def go(first, width, sem):
        for k, (src, dst) in enumerate(((grads, grads_out), (grads1, grads1_out))):
            cols = pl.ds(first, width)
            yield pltpu.make_async_copy(src.at[:, :, cols], dst.at[:, :, cols], sem(k))

    def outer(f, _):
        g = nn(lowt[...], gact[:, pl.ds(pl.multiple_of(f * FQ, FQ), FQ)]).astype(BF)
        at = pl.multiple_of((f & 1) * CH + (f >> 1) * FQ, FQ)
        store_rows(grads, grads1, g, pl.ds(at, FQ))

        @pl.when(f >= 2)
        def _():
            for c in go(pl.multiple_of((f & 1) * CH, CH), FHALF, lambda k: goes.at[k, f & 1]):
                c.start()

        return 0

    lax.fori_loop(0, 4, outer, 0)

    def inner(m, _):
        f = m + 2
        at = pl.multiple_of(f * FQ, FQ)
        du = (nn(df[...], weight(wt, at, FQ)) * slope[f]).astype(BF)
        dinb[:, pl.ds(pl.multiple_of(m * FQ, FQ), FQ)] = jnp.sum(
            du.astype(F32), axis=0, keepdims=True
        )
        big[...] += nt(du, weight(wi, at, FQ))
        g = nn(hts[1], du).astype(BF)
        to = pl.multiple_of(m * CH + FHALF, FQ)
        store_rows(grads, grads1, g, pl.ds(to, FQ))
        for c in go(to, FQ, lambda k: goes.at[2 + k, m]):
            c.start()
        return 0

    lax.fori_loop(0, 2, inner, 0)
    for m in range(2):
        keep += list(go(m * CH, FHALF, lambda k, m=m: goes.at[k, m]))
        keep += list(go(m * CH + FHALF, FQ, lambda k, m=m: goes.at[2 + k, m]))
    d = big[...]
    hi = d.astype(BF)
    lo = (d - hi.astype(F32)).astype(BF)
    da[...] = nt(hi, swap[...]) + nt(lo, swap[...])
    for k in keep:
        k.wait()


def down_units(df, wi, wt, slope, big, h1t, dinb, grads, grads1, sems, keeps, slope_in):
    def down(f, _):
        at = pl.multiple_of(f * FQ, FQ)
        wait_weight(wt, at, FQ, sems.at[2 * f])
        pltpu.make_async_copy(slope_in.at[f], slope.at[f], keeps.at[f]).wait()
        du = (nn(df[...], weight(wt, at, FQ)) * slope[f]).astype(BF)
        dinb[pl.ds(f, 1), :] = jnp.sum(du.astype(F32), axis=0, keepdims=True)
        wait_weight(wi, at, FQ, sems.at[2 * f + 1])
        big[...] += nt(du, weight(wi, at, FQ))
        g = nn(h1t[...], du).astype(BF)
        store_rows(grads, grads1, g, pl.ds(pl.multiple_of(f * CQ + HALF, HALF), FQ))
        return 0

    lax.fori_loop(0, 2, down, 0)


def start_units(units, ap, bp, wi, wt, slope_in, slope, sems, keeps):
    for i, f in enumerate(units):
        first, col, m = unit_source(f)
        start_weight(bp, (f >> 1) * FQ, FQ, wt, i * FQ, m, sems.at[2 * i])
        pltpu.make_async_copy(slope_in.at[f], slope.at[i], keeps.at[i]).start()
        start_weight(ap if first else bp, col, FQ, wi, i * FQ, m, sems.at[2 * i + 1])


def down_kernel1(
    h1t, r1, df, dinb, sums, vr, ctx_all, n1_all, da_in, order_a_all, order_b_all, slope_in,
    a0, a1, a2, a3, a4, a5, a6, a7, a8, a9, b0, b1, b2, b3, b4, b5, b6, b7, b8, b9,
    dc, dr, grads, grads1,
    wo, wi, wt, slope, big, lowt, inner, ctx, n1, order_a, order_b, sems, keeps, loads,
):
    ap = (a0, a1, a2, a3, a4, a5, a6, a7, a8, a9)
    bp = (b0, b1, b2, b3, b4, b5, b6, b7, b8, b9)
    start_units((0, 1), ap, bp, wi, wt, slope_in, slope, sems, keeps)
    for m in range(2):
        start_weight(ap, 3 * HALF, HALF, wo, m * HALF, m, sems.at[4])
    copies = [
        pltpu.make_async_copy(src, dst, loads.at[i])
        for i, (src, dst) in enumerate(
            (
                (da_in, big),
                (n1_all, n1),
                (ctx_all, ctx),
                (order_a_all, order_a),
                (order_b_all, order_b),
            )
        )
    ]
    for c in copies:
        c.start()
    copies[0].wait()
    down_units(df, wi, wt, slope, big, h1t, inner, grads, grads1, sems, keeps, slope_in)
    for c in copies[1:]:
        c.wait()
    dh = big[...]
    nrm = n1[...]
    g1 = vr[1:2, :]
    dg1 = jnp.sum(dh * nrm, axis=0, keepdims=True)
    ds1 = jnp.sum(dh, axis=0, keepdims=True)
    d = norm_back(dh, nrm, r1[:, 0:1], g1)
    dr[...] = d
    da = d.astype(BF)
    dob = jnp.sum(da.astype(F32), axis=0, keepdims=True)
    wait_weight(wo, 0, D, sems.at[4])
    dc[...] = nn(da, weight(wo, 0, D)).astype(BF)
    lowt[...] = d.T.astype(BF)
    g = nn(lowt[...], ctx[...]).astype(BF)
    for m in range(2):
        store_rows(grads, grads1, g[:, m * HALF : (m + 1) * HALF], pl.ds(m * CQ, HALF))
    sa = exact(
        jnp.concatenate([dob, dg1, ds1, dob, dob, dob, dob, dob], axis=0),
        order_a[...].astype(F32),
        ((1,), (1,)),
    )
    sb = exact(sums[...], order_b[...].astype(F32), ((1,), (1,)))
    sides = []
    for m in range(2):
        line = jnp.concatenate(
            [inner[m : m + 1, :], dinb[:, m * FQ : (m + 1) * FQ]]
            + [sa[i : i + 1] for i in range(3)]
            + [sb[i : i + 1] for i in range(3)]
            + [jnp.zeros((1, 6 * CQ - 8 * FQ), F32)],
            axis=1,
        )
        rows = [line[:, i * CQ : (i + 1) * CQ] for i in range(6)]
        sides.append(jnp.concatenate(rows + [jnp.zeros((2, CQ), F32)], axis=0))
    store_vectors(grads, grads1, jnp.concatenate(sides, axis=1).astype(BF))


def back_half(
    m, index, buckets, lengths, q, k, v, dc, lse, xb_all, w_all, dr,
    grads, grads1, mask, dqkv, big, qb, vb, xt_ref, w, xb, sems,
):
    copies = [
        pltpu.make_async_copy(w_all.at[:, :, pl.ds(m * 3 * HALF, 3 * HALF)], w, sems.at[0]),
        pltpu.make_async_copy(xb_all, xb, sems.at[1]),
        pltpu.make_async_copy(dr, big, sems.at[2]),
    ]
    for c in copies:
        c.start()
    mask[...] = mask_bias((index, buckets, lengths), 0)
    lane = lax.broadcasted_iota(jnp.int32, (1, 128), 1)

    def pair(i, _):
        head = pl.ds(pl.multiple_of(m * HALF + i * 128, 128), 128)
        cols = pl.ds(pl.multiple_of(i * 128, 128), 128)
        q2, k2, v2, c2 = q[:, head], k[:, head], v[:, head], dc[:, head]
        outs = []
        for half in range(2):
            mine = (lane < 64) if half == 0 else (lane >= 64)
            s = nt(jnp.where(mine, k2, BF(0)), q2) + mask[...]
            p = jnp.exp(s - lse[pl.ds(m * 6 + i * 2 + half, 1), :])
            dp = nt(jnp.where(mine, v2, BF(0)), c2)
            delta = jnp.sum(dp * p, axis=0, keepdims=True)
            ds = (p * (dp - delta)).astype(BF)
            outs.append((tn(ds, k2), nn(ds, q2), nn(p.astype(BF), c2)))
        first = lane < 64
        dq2, dk2, dv2 = (jnp.where(first, a, b) for a, b in zip(*outs))
        dq2 = (dq2 * 0.125).astype(BF)
        dk2 = dk2.astype(BF)
        dv2 = dv2.astype(BF)
        dqkv[0, :, cols] = dq2
        dqkv[1, :, cols] = dk2
        dqkv[2, :, cols] = dv2
        qb[:, cols] = jnp.sum(dq2.astype(F32), axis=0, keepdims=True)
        vb[:, cols] = jnp.sum(dv2.astype(F32), axis=0, keepdims=True)
        return 0

    lax.fori_loop(0, 3, pair, 0)
    for c in copies:
        c.wait()
    xt_ref[...] = xb[...].astype(F32).T.astype(BF)

    def weights(i, _):
        to = pl.multiple_of(i * HALF, HALF)
        a = dqkv[i]
        store_rows(grads, grads1, nn(xt_ref[...], a).astype(BF), pl.ds(to, HALF))
        big[...] += nt(a, weight(w, to, HALF))
        return 0

    lax.fori_loop(0, 3, weights, 0)
    line = jnp.concatenate([qb[...], vb[...], jnp.zeros((1, HALF), F32)], axis=1)
    line = jnp.concatenate([line, jnp.zeros((7, CQ), F32)], axis=0)
    store_vectors(grads, grads1, line.astype(BF))


def back_kernel0(
    index, buckets, lengths, q, k, v, dc, lse, xb, w, dr,
    grads, grads1, out, mask, dqkv, *scratch,
):
    ins = (index, buckets, lengths, q, k, v, dc, lse, xb, w, dr)
    big = scratch[0]
    back_half(0, *ins, grads, grads1, mask, dqkv, *scratch)
    out[...] = big[...]


def back_kernel1(
    index, buckets, lengths, q, k, v, dc, lse, xb, w, dr,
    grads, grads1, gin, mask, dqkv, *scratch,
):
    ins = (index, buckets, lengths, q, k, v, dc, lse, xb, w, dr)
    big = scratch[0]
    back_half(1, *ins, grads, grads1, mask, dqkv, *scratch)
    gin[...] = big[...].astype(BF)


def last_kernel(gin, order, out):
    out[...] = nt(gin[...], order[...]).astype(BF)


def call(kernel, outs, args, scratch=(), vmem=48, flops=0, smem=0, hbm=(), anyouts=()):
    specs = []
    for i in range(len(args)):
        if i < smem:
            specs.append(pl.BlockSpec(memory_space=pltpu.SMEM))
        elif i in hbm:
            specs.append(pl.BlockSpec(memory_space=pl.ANY))
        else:
            specs.append(pl.BlockSpec(memory_space=VMEM))
    return pl.pallas_call(
        kernel,
        out_shape=[jax.ShapeDtypeStruct(s, d) for s, d in outs],
        in_specs=specs,
        out_specs=[
            pl.BlockSpec(memory_space=pl.ANY if i in anyouts else VMEM) for i in range(len(outs))
        ],
        scratch_shapes=list(scratch),
        compiler_params=pltpu.CompilerParams(vmem_limit_bytes=vmem * 2**20),
        cost_estimate=pl.CostEstimate(flops=flops // 1000, bytes_accessed=1000, transcendentals=0),
    )(*args)


def body(
    hidden_in, buckets, lengths, query_weight, key_weight, value_weight, query_bias, value_bias,
    output_weight, output_bias, first_gain, first_shift, inner_weight, inner_bias, outer_weight,
    outer_bias, second_gain, second_shift, cotangent,
):
    mp = lax.axis_index("mp")
    index = lax.axis_index((*DP, "mp")).astype(jnp.int32).reshape(1)
    info = (index, buckets, lengths)
    (shard,) = call(
        pack_kernel,
        [((3, 4, 2 * CH), BF)],
        (query_weight, key_weight, value_weight, output_weight.T, inner_weight, outer_weight.T),
        vmem=60,
    )
    biases = jnp.concatenate([query_bias, value_bias, inner_bias])
    others = flip(biases, "mp", 1)
    def sides(mine, other):
        return jnp.where(
            mp == 0, jnp.concatenate([mine, other], axis=0), jnp.concatenate([other, mine], axis=0)
        )

    square = ((D, D), BF)
    tokens = ((T, D), BF)
    order_a, order_b, swap, xr, xb, yr, vr = call(
        order_kernel,
        [square, square, square, tokens, tokens, tokens, ((16, D), F32)],
        (
            index,
            hidden_in,
            cotangent,
            output_bias,
            first_gain,
            first_shift,
            outer_bias,
            second_gain,
            second_shift,
        ),
        [VMEM((T, D), BF), VMEM((T, D), BF), pltpu.SemaphoreType.DMA((2,))],
        smem=1,
        hbm=(1, 2),
        vmem=60,
        flops=2 * 10**9,
    )
    pa, pb, (xr, xb, yr, others) = gather(shard, (xr, xb, yr, others))
    pa = with_other_core(pa)
    q, k, v, ctx, lse, w = call(
        attention_kernel,
        [tokens, tokens, tokens, tokens, ((16, T), F32), ((6, 128, 6 * HALF), BF)],
        (*info, xr, query_bias, value_bias, others, *pa),
        [
            VMEM((6, 128, 6 * HALF), BF),
            VMEM((6, T, HALF), BF),
            VMEM((8, HALF), F32),
            VMEM((T, T), F32),
            VMEM((T, 128), F32),
            pltpu.SemaphoreType.DMA(()),
            pltpu.SemaphoreType.DMA(()),
        ],
        smem=3,
        hbm=range(7, 17),
        anyouts=(5,),
        vmem=60,
        flops=10 * 10**9,
    )
    ctx, pb[3], pb[4] = lax.optimization_barrier((ctx, pb[3], pb[4]))
    pb = with_other_core(pb)
    gb, ga = ((4, 96, 2 * CH), BF), ((4, 104, 2 * CQ), BF)
    wide = ((T, D), F32)
    out, h1t, n1, r1, df, da, dinb, sums, slope, grads_b, grads_b1 = call(
        up_kernel,
        [
            tokens,
            ((D, T), BF),
            wide,
            ((T, 128), F32),
            tokens,
            wide,
            ((1, 2 * FQ), F32),
            ((8, D), F32),
            ((2, T, FQ), F32),
            gb,
            gb,
        ],
        (ctx, xr, yr, vr, inner_bias, others, order_b, swap, *pa, *pb),
        [
            VMEM((6, 128, D), BF),
            VMEM((6, 128, FF), BF),
            VMEM((6, 128, FF), BF),
            VMEM((2, T, D), BF),
            VMEM((2, D, T), BF),
            VMEM((8, FQ), F32),
            VMEM((T, D), F32),
            VMEM((T, FF), BF),
            VMEM((4, T, FQ), F32),
            VMEM((T, D), F32),
            VMEM((D, T), BF),
            VMEM(*gb),
            VMEM(*gb),
            pltpu.SemaphoreType.DMA((9,)),
            pltpu.SemaphoreType.DMA((4,)),
            pltpu.SemaphoreType.DMA((4, 2)),
        ],
        hbm=range(8, 28),
        anyouts=(1, 2, 8, 9, 10),
        vmem=56,
        flops=8 * 10**9,
    )
    grads_b1 = flip(grads_b1, AC, 1)
    out_own, out = out, flip(out, "mp", 1)
    half = [VMEM((6, 128, 2 * FQ), BF)] * 2 + [VMEM((2, T, FQ), F32), VMEM((T, D), F32)]
    dc, dr, grads_a, grads_a1 = call(
        down_kernel1,
        [tokens, wide, ga, ga],
        (h1t, r1, df, dinb, sums, vr, ctx, n1, da, order_a, order_b, slope, *pa, *pb),
        [VMEM((6, 128, D), BF)]
        + half
        + [
            VMEM((D, T), BF),
            VMEM((8, FQ), F32),
            VMEM((T, D), BF),
            VMEM((T, D), F32),
            VMEM((D, D), BF),
            VMEM((D, D), BF),
            pltpu.SemaphoreType.DMA((5,)),
            pltpu.SemaphoreType.DMA((2,)),
            pltpu.SemaphoreType.DMA((5,)),
        ],
        hbm=range(6, 32),
        vmem=60,
        flops=4 * 10**9,
    )
    b0, b1, b3, bl, br = core_sums([(grads_b, grads_b1)], 96)
    grads_a1 = flip(grads_a1, AC, 1)
    b0, grads_a1 = lax.optimization_barrier((b0, grads_a1))
    a0, a1, a3, al, ar = core_sums([(grads_a, grads_a1)], 104)
    dc, b0, b1, b3, bl, br, a0, a1, a3, al, ar = lax.optimization_barrier(
        (dc, b0, b1, b3, bl, br, a0, a1, a3, al, ar)
    )
    bl, br = flip(bl, AY, 1), flip(br, AY, 3)
    al, ar = flip(al, AZ, 1), flip(ar, AZ, 3)
    gq = ((4, 104, CQ), BF)
    scratch = [
        VMEM((T, T), F32),
        VMEM((3, T, HALF), BF),
        VMEM((T, D), F32),
        VMEM((1, HALF), F32),
        VMEM((1, HALF), F32),
        VMEM((D, T), BF),
        VMEM((6, 128, 3 * HALF), BF),
        VMEM((T, D), BF),
        pltpu.SemaphoreType.DMA((3,)),
    ]
    q00, q01, big = call(
        back_kernel0,
        [gq, gq, wide],
        (*info, q, k, v, dc, lse, xb, w, dr),
        scratch,
        smem=3,
        hbm=(8, 9, 10),
        vmem=34,
        flops=7 * 10**9,
    )
    b1, b3 = relayed((2 * CH,), b1, b3, bl, br)
    a1, a3 = relayed((2 * CQ,), a1, a3, al, ar)
    big, b1, b3, a1, a3, out = lax.optimization_barrier((big, b1, b3, a1, a3, out))
    b1, b3 = flip(b1, AY, 1), flip(b3, AY, 3)
    a1, a3 = flip(a1, AZ, 1), flip(a3, AZ, 3)
    q10, q11, gin = call(
        back_kernel1,
        [gq, gq, tokens],
        (*info, q, k, v, dc, lse, xb, w, big),
        scratch,
        smem=3,
        hbm=(8, 9, 10),
        vmem=34,
        flops=7 * 10**9,
    )
    q01, q11, b1, b3, a1, a3 = lax.optimization_barrier((q01, q11, b1, b3, a1, a3))
    q01, q11 = flip(q01, AC, 1), flip(q11, AC, 1)
    whole, part = ((104, 2 * CQ), BF), ((104, CQ), BF)
    q0, q1, q3, left, right = call(
        pair_kernel, [whole, whole, whole, part, part], (q00, q01, q10, q11), vmem=24
    )
    left, right = flip(left, AY, 1), flip(right, AY, 3)
    q1, q3 = relayed((2 * CQ,), q1, q3, left, right)
    q1, q3 = flip(q1, AY, 1), flip(q3, AY, 3)
    (gin,) = call(last_kernel, [tokens], (gin, order_a), vmem=16)
    theirs = flip(gin, "mp", 1)
    q0, q1, q3, theirs = lax.optimization_barrier((q0, q1, q3, theirs))
    fa = sent(call(second_kernel, [((32, 2 * CQ), BF)] * 4, (a0, a1, a3), vmem=24), AY)
    fa = sent(call(third_kernel, [((20, CQ), BF)] * 4, fa, vmem=24), AX)
    (blocks,) = call(
        last_sums_kernel,
        [((16, 8, 14 * HALF), BF)],
        (index, b0, b1, b3, q0, q1, q3),
        smem=1,
        vmem=32,
    )
    blocks = exchanged(blocks, (*AX, AZ))
    small, inner, vector = ((12, HALF), F32), ((12, FHALF), F32), ((D,), F32)
    half = ((HALF,), F32)
    wq, wk, wv, wo, wi, wt, qb, vb, ib, *vecs = call(
        final_kernel,
        [small] * 4 + [inner] * 2 + [half] * 2 + [((FHALF,), F32)] + [vector] * 6,
        (*fa, blocks),
        vmem=24,
    )
    layer_out = sides(out_own, out)
    input_grad = sides(gin, theirs).astype(F32)
    dob, dg1, ds1, dfb, dg2, ds2 = vecs
    return (
        layer_out, input_grad, wq, wk, wv, qb, vb, wo.T, dob, dg1, ds1, wi, ib, wt.T, dfb, dg2, ds2
    )


def solution(mesh):
    torus = Mesh(
        mesh.devices.reshape(2, 4, 4, 2, mesh.shape["mp"]), ("dp_0", "dp_1", "dp_2", "dp_3", "mp")
    )
    row, col, half = P(DP, "mp"), P("mp", DP), P("mp")
    in_specs = (
        P(DP, None), P(DP, None), P(DP, None, None), row, row, row, half, half, col, P(), P(), P(),
        row, half, col, P(), P(), P(), P(DP, None),
    )
    out_specs = (
        P(DP, None), P(DP, None), row, row, row, half, half, col, P(), P(), P(), row, half, col,
        P(), P(), P(),
    )
    return jax.shard_map(body, mesh=torus, in_specs=in_specs, out_specs=out_specs, check_vma=False)
```

```python
import functools

import jax
import jax.numpy as jnp
from jax import lax
from jax.experimental import pallas as pl
from jax.experimental.pallas import tpu as pltpu
from jax.sharding import Mesh
from jax.sharding import PartitionSpec as P

DP = ("dp_0", "dp_1", "dp_2", "dp_3")
AX = ("dp_0", "mp")
AZ, AY, AC = "dp_1", "dp_2", "dp_3"
D = 768
T = 512
DH = 64
FF = 3072
HALF = 384
FHALF = 1536
FQ = 768
CH = 2304
CQ = 1152
CA = 1920
EPS = 1e-12
BF = jnp.bfloat16
F32 = jnp.float32
VMEM = pltpu.VMEM
INV_SQRT2 = 0.7071067811865476
INV_SQRT2PI = 0.3989422804014327


def nn(a, b):
    return lax.dot_general(a, b, (((1,), (0,)), ((), ())), preferred_element_type=F32)


def nt(a, b):
    return lax.dot_general(a, b, (((1,), (1,)), ((), ())), preferred_element_type=F32)


def tn(a, b):
    return lax.dot_general(a, b, (((0,), (0,)), ((), ())), preferred_element_type=F32)


def flip(a, axis, s):
    n = 4 if axis in (AX, AY, AZ) else 2
    return lax.ppermute(a, axis, [(i, i ^ s) for i in range(n)])


def joined(a, axis):
    return jnp.concatenate([a] + [flip(a, axis, s) for s in (1, 2, 3)], axis=1)


def gather(shard, ready):
    a = shard
    p1, p2, p3 = (flip(a, AX, s) for s in (1, 2, 3))
    parts = []
    for first in (0, CH):
        cols = slice(first, first + CH)
        a0, a1, a2, a3 = (p[:, :, cols] for p in (a, p1, p2, p3))
        parts.append(
            jnp.concatenate(
                [jnp.concatenate([a0, a2], axis=1), jnp.concatenate([a1, a3], axis=1)], axis=2
            )
        )
    parts = lax.optimization_barrier((joined(parts[0], AY), joined(parts[1], AZ)))
    near = [[flip(b, axis, s) for s in (1, 3)] for b, axis in zip(parts, (AZ, AY))]
    near, ready = lax.optimization_barrier((near, ready))
    out = []
    for b, axis, (n1, n3) in zip(parts, (AZ, AY), near):
        far = [flip(n1[:, :, :CH], axis, 3), flip(n3[:, :, CH:], axis, 1)]
        out.append([b, n1, n3, *far])
    return *out, ready


def with_other_core(own):
    return own + [flip(o, AC, 1) for o in own]


def add(*parts):
    total = parts[0].astype(F32)
    for p in parts[1:]:
        total = total + p.astype(F32)
    return total


def low_sum(*parts):
    return add(*parts).astype(BF)


def core_kernel(*refs):
    c0, c1, c3, left, right = refs[-5:]
    pairs = [refs[i : i + 2] for i in range(0, len(refs) - 5, 2)]
    at = 0
    for own, other in pairs:
        rows, n = own.shape[1:]
        for s, dst in ((0, c0), (1, c1), (3, c3), (2, None)):
            total = low_sum(own[s], other[s])
            if s == 2:
                left[:rows, at // 2 : (at + n) // 2] = total[:, : n // 2]
                right[:rows, at // 2 : (at + n) // 2] = total[:, n // 2 :]
                dsts = (left, right)
            else:
                dst[:rows, at : at + n] = total
                dsts = (dst,)
            for d in dsts:
                if rows < d.shape[0]:
                    lo, hi = (at // 2, (at + n) // 2) if s == 2 else (at, at + n)
                    d[rows:, lo:hi] = jnp.zeros((d.shape[0] - rows, hi - lo), BF)
        at += n


def core_sums(pairs, rows):
    n = sum(own.shape[2] for own, _ in pairs)
    whole, half = ((rows, n), BF), ((rows, n // 2), BF)
    return call(
        core_kernel, [whole, whole, whole, half, half], [a for p in pairs for a in p], vmem=32
    )


def relay_kernel(widths, c1, c3, left, right, out1, out3):
    at = 0
    for n in widths:
        h = n // 2
        part = slice(at // 2, at // 2 + h)
        out3[:, at : at + h] = low_sum(c3[:, at : at + h], left[:, part])
        out3[:, at + h : at + n] = c3[:, at + h : at + n]
        out1[:, at : at + h] = c1[:, at : at + h]
        out1[:, at + h : at + n] = low_sum(c1[:, at + h : at + n], right[:, part])
        at += n


def relayed(widths, c1, c3, left, right):
    whole = (c1.shape, BF)
    return call(
        functools.partial(relay_kernel, widths), [whole, whole], (c1, c3, left, right), vmem=24
    )


def pair_kernel(a, a1, b, b1, c0, c1, c3, left, right):
    n = a.shape[2]
    for s, dst in ((0, c0), (1, c1), (3, c3)):
        dst[:, :n] = low_sum(a[s], a1[s])
        dst[:, n:] = low_sum(b[s], b1[s])
    left[...] = low_sum(a[2], a1[2])
    right[...] = low_sum(b[2], b1[2])


def sent(parts, axis):
    return [parts[0]] + [flip(parts[s], axis, s) for s in (1, 2, 3)]


def second_kernel(a0, a1, a3, *outs):
    total = add(a0[...], a1[...], a3[...]).astype(BF)
    for y in range(4):
        for g in range(3):
            at = g * 32 + y * 8
            outs[y][g * 8 : (g + 1) * 8, :] = total[at : at + 8]
        outs[y][24:, :] = total[96:]


def third_kernel(m0, m1, m2, m3, *outs):
    total = add(m0[...], m1[...], m2[...], m3[...])
    for m in range(2):
        part = total[:, m * CQ : (m + 1) * CQ]
        for hi in range(2):
            rows = [part[g * 8 + hi * 4 : g * 8 + hi * 4 + 4] for g in range(3)]
            rows = jnp.concatenate(rows + [part[24:]], axis=0)
            outs[hi * 2 + m][...] = rows.astype(BF)


def last_sums_kernel(index, b0, b1, b3, q0, q1, q3, out):
    (hi0, z0, _, _), m0 = decoded(index[0])
    outer = add(b0[...], b1[...], b3[...])
    attn = add(q0[...], q1[...], q3[...])
    blank = jnp.zeros((2, HALF), F32)
    for m in range(2):
        part = jnp.concatenate(
            [outer[:, m * CH : (m + 1) * CH], attn[:96, m * CQ : (m + 1) * CQ]], axis=1
        )
        n = CH + CQ
        vec = [attn[96:97, m * CQ + i * HALF : m * CQ + (i + 1) * HALF] for i in range(2)]
        vec = jnp.concatenate(vec + [blank], axis=0)
        for z in range(4):
            for hi in range(2):
                r0, r1, r2 = (
                    part[g * 32 + z * 8 + hi * 4 : g * 32 + z * 8 + hi * 4 + 4] for g in range(3)
                )
                block = jnp.concatenate(
                    [
                        jnp.concatenate([r0, r2[:, : 5 * HALF]], axis=1),
                        jnp.concatenate([r1, r2[:, 5 * HALF :], vec], axis=1),
                    ],
                    axis=0,
                )
                out[((hi ^ hi0) * 2 + (m ^ m0)) * 4 + (z ^ z0)] = block.astype(BF)


def exchanged(blocks, axes):
    return lax.all_to_all(blocks, axes, 0, 0, tiled=True)


def total_of(blocks):
    total = blocks[0].astype(F32)
    for i in range(1, blocks.shape[0]):
        total = total + blocks[i].astype(F32)
    return total


def final_kernel(n0, n1, n2, n3, blocks, wq, wk, wv, wo, wi, wt, qb, vb, ib, ob, g1, s1, fb, g2, s2):
    total = add(n0[...], n1[...], n2[...], n3[...])
    wo[...] = total[:12, :HALF]
    wi[:, :FQ] = total[:12, HALF:]
    vec = jnp.concatenate([total[12 + i : 13 + i, :CQ] for i in range(6)], axis=1)
    at = 0
    for dst in (ib, ob, g1, s1, fb, g2, s2):
        dst[...] = vec[0, at : at + dst.shape[0]]
        at += dst.shape[0]
    total = total_of(blocks)
    n = CH + CQ
    tail = jnp.concatenate([total[:4, n:], total[4:, n : n + 4 * HALF]], axis=1)
    at = 0
    for dst, first, width in (
        (wt, 0, FHALF), (wi, FQ, FQ), (wq, 0, HALF), (wk, 0, HALF), (wv, 0, HALF)
    ):
        dst[:8, first : first + width] = total[:, at : at + width]
        dst[8:, first : first + width] = tail[:, at : at + width]
        at += width
    qb[...] = total[4, n + 4 * HALF :]
    vb[...] = total[5, n + 4 * HALF :]


def decoded(index):
    return (index >> 6, (index >> 4) & 3, (index >> 2) & 3, (index >> 1) & 1), index & 1


def row_of(vector):
    return vector[...].reshape(1, -1)


def order_matrix(place, swap):
    r = lax.broadcasted_iota(jnp.int32, (1, D), 1)
    j = r & 3
    hi = ((r >> 2) & 1) ^ place[0]
    near, far = (r >> 3) & 3, (r >> 5) & 3
    y = (far if swap else near) ^ place[2]
    z = (near if swap else far) ^ place[1]
    block = r >> 7
    core = jnp.where(block >= 3, 1, 0)
    group = block - 3 * core
    core = core ^ place[3]
    source = (((hi * 4 + z) * 4 + y) * 2 + core) * 12 + group * 4 + j
    rows = lax.broadcasted_iota(jnp.int32, (D, D), 0)
    return jnp.where(rows == source, 1.0, 0.0)


def swap_matrix():
    r = lax.broadcasted_iota(jnp.int32, (1, D), 1)
    source = (r & ~0x78) | ((r & 0x18) << 2) | ((r & 0x60) >> 2)
    rows = lax.broadcasted_iota(jnp.int32, (D, D), 0)
    return jnp.where(rows == source, 1.0, 0.0)


def exact(a, b, dims):
    return lax.dot_general(
        a, b, (dims, ((), ())), preferred_element_type=F32, precision=lax.Precision.HIGHEST
    )


def pack_kernel(wq, wk, wv, wo, wi, wt, out):
    at = 0
    for src, first, n in (
        (wq, 0, HALF),
        (wk, 0, HALF),
        (wv, 0, HALF),
        (wo, 0, HALF),
        (wi, 0, FQ),
        (wt, 0, FHALF),
        (wi, FQ, FQ),
    ):
        for g in range(3):
            out[g, :, at : at + n] = src[g * 4 : (g + 1) * 4, first : first + n]
        at += n


def decoded(index):
    return (index >> 6, (index >> 4) & 3, (index >> 2) & 3, (index >> 1) & 1), index & 1


def row_of(vector):
    return vector[...].reshape(1, -1)


def order_matrix(place, swap):
    r = lax.broadcasted_iota(jnp.int32, (1, D), 1)
    j = r & 3
    hi = ((r >> 2) & 1) ^ place[0]
    near, far = (r >> 3) & 3, (r >> 5) & 3
    y = (far if swap else near) ^ place[2]
    z = (near if swap else far) ^ place[1]
    block = r >> 7
    core = jnp.where(block >= 3, 1, 0)
    group = block - 3 * core
    core = core ^ place[3]
    source = (((hi * 4 + z) * 4 + y) * 2 + core) * 12 + group * 4 + j
    rows = lax.broadcasted_iota(jnp.int32, (D, D), 0)
    return jnp.where(rows == source, 1.0, 0.0)


def swap_matrix():
    r = lax.broadcasted_iota(jnp.int32, (1, D), 1)
    source = (r & ~0x78) | ((r & 0x18) << 2) | ((r & 0x60) >> 2)
    rows = lax.broadcasted_iota(jnp.int32, (D, D), 0)
    return jnp.where(rows == source, 1.0, 0.0)


def exact(a, b, dims):
    return lax.dot_general(
        a, b, (dims, ((), ())), preferred_element_type=F32, precision=lax.Precision.HIGHEST
    )


def order_kernel(
    index, x_all, y_all, ob, g1, s1, fb, g2, s2,
    order_a, order_b, swap, xr, xb, yr, vr, x, y, sems,
):
    place, mp = decoded(index[0])
    rows = pl.ds(pl.multiple_of(mp * T, T), T)
    copies = [
        pltpu.make_async_copy(src.at[rows, :], dst, sems.at[i])
        for i, (src, dst) in enumerate(((x_all, x), (y_all, y)))
    ]
    for c in copies:
        c.start()
    m = order_matrix(place, False)
    order_a[...] = m.astype(BF)
    blank = jnp.zeros((5, D), F32)
    vr[0:8, :] = exact(
        jnp.concatenate([row_of(ob), row_of(g1), row_of(s1), blank], axis=0), m, ((1,), (0,))
    )
    m = order_matrix(place, True)
    order_b[...] = m.astype(BF)
    vr[8:16, :] = exact(
        jnp.concatenate([row_of(fb), row_of(g2), row_of(s2), blank], axis=0), m, ((1,), (0,))
    )
    swap[...] = swap_matrix().astype(BF)
    for c in copies:
        c.wait()
    xr[...] = nn(x[...], order_a[...]).astype(BF)
    xb[...] = nn(x[...], order_b[...]).astype(BF)
    yr[...] = nn(y[...], order_b[...]).astype(BF)


def start_weight(pieces, first, width, dst, at, m, sem):
    for core in range(2):
        for i, z in enumerate((0, 1, 3, 2)):
            src = pieces[core * 5 + i + (m if z == 2 else 0)]
            col = first + (0 if z == 2 else m * CH)
            pltpu.make_async_copy(
                src.at[:, :, pl.ds(col, width)],
                dst.at[pl.ds(core * 3, 3), pl.ds(z * 32, 32), pl.ds(at, width)],
                sem,
            ).start()


def wait_weight(dst, at, width, sem):
    part = dst.at[:, :, pl.ds(at, width)]
    pltpu.make_async_copy(part, part, sem).wait()


def weight(w, at, width):
    return w[:, :, pl.ds(at, width)].reshape(D, width)


def row_starts(info, shape, axis):
    index, buckets, lengths = info
    mp = index[0] & 1
    shift = 7 + buckets[0, mp]
    pos = lax.broadcasted_iota(jnp.int32, shape, axis)
    seq = lax.shift_right_logical(pos, shift)
    within = pos & (lax.shift_left(1, shift) - 1)
    n0, n1, n2, n3 = (lengths[0, mp, i] for i in range(4))
    live = jnp.where(seq == 0, n0, jnp.where(seq == 1, n1, jnp.where(seq == 2, n2, n3)))
    return seq, within < live


def mask_bias(info, key_axis):
    kshape = (T, 1) if key_axis == 0 else (1, T)
    qshape = (1, T) if key_axis == 0 else (T, 1)
    kseq, live = row_starts(info, kshape, key_axis)
    qseq, _ = row_starts(info, qshape, 1 - key_axis)
    kseq = jnp.where(live, kseq, -1)
    return jnp.where(kseq == qseq, 0.0, -1e30)


def attention_kernel(
    index, buckets, lengths, xr, qb, vb, others, p0, p1, p2, p3, p4, p5, p6, p7, p8, p9,
    q, k, v, ctx, lse, w_out, w, qkv, biases, mask, lcol, sem, sem2,
):
    pieces = (p0, p1, p2, p3, p4, p5, p6, p7, p8, p9)
    for m in range(2):
        start_weight(pieces, 0, 3 * HALF, w, m * 3 * HALF, m, sem)
    mask[...] = mask_bias((index, buckets, lengths), 1)
    wait_weight(w, 0, 6 * HALF, sem)
    keep = pltpu.make_async_copy(w, w_out, sem2)
    keep.start()
    zero = jnp.zeros((1, HALF), F32)
    for m in range(2):
        for i, own in enumerate((qb, None, vb)):
            if i == 1:
                b = zero
            elif m == 0:
                b = row_of(own)
            else:
                b = others[pl.ds((i >> 1) * HALF, HALF)].reshape(1, HALF)
            biases[m * 3 + i : m * 3 + i + 1, :] = b

    def project(i, _):
        a = nn(xr[...], weight(w, pl.multiple_of(i * HALF, HALF), HALF)) + biases[pl.ds(i, 1), :]
        scale = jnp.where((i == 0) | (i == 3), 0.125, 1.0)
        qkv[i] = (a.astype(BF).astype(F32) * scale).astype(BF)
        return 0

    lax.fori_loop(0, 6, project, 0)
    for i in range(6):
        (q, k, v)[i % 3][:, (i // 3) * HALF : (i // 3 + 1) * HALF] = qkv[i]
    lcol[...] = jnp.zeros_like(lcol)
    lane = lax.broadcasted_iota(jnp.int32, (1, 128), 1)

    def pair(i, _):
        cols = pl.ds(pl.multiple_of(i * 128, 128), 128)
        q2, k2, v2 = q[:, cols], k[:, cols], v[:, cols]
        total = None
        for half in range(2):
            mine = (lane < 64) if half == 0 else (lane >= 64)
            s = nt(jnp.where(mine, q2, BF(0)), k2) + mask[...]
            peak = jnp.max(s, axis=1, keepdims=True)
            e = jnp.exp(s - peak)
            z = jnp.sum(e, axis=1, keepdims=True)
            p = (e * (1.0 / z)).astype(BF)
            c = nn(p, jnp.where(mine, v2, BF(0)))
            total = c if total is None else total + c
            l = peak + jnp.log(z)
            lcol[...] = jnp.where(lane == i * 2 + half, l, lcol[...])
        ctx[:, cols] = total.astype(BF)
        return 0

    lax.fori_loop(0, 6, pair, 0, unroll=3)
    lse[...] = lcol[...].T[0:16, :]
    keep.wait()


def stats(a):
    mean = jnp.mean(a, axis=1, keepdims=True)
    a = a - mean
    r = lax.rsqrt(jnp.mean(a * a, axis=1, keepdims=True) + EPS)
    return a * r, r


def norm_back(dy, n, r, gain):
    a = dy * gain
    return r * (
        a - jnp.mean(a, axis=1, keepdims=True) - n * jnp.mean(a * n, axis=1, keepdims=True)
    )


def store_rows(own, other, value, cols):
    for core, dst in enumerate((own, other)):
        for g in range(3):
            for z in range(4):
                at = ((core * 3 + g) * 4 + z) * 32
                dst[z, g * 32 : (g + 1) * 32, cols] = value[at : at + 32]


def store_vectors(own, other, value):
    for dst in (own, other):
        for z in range(4):
            dst[z, 96:104, :] = value


def unit_source(f):
    return f < 2, (4 * HALF if f < 2 else 2 * FQ), f & 1


def up_kernel(
    ctx, xr, yr, vr, inb, others, order_b, swap,
    a0, a1, a2, a3, a4, a5, a6, a7, a8, a9, b0, b1, b2, b3, b4, b5, b6, b7, b8, b9,
    out, h1t_out, n1_out, r1, df, da, dinb, sums, slope_out, grads_out, grads1_out,
    wo, wi, wt, hs, hts, biases, n1, gact, slope, big, lowt, grads, grads1, sems, keeps, goes,
):
    ap = (a0, a1, a2, a3, a4, a5, a6, a7, a8, a9)
    bp = (b0, b1, b2, b3, b4, b5, b6, b7, b8, b9)
    for m in range(2):
        start_weight(ap, 3 * HALF, HALF, wo, m * HALF, m, sems.at[0])
    for f in range(4):
        first, col, m = unit_source(f)
        start_weight(ap if first else bp, col, FQ, wi, f * FQ, m, sems.at[1 + f])
        start_weight(bp, (f >> 1) * FQ, FQ, wt, f * FQ, m, sems.at[5 + f])
    wait_weight(wo, 0, D, sems.at[0])
    ob, g1, s1 = (vr[i : i + 1, :] for i in range(3))
    fb, g2, s2 = (vr[i : i + 1, :] for i in range(8, 11))
    nrm, r = stats(nt(ctx[...], weight(wo, 0, D)) + ob + xr[...].astype(F32))
    n1[...] = nrm
    keep = []

    def send(src, dst, sem):
        keep.append(pltpu.make_async_copy(src, dst, sem))
        keep[-1].start()

    send(n1, n1_out, keeps.at[2])
    r1[...] = jnp.broadcast_to(r, (T, 128))
    low = nrm * g1 + s1
    hs[0] = low.astype(BF)
    hts[0] = low.T.astype(BF)
    send(hts.at[0], h1t_out, keeps.at[3])
    low = nn(hs[0], swap[...])
    hs[1] = low.astype(BF)
    hts[1] = low.T.astype(BF)
    big[...] = hs[1].astype(F32) + fb
    for f in range(4):
        bias, at = (inb, 0) if f & 1 == 0 else (others, D)
        biases[f : f + 1, :] = bias[pl.ds(at + (f >> 1) * FQ, FQ)].reshape(1, FQ)

    def up(f, _):
        at = pl.multiple_of(f * FQ, FQ)
        wait_weight(wi, at, FQ, sems.at[1 + f])
        u = nn(hs[f >> 1], weight(wi, at, FQ)) + biases[pl.ds(f, 1), :]
        phi = 0.5 + 0.5 * lax.erf(u * INV_SQRT2)
        slope[f] = phi + u * (jnp.exp(-0.5 * u * u) * INV_SQRT2PI)

        @pl.when(f < 2)
        def _():
            pltpu.make_async_copy(slope.at[f], slope_out.at[f], keeps.at[f]).start()

        g = (u * phi).astype(BF)
        gact[:, pl.ds(at, FQ)] = g
        wait_weight(wt, at, FQ, sems.at[5 + f])
        big[...] += nt(g, weight(wt, at, FQ))
        return 0

    lax.fori_loop(0, 4, up, 0)
    keep += [pltpu.make_async_copy(slope.at[f], slope_out.at[f], keeps.at[f]) for f in range(2)]
    n2, r2 = stats(big[...])
    low = (n2 * g2 + s2).astype(BF)
    out[...] = nt(low, order_b[...]).astype(BF)
    y = yr[...].astype(F32)
    sums[1:2, :] = jnp.sum(y * n2, axis=0, keepdims=True)
    sums[2:3, :] = jnp.sum(y, axis=0, keepdims=True)
    d = norm_back(y, n2, r2, g2)
    big[...] = d
    low = d.astype(BF)
    df[...] = low
    sums[0:1, :] = jnp.sum(low.astype(F32), axis=0, keepdims=True)
    sums[3:8, :] = jnp.zeros((5, D), F32)
    lowt[...] = d.T.astype(BF)

    def go(first, width, sem):
        for k, (src, dst) in enumerate(((grads, grads_out), (grads1, grads1_out))):
            cols = pl.ds(first, width)
            yield pltpu.make_async_copy(src.at[:, :, cols], dst.at[:, :, cols], sem(k))

    def outer(f, _):
        g = nn(lowt[...], gact[:, pl.ds(pl.multiple_of(f * FQ, FQ), FQ)]).astype(BF)
        at = pl.multiple_of((f & 1) * CH + (f >> 1) * FQ, FQ)
        store_rows(grads, grads1, g, pl.ds(at, FQ))

        @pl.when(f >= 2)
        def _():
            for c in go(pl.multiple_of((f & 1) * CH, CH), FHALF, lambda k: goes.at[k, f & 1]):
                c.start()

        return 0

    lax.fori_loop(0, 4, outer, 0)

    def inner(m, _):
        f = m + 2
        at = pl.multiple_of(f * FQ, FQ)
        du = (nn(df[...], weight(wt, at, FQ)) * slope[f]).astype(BF)
        dinb[:, pl.ds(pl.multiple_of(m * FQ, FQ), FQ)] = jnp.sum(
            du.astype(F32), axis=0, keepdims=True
        )
        big[...] += nt(du, weight(wi, at, FQ))
        g = nn(hts[1], du).astype(BF)
        to = pl.multiple_of(m * CH + FHALF, FQ)
        store_rows(grads, grads1, g, pl.ds(to, FQ))
        for c in go(to, FQ, lambda k: goes.at[2 + k, m]):
            c.start()
        return 0

    lax.fori_loop(0, 2, inner, 0)
    for m in range(2):
        keep += list(go(m * CH, FHALF, lambda k, m=m: goes.at[k, m]))
        keep += list(go(m * CH + FHALF, FQ, lambda k, m=m: goes.at[2 + k, m]))
    d = big[...]
    hi = d.astype(BF)
    lo = (d - hi.astype(F32)).astype(BF)
    da[...] = nt(hi, swap[...]) + nt(lo, swap[...])
    for k in keep:
        k.wait()


def down_units(df, wi, wt, slope, big, h1t, dinb, grads, grads1, sems, keeps, slope_in):
    def down(f, _):
        at = pl.multiple_of(f * FQ, FQ)
        wait_weight(wt, at, FQ, sems.at[2 * f])
        pltpu.make_async_copy(slope_in.at[f], slope.at[f], keeps.at[f]).wait()
        du = (nn(df[...], weight(wt, at, FQ)) * slope[f]).astype(BF)
        dinb[pl.ds(f, 1), :] = jnp.sum(du.astype(F32), axis=0, keepdims=True)
        wait_weight(wi, at, FQ, sems.at[2 * f + 1])
        big[...] += nt(du, weight(wi, at, FQ))
        g = nn(h1t[...], du).astype(BF)
        store_rows(grads, grads1, g, pl.ds(pl.multiple_of(f * CQ + HALF, HALF), FQ))
        return 0

    lax.fori_loop(0, 2, down, 0)


def start_units(units, ap, bp, wi, wt, slope_in, slope, sems, keeps):
    for i, f in enumerate(units):
        first, col, m = unit_source(f)
        start_weight(bp, (f >> 1) * FQ, FQ, wt, i * FQ, m, sems.at[2 * i])
        pltpu.make_async_copy(slope_in.at[f], slope.at[i], keeps.at[i]).start()
        start_weight(ap if first else bp, col, FQ, wi, i * FQ, m, sems.at[2 * i + 1])


def down_kernel1(
    h1t, r1, df, dinb, sums, vr, ctx_all, n1_all, da_in, order_a_all, order_b_all, slope_in,
    a0, a1, a2, a3, a4, a5, a6, a7, a8, a9, b0, b1, b2, b3, b4, b5, b6, b7, b8, b9,
    dc, dr, grads, grads1,
    wo, wi, wt, slope, big, lowt, inner, ctx, n1, order_a, order_b, sems, keeps, loads,
):
    ap = (a0, a1, a2, a3, a4, a5, a6, a7, a8, a9)
    bp = (b0, b1, b2, b3, b4, b5, b6, b7, b8, b9)
    start_units((0, 1), ap, bp, wi, wt, slope_in, slope, sems, keeps)
    for m in range(2):
        start_weight(ap, 3 * HALF, HALF, wo, m * HALF, m, sems.at[4])
    copies = [
        pltpu.make_async_copy(src, dst, loads.at[i])
        for i, (src, dst) in enumerate(
            (
                (da_in, big),
                (n1_all, n1),
                (ctx_all, ctx),
                (order_a_all, order_a),
                (order_b_all, order_b),
            )
        )
    ]
    for c in copies:
        c.start()
    copies[0].wait()
    down_units(df, wi, wt, slope, big, h1t, inner, grads, grads1, sems, keeps, slope_in)
    for c in copies[1:]:
        c.wait()
    dh = big[...]
    nrm = n1[...]
    g1 = vr[1:2, :]
    dg1 = jnp.sum(dh * nrm, axis=0, keepdims=True)
    ds1 = jnp.sum(dh, axis=0, keepdims=True)
    d = norm_back(dh, nrm, r1[:, 0:1], g1)
    dr[...] = d
    da = d.astype(BF)
    dob = jnp.sum(da.astype(F32), axis=0, keepdims=True)
    wait_weight(wo, 0, D, sems.at[4])
    dc[...] = nn(da, weight(wo, 0, D)).astype(BF)
    lowt[...] = d.T.astype(BF)
    g = nn(lowt[...], ctx[...]).astype(BF)
    for m in range(2):
        store_rows(grads, grads1, g[:, m * HALF : (m + 1) * HALF], pl.ds(m * CQ, HALF))
    sa = exact(
        jnp.concatenate([dob, dg1, ds1, dob, dob, dob, dob, dob], axis=0),
        order_a[...].astype(F32),
        ((1,), (1,)),
    )
    sb = exact(sums[...], order_b[...].astype(F32), ((1,), (1,)))
    sides = []
    for m in range(2):
        line = jnp.concatenate(
            [inner[m : m + 1, :], dinb[:, m * FQ : (m + 1) * FQ]]
            + [sa[i : i + 1] for i in range(3)]
            + [sb[i : i + 1] for i in range(3)]
            + [jnp.zeros((1, 6 * CQ - 8 * FQ), F32)],
            axis=1,
        )
        rows = [line[:, i * CQ : (i + 1) * CQ] for i in range(6)]
        sides.append(jnp.concatenate(rows + [jnp.zeros((2, CQ), F32)], axis=0))
    store_vectors(grads, grads1, jnp.concatenate(sides, axis=1).astype(BF))


def back_half(
    m, index, buckets, lengths, q, k, v, dc, lse, xb_all, w_all, dr,
    grads, grads1, mask, dqkv, big, qb, vb, xt_ref, w, xb, sems,
):
    copies = [
        pltpu.make_async_copy(w_all.at[:, :, pl.ds(m * 3 * HALF, 3 * HALF)], w, sems.at[0]),
        pltpu.make_async_copy(xb_all, xb, sems.at[1]),
        pltpu.make_async_copy(dr, big, sems.at[2]),
    ]
    for c in copies:
        c.start()
    mask[...] = mask_bias((index, buckets, lengths), 0)
    lane = lax.broadcasted_iota(jnp.int32, (1, 128), 1)

    def pair(i, _):
        head = pl.ds(pl.multiple_of(m * HALF + i * 128, 128), 128)
        cols = pl.ds(pl.multiple_of(i * 128, 128), 128)
        q2, k2, v2, c2 = q[:, head], k[:, head], v[:, head], dc[:, head]
        k2t = k2.astype(F32).T.astype(BF)
        outs = []
        for half in range(2):
            mine = (lane < 64) if half == 0 else (lane >= 64)
            s = nt(jnp.where(mine, k2, BF(0)), q2) + mask[...]
            p = jnp.exp(s - lse[pl.ds(m * 6 + i * 2 + half, 1), :])
            dp = nt(jnp.where(mine, v2, BF(0)), c2)
            delta = jnp.sum(dp * p, axis=0, keepdims=True)
            ds = (p * (dp - delta)).astype(BF)
            outs.append((nn(k2t, ds), nn(ds, q2), nn(p.astype(BF), c2)))
        first = lane < 64
        (qa, ka, va), (qz, kz, vz) = outs
        dq2 = jnp.concatenate([qa[:64], qz[64:]], axis=0).T
        dk2, dv2 = jnp.where(first, ka, kz), jnp.where(first, va, vz)
        dq2 = (dq2 * 0.125).astype(BF)
        dk2 = dk2.astype(BF)
        dv2 = dv2.astype(BF)
        dqkv[0, :, cols] = dq2
        dqkv[1, :, cols] = dk2
        dqkv[2, :, cols] = dv2
        qb[:, cols] = jnp.sum(dq2.astype(F32), axis=0, keepdims=True)
        vb[:, cols] = jnp.sum(dv2.astype(F32), axis=0, keepdims=True)
        return 0

    lax.fori_loop(0, 3, pair, 0, unroll=3)
    for c in copies:
        c.wait()
    xt_ref[...] = xb[...].astype(F32).T.astype(BF)

    def weights(i, _):
        to = pl.multiple_of(i * HALF, HALF)
        a = dqkv[i]
        store_rows(grads, grads1, nn(xt_ref[...], a).astype(BF), pl.ds(to, HALF))
        big[...] += nt(a, weight(w, to, HALF))
        return 0

    lax.fori_loop(0, 3, weights, 0)
    line = jnp.concatenate([qb[...], vb[...], jnp.zeros((1, HALF), F32)], axis=1)
    line = jnp.concatenate([line, jnp.zeros((7, CQ), F32)], axis=0)
    store_vectors(grads, grads1, line.astype(BF))


def back_kernel0(
    index, buckets, lengths, q, k, v, dc, lse, xb, w, dr,
    grads, grads1, out, mask, dqkv, *scratch,
):
    ins = (index, buckets, lengths, q, k, v, dc, lse, xb, w, dr)
    big = scratch[0]
    back_half(0, *ins, grads, grads1, mask, dqkv, *scratch)
    out[...] = big[...]


def back_kernel1(
    index, buckets, lengths, q, k, v, dc, lse, xb, w, dr,
    grads, grads1, gin, mask, dqkv, *scratch,
):
    ins = (index, buckets, lengths, q, k, v, dc, lse, xb, w, dr)
    big = scratch[0]
    back_half(1, *ins, grads, grads1, mask, dqkv, *scratch)
    gin[...] = big[...].astype(BF)


def last_kernel(gin, order, out):
    out[...] = nt(gin[...], order[...]).astype(BF)


def call(kernel, outs, args, scratch=(), vmem=48, flops=0, smem=0, hbm=(), anyouts=()):
    specs = []
    for i in range(len(args)):
        if i < smem:
            specs.append(pl.BlockSpec(memory_space=pltpu.SMEM))
        elif i in hbm:
            specs.append(pl.BlockSpec(memory_space=pl.ANY))
        else:
            specs.append(pl.BlockSpec(memory_space=VMEM))
    return pl.pallas_call(
        kernel,
        out_shape=[jax.ShapeDtypeStruct(s, d) for s, d in outs],
        in_specs=specs,
        out_specs=[
            pl.BlockSpec(memory_space=pl.ANY if i in anyouts else VMEM) for i in range(len(outs))
        ],
        scratch_shapes=list(scratch),
        compiler_params=pltpu.CompilerParams(vmem_limit_bytes=vmem * 2**20),
        cost_estimate=pl.CostEstimate(flops=flops // 1000, bytes_accessed=1000, transcendentals=0),
    )(*args)


def body(
    hidden_in, buckets, lengths, query_weight, key_weight, value_weight, query_bias, value_bias,
    output_weight, output_bias, first_gain, first_shift, inner_weight, inner_bias, outer_weight,
    outer_bias, second_gain, second_shift, cotangent,
):
    mp = lax.axis_index("mp")
    index = lax.axis_index((*DP, "mp")).astype(jnp.int32).reshape(1)
    info = (index, buckets, lengths)
    (shard,) = call(
        pack_kernel,
        [((3, 4, 2 * CH), BF)],
        (query_weight, key_weight, value_weight, output_weight.T, inner_weight, outer_weight.T),
        vmem=60,
    )
    biases = jnp.concatenate([query_bias, value_bias, inner_bias])
    others = flip(biases, "mp", 1)
    def sides(mine, other):
        return jnp.where(
            mp == 0, jnp.concatenate([mine, other], axis=0), jnp.concatenate([other, mine], axis=0)
        )

    square = ((D, D), BF)
    tokens = ((T, D), BF)
    order_a, order_b, swap, xr, xb, yr, vr = call(
        order_kernel,
        [square, square, square, tokens, tokens, tokens, ((16, D), F32)],
        (
            index,
            hidden_in,
            cotangent,
            output_bias,
            first_gain,
            first_shift,
            outer_bias,
            second_gain,
            second_shift,
        ),
        [VMEM((T, D), BF), VMEM((T, D), BF), pltpu.SemaphoreType.DMA((2,))],
        smem=1,
        hbm=(1, 2),
        vmem=60,
        flops=2 * 10**9,
    )
    pa, pb, (xr, xb, yr, others) = gather(shard, (xr, xb, yr, others))
    pa = with_other_core(pa)
    q, k, v, ctx, lse, w = call(
        attention_kernel,
        [tokens, tokens, tokens, tokens, ((16, T), F32), ((6, 128, 6 * HALF), BF)],
        (*info, xr, query_bias, value_bias, others, *pa),
        [
            VMEM((6, 128, 6 * HALF), BF),
            VMEM((6, T, HALF), BF),
            VMEM((8, HALF), F32),
            VMEM((T, T), F32),
            VMEM((T, 128), F32),
            pltpu.SemaphoreType.DMA(()),
            pltpu.SemaphoreType.DMA(()),
        ],
        smem=3,
        hbm=range(7, 17),
        anyouts=(5,),
        vmem=60,
        flops=10 * 10**9,
    )
    ctx, pb[3], pb[4] = lax.optimization_barrier((ctx, pb[3], pb[4]))
    pb = with_other_core(pb)
    gb, ga = ((4, 96, 2 * CH), BF), ((4, 104, 2 * CQ), BF)
    wide = ((T, D), F32)
    out, h1t, n1, r1, df, da, dinb, sums, slope, grads_b, grads_b1 = call(
        up_kernel,
        [
            tokens,
            ((D, T), BF),
            wide,
            ((T, 128), F32),
            tokens,
            wide,
            ((1, 2 * FQ), F32),
            ((8, D), F32),
            ((2, T, FQ), F32),
            gb,
            gb,
        ],
        (ctx, xr, yr, vr, inner_bias, others, order_b, swap, *pa, *pb),
        [
            VMEM((6, 128, D), BF),
            VMEM((6, 128, FF), BF),
            VMEM((6, 128, FF), BF),
            VMEM((2, T, D), BF),
            VMEM((2, D, T), BF),
            VMEM((8, FQ), F32),
            VMEM((T, D), F32),
            VMEM((T, FF), BF),
            VMEM((4, T, FQ), F32),
            VMEM((T, D), F32),
            VMEM((D, T), BF),
            VMEM(*gb),
            VMEM(*gb),
            pltpu.SemaphoreType.DMA((9,)),
            pltpu.SemaphoreType.DMA((4,)),
            pltpu.SemaphoreType.DMA((4, 2)),
        ],
        hbm=range(8, 28),
        anyouts=(1, 2, 8, 9, 10),
        vmem=56,
        flops=8 * 10**9,
    )
    grads_b1 = flip(grads_b1, AC, 1)
    out_own, out = out, flip(out, "mp", 1)
    half = [VMEM((6, 128, 2 * FQ), BF)] * 2 + [VMEM((2, T, FQ), F32), VMEM((T, D), F32)]
    dc, dr, grads_a, grads_a1 = call(
        down_kernel1,
        [tokens, wide, ga, ga],
        (h1t, r1, df, dinb, sums, vr, ctx, n1, da, order_a, order_b, slope, *pa, *pb),
        [VMEM((6, 128, D), BF)]
        + half
        + [
            VMEM((D, T), BF),
            VMEM((8, FQ), F32),
            VMEM((T, D), BF),
            VMEM((T, D), F32),
            VMEM((D, D), BF),
            VMEM((D, D), BF),
            pltpu.SemaphoreType.DMA((5,)),
            pltpu.SemaphoreType.DMA((2,)),
            pltpu.SemaphoreType.DMA((5,)),
        ],
        hbm=range(6, 32),
        vmem=60,
        flops=4 * 10**9,
    )
    b0, b1, b3, bl, br = core_sums([(grads_b, grads_b1)], 96)
    grads_a1 = flip(grads_a1, AC, 1)
    b0, grads_a1 = lax.optimization_barrier((b0, grads_a1))
    a0, a1, a3, al, ar = core_sums([(grads_a, grads_a1)], 104)
    dc, b0, b1, b3, bl, br, a0, a1, a3, al, ar = lax.optimization_barrier(
        (dc, b0, b1, b3, bl, br, a0, a1, a3, al, ar)
    )
    bl, br = flip(bl, AY, 1), flip(br, AY, 3)
    al, ar = flip(al, AZ, 1), flip(ar, AZ, 3)
    gq = ((4, 104, CQ), BF)
    scratch = [
        VMEM((T, T), F32),
        VMEM((3, T, HALF), BF),
        VMEM((T, D), F32),
        VMEM((1, HALF), F32),
        VMEM((1, HALF), F32),
        VMEM((D, T), BF),
        VMEM((6, 128, 3 * HALF), BF),
        VMEM((T, D), BF),
        pltpu.SemaphoreType.DMA((3,)),
    ]
    q00, q01, big = call(
        back_kernel0,
        [gq, gq, wide],
        (*info, q, k, v, dc, lse, xb, w, dr),
        scratch,
        smem=3,
        hbm=(8, 9, 10),
        vmem=34,
        flops=7 * 10**9,
    )
    b1, b3 = relayed((2 * CH,), b1, b3, bl, br)
    a1, a3 = relayed((2 * CQ,), a1, a3, al, ar)
    big, b1, b3, a1, a3, out = lax.optimization_barrier((big, b1, b3, a1, a3, out))
    b1, b3 = flip(b1, AY, 1), flip(b3, AY, 3)
    a1, a3 = flip(a1, AZ, 1), flip(a3, AZ, 3)
    q10, q11, gin = call(
        back_kernel1,
        [gq, gq, tokens],
        (*info, q, k, v, dc, lse, xb, w, big),
        scratch,
        smem=3,
        hbm=(8, 9, 10),
        vmem=34,
        flops=7 * 10**9,
    )
    q01, q11, b1, b3, a1, a3 = lax.optimization_barrier((q01, q11, b1, b3, a1, a3))
    q01, q11 = flip(q01, AC, 1), flip(q11, AC, 1)
    whole, part = ((104, 2 * CQ), BF), ((104, CQ), BF)
    q0, q1, q3, left, right = call(
        pair_kernel, [whole, whole, whole, part, part], (q00, q01, q10, q11), vmem=24
    )
    left, right = flip(left, AY, 1), flip(right, AY, 3)
    q1, q3 = relayed((2 * CQ,), q1, q3, left, right)
    q1, q3 = flip(q1, AY, 1), flip(q3, AY, 3)
    (gin,) = call(last_kernel, [tokens], (gin, order_a), vmem=16)
    theirs = flip(gin, "mp", 1)
    q0, q1, q3, theirs = lax.optimization_barrier((q0, q1, q3, theirs))
    fa = sent(call(second_kernel, [((32, 2 * CQ), BF)] * 4, (a0, a1, a3), vmem=24), AY)
    fa = sent(call(third_kernel, [((20, CQ), BF)] * 4, fa, vmem=24), AX)
    (blocks,) = call(
        last_sums_kernel,
        [((16, 8, 14 * HALF), BF)],
        (index, b0, b1, b3, q0, q1, q3),
        smem=1,
        vmem=32,
    )
    blocks = exchanged(blocks, (*AX, AZ))
    small, inner, vector = ((12, HALF), F32), ((12, FHALF), F32), ((D,), F32)
    half = ((HALF,), F32)
    wq, wk, wv, wo, wi, wt, qb, vb, ib, *vecs = call(
        final_kernel,
        [small] * 4 + [inner] * 2 + [half] * 2 + [((FHALF,), F32)] + [vector] * 6,
        (*fa, blocks),
        vmem=24,
    )
    layer_out = sides(out_own, out)
    input_grad = sides(gin, theirs).astype(F32)
    dob, dg1, ds1, dfb, dg2, ds2 = vecs
    return (
        layer_out, input_grad, wq, wk, wv, qb, vb, wo.T, dob, dg1, ds1, wi, ib, wt.T, dfb, dg2, ds2
    )


def solution(mesh):
    torus = Mesh(
        mesh.devices.reshape(2, 4, 4, 2, mesh.shape["mp"]), ("dp_0", "dp_1", "dp_2", "dp_3", "mp")
    )
    row, col, half = P(DP, "mp"), P("mp", DP), P("mp")
    in_specs = (
        P(DP, None), P(DP, None), P(DP, None, None), row, row, row, half, half, col, P(), P(), P(),
        row, half, col, P(), P(), P(), P(DP, None),
    )
    out_specs = (
        P(DP, None), P(DP, None), row, row, row, half, half, col, P(), P(), P(), row, half, col,
        P(), P(), P(),
    )
    return jax.shard_map(body, mesh=torus, in_specs=in_specs, out_specs=out_specs, check_vma=False)
```

```python
import functools

import jax
import jax.numpy as jnp
from jax import lax
from jax.experimental import pallas as pl
from jax.experimental.pallas import tpu as pltpu
from jax.sharding import Mesh
from jax.sharding import PartitionSpec as P

DP = ("dp_0", "dp_1", "dp_2", "dp_3")
AX = ("dp_0", "mp")
AZ, AY, AC = "dp_1", "dp_2", "dp_3"
D = 768
T = 512
DH = 64
FF = 3072
HALF = 384
FHALF = 1536
FQ = 768
CH = 2304
CQ = 1152
CA = 1920
EPS = 1e-12
BF = jnp.bfloat16
F32 = jnp.float32
VMEM = pltpu.VMEM
INV_SQRT2 = 0.7071067811865476
INV_SQRT2PI = 0.3989422804014327


def nn(a, b):
    return lax.dot_general(a, b, (((1,), (0,)), ((), ())), preferred_element_type=F32)


def nt(a, b):
    return lax.dot_general(a, b, (((1,), (1,)), ((), ())), preferred_element_type=F32)


def tn(a, b):
    return lax.dot_general(a, b, (((0,), (0,)), ((), ())), preferred_element_type=F32)


def flip(a, axis, s):
    n = 4 if axis in (AX, AY, AZ) else 2
    return lax.ppermute(a, axis, [(i, i ^ s) for i in range(n)])


def joined(a, axis):
    return jnp.concatenate([a] + [flip(a, axis, s) for s in (1, 2, 3)], axis=1)


def gather(shard, ready):
    a = shard
    p1, p2, p3 = (flip(a, AX, s) for s in (1, 2, 3))
    parts = []
    for first in (0, CH):
        cols = slice(first, first + CH)
        a0, a1, a2, a3 = (p[:, :, cols] for p in (a, p1, p2, p3))
        parts.append(
            jnp.concatenate(
                [jnp.concatenate([a0, a2], axis=1), jnp.concatenate([a1, a3], axis=1)], axis=2
            )
        )
    parts = lax.optimization_barrier((joined(parts[0], AY), joined(parts[1], AZ)))
    near = [[flip(b, axis, s) for s in (1, 3)] for b, axis in zip(parts, (AZ, AY))]
    near, ready = lax.optimization_barrier((near, ready))
    out = []
    for b, axis, (n1, n3) in zip(parts, (AZ, AY), near):
        far = [flip(n1[:, :, :CH], axis, 3), flip(n3[:, :, CH:], axis, 1)]
        out.append([b, n1, n3, *far])
    return *out, ready


def with_other_core(own):
    return own + [flip(o, AC, 1) for o in own]


def add(*parts):
    total = parts[0].astype(F32)
    for p in parts[1:]:
        total = total + p.astype(F32)
    return total


def low_sum(*parts):
    return add(*parts).astype(BF)


def core_kernel(*refs):
    c0, c1, c3, left, right = refs[-5:]
    pairs = [refs[i : i + 2] for i in range(0, len(refs) - 5, 2)]
    at = 0
    for own, other in pairs:
        rows, n = own.shape[1:]
        for s, dst in ((0, c0), (1, c1), (3, c3), (2, None)):
            total = low_sum(own[s], other[s])
            if s == 2:
                left[:rows, at // 2 : (at + n) // 2] = total[:, : n // 2]
                right[:rows, at // 2 : (at + n) // 2] = total[:, n // 2 :]
                dsts = (left, right)
            else:
                dst[:rows, at : at + n] = total
                dsts = (dst,)
            for d in dsts:
                if rows < d.shape[0]:
                    lo, hi = (at // 2, (at + n) // 2) if s == 2 else (at, at + n)
                    d[rows:, lo:hi] = jnp.zeros((d.shape[0] - rows, hi - lo), BF)
        at += n


def core_sums(pairs, rows):
    n = sum(own.shape[2] for own, _ in pairs)
    whole, half = ((rows, n), BF), ((rows, n // 2), BF)
    return call(
        core_kernel, [whole, whole, whole, half, half], [a for p in pairs for a in p], vmem=32
    )


def relay_kernel(widths, c1, c3, left, right, out1, out3):
    at = 0
    for n in widths:
        h = n // 2
        part = slice(at // 2, at // 2 + h)
        out3[:, at : at + h] = low_sum(c3[:, at : at + h], left[:, part])
        out3[:, at + h : at + n] = c3[:, at + h : at + n]
        out1[:, at : at + h] = c1[:, at : at + h]
        out1[:, at + h : at + n] = low_sum(c1[:, at + h : at + n], right[:, part])
        at += n


def relayed(widths, c1, c3, left, right):
    whole = (c1.shape, BF)
    return call(
        functools.partial(relay_kernel, widths), [whole, whole], (c1, c3, left, right), vmem=24
    )


def pair_kernel(a, a1, b, b1, c0, c1, c3, left, right):
    n = a.shape[2]
    for s, dst in ((0, c0), (1, c1), (3, c3)):
        dst[:, :n] = low_sum(a[s], a1[s])
        dst[:, n:] = low_sum(b[s], b1[s])
    left[...] = low_sum(a[2], a1[2])
    right[...] = low_sum(b[2], b1[2])


def sent(parts, axis):
    return [parts[0]] + [flip(parts[s], axis, s) for s in (1, 2, 3)]


def second_kernel(a0, a1, a3, *outs):
    total = add(a0[...], a1[...], a3[...]).astype(BF)
    for y in range(4):
        for g in range(3):
            at = g * 32 + y * 8
            outs[y][g * 8 : (g + 1) * 8, :] = total[at : at + 8]
        outs[y][24:, :] = total[96:]


def third_kernel(m0, m1, m2, m3, *outs):
    total = add(m0[...], m1[...], m2[...], m3[...])
    for m in range(2):
        part = total[:, m * CQ : (m + 1) * CQ]
        for hi in range(2):
            rows = [part[g * 8 + hi * 4 : g * 8 + hi * 4 + 4] for g in range(3)]
            rows = jnp.concatenate(rows + [part[24:]], axis=0)
            outs[hi * 2 + m][...] = rows.astype(BF)


def last_sums_kernel(index, b0, b1, b3, q0, q1, q3, out):
    (hi0, z0, _, _), m0 = decoded(index[0])
    outer = add(b0[...], b1[...], b3[...])
    attn = add(q0[...], q1[...], q3[...])
    blank = jnp.zeros((2, HALF), F32)
    for m in range(2):
        part = jnp.concatenate(
            [outer[:, m * CH : (m + 1) * CH], attn[:96, m * CQ : (m + 1) * CQ]], axis=1
        )
        n = CH + CQ
        vec = [attn[96:97, m * CQ + i * HALF : m * CQ + (i + 1) * HALF] for i in range(2)]
        vec = jnp.concatenate(vec + [blank], axis=0)
        for z in range(4):
            for hi in range(2):
                r0, r1, r2 = (
                    part[g * 32 + z * 8 + hi * 4 : g * 32 + z * 8 + hi * 4 + 4] for g in range(3)
                )
                block = jnp.concatenate(
                    [
                        jnp.concatenate([r0, r2[:, : 5 * HALF]], axis=1),
                        jnp.concatenate([r1, r2[:, 5 * HALF :], vec], axis=1),
                    ],
                    axis=0,
                )
                out[((hi ^ hi0) * 2 + (m ^ m0)) * 4 + (z ^ z0)] = block.astype(BF)


def exchanged(blocks, axes):
    return lax.all_to_all(blocks, axes, 0, 0, tiled=True)


def total_of(blocks):
    total = blocks[0].astype(F32)
    for i in range(1, blocks.shape[0]):
        total = total + blocks[i].astype(F32)
    return total


def final_kernel(n0, n1, n2, n3, blocks, wq, wk, wv, wo, wi, wt, qb, vb, ib, ob, g1, s1, fb, g2, s2):
    total = add(n0[...], n1[...], n2[...], n3[...])
    wo[...] = total[:12, :HALF]
    wi[:, :FQ] = total[:12, HALF:]
    vec = jnp.concatenate([total[12 + i : 13 + i, :CQ] for i in range(6)], axis=1)
    at = 0
    for dst in (ib, ob, g1, s1, fb, g2, s2):
        dst[...] = vec[0, at : at + dst.shape[0]]
        at += dst.shape[0]
    total = total_of(blocks)
    n = CH + CQ
    tail = jnp.concatenate([total[:4, n:], total[4:, n : n + 4 * HALF]], axis=1)
    at = 0
    for dst, first, width in (
        (wt, 0, FHALF), (wi, FQ, FQ), (wq, 0, HALF), (wk, 0, HALF), (wv, 0, HALF)
    ):
        dst[:8, first : first + width] = total[:, at : at + width]
        dst[8:, first : first + width] = tail[:, at : at + width]
        at += width
    qb[...] = total[4, n + 4 * HALF :]
    vb[...] = total[5, n + 4 * HALF :]


def decoded(index):
    return (index >> 6, (index >> 4) & 3, (index >> 2) & 3, (index >> 1) & 1), index & 1


def row_of(vector):
    return vector[...].reshape(1, -1)


def order_matrix(place, swap):
    r = lax.broadcasted_iota(jnp.int32, (1, D), 1)
    j = r & 3
    hi = ((r >> 2) & 1) ^ place[0]
    near, far = (r >> 3) & 3, (r >> 5) & 3
    y = (far if swap else near) ^ place[2]
    z = (near if swap else far) ^ place[1]
    block = r >> 7
    core = jnp.where(block >= 3, 1, 0)
    group = block - 3 * core
    core = core ^ place[3]
    source = (((hi * 4 + z) * 4 + y) * 2 + core) * 12 + group * 4 + j
    rows = lax.broadcasted_iota(jnp.int32, (D, D), 0)
    return jnp.where(rows == source, 1.0, 0.0)


def swap_matrix():
    r = lax.broadcasted_iota(jnp.int32, (1, D), 1)
    source = (r & ~0x78) | ((r & 0x18) << 2) | ((r & 0x60) >> 2)
    rows = lax.broadcasted_iota(jnp.int32, (D, D), 0)
    return jnp.where(rows == source, 1.0, 0.0)


def exact(a, b, dims):
    return lax.dot_general(
        a, b, (dims, ((), ())), preferred_element_type=F32, precision=lax.Precision.HIGHEST
    )


def pack_kernel(wq, wk, wv, wo, wi, wt, out):
    at = 0
    for src, first, n in (
        (wq, 0, HALF),
        (wk, 0, HALF),
        (wv, 0, HALF),
        (wo, 0, HALF),
        (wi, 0, FQ),
        (wt, 0, FHALF),
        (wi, FQ, FQ),
    ):
        for g in range(3):
            out[g, :, at : at + n] = src[g * 4 : (g + 1) * 4, first : first + n]
        at += n


def decoded(index):
    return (index >> 6, (index >> 4) & 3, (index >> 2) & 3, (index >> 1) & 1), index & 1


def row_of(vector):
    return vector[...].reshape(1, -1)


def order_matrix(place, swap):
    r = lax.broadcasted_iota(jnp.int32, (1, D), 1)
    j = r & 3
    hi = ((r >> 2) & 1) ^ place[0]
    near, far = (r >> 3) & 3, (r >> 5) & 3
    y = (far if swap else near) ^ place[2]
    z = (near if swap else far) ^ place[1]
    block = r >> 7
    core = jnp.where(block >= 3, 1, 0)
    group = block - 3 * core
    core = core ^ place[3]
    source = (((hi * 4 + z) * 4 + y) * 2 + core) * 12 + group * 4 + j
    rows = lax.broadcasted_iota(jnp.int32, (D, D), 0)
    return jnp.where(rows == source, 1.0, 0.0)


def swap_matrix():
    r = lax.broadcasted_iota(jnp.int32, (1, D), 1)
    source = (r & ~0x78) | ((r & 0x18) << 2) | ((r & 0x60) >> 2)
    rows = lax.broadcasted_iota(jnp.int32, (D, D), 0)
    return jnp.where(rows == source, 1.0, 0.0)


def exact(a, b, dims):
    return lax.dot_general(
        a, b, (dims, ((), ())), preferred_element_type=F32, precision=lax.Precision.HIGHEST
    )


def order_kernel(
    index, x_all, y_all, ob, g1, s1, fb, g2, s2,
    order_a, order_b, swap, xr, xb, yr, vr, x, y, sems,
):
    place, mp = decoded(index[0])
    rows = pl.ds(pl.multiple_of(mp * T, T), T)
    copies = [
        pltpu.make_async_copy(src.at[rows, :], dst, sems.at[i])
        for i, (src, dst) in enumerate(((x_all, x), (y_all, y)))
    ]
    for c in copies:
        c.start()
    m = order_matrix(place, False)
    order_a[...] = m.astype(BF)
    blank = jnp.zeros((5, D), F32)
    vr[0:8, :] = exact(
        jnp.concatenate([row_of(ob), row_of(g1), row_of(s1), blank], axis=0), m, ((1,), (0,))
    )
    m = order_matrix(place, True)
    order_b[...] = m.astype(BF)
    vr[8:16, :] = exact(
        jnp.concatenate([row_of(fb), row_of(g2), row_of(s2), blank], axis=0), m, ((1,), (0,))
    )
    swap[...] = swap_matrix().astype(BF)
    for c in copies:
        c.wait()
    xr[...] = nn(x[...], order_a[...]).astype(BF)
    xb[...] = nn(x[...], order_b[...]).astype(BF)
    yr[...] = nn(y[...], order_b[...]).astype(BF)


def start_weight(pieces, first, width, dst, at, m, sem):
    for core in range(2):
        for i, z in enumerate((0, 1, 3, 2)):
            src = pieces[core * 5 + i + (m if z == 2 else 0)]
            col = first + (0 if z == 2 else m * CH)
            pltpu.make_async_copy(
                src.at[:, :, pl.ds(col, width)],
                dst.at[pl.ds(core * 3, 3), pl.ds(z * 32, 32), pl.ds(at, width)],
                sem,
            ).start()


def wait_weight(dst, at, width, sem):
    part = dst.at[:, :, pl.ds(at, width)]
    pltpu.make_async_copy(part, part, sem).wait()


def weight(w, at, width):
    return w[:, :, pl.ds(at, width)].reshape(D, width)


def row_starts(info, shape, axis):
    index, buckets, lengths = info
    mp = index[0] & 1
    shift = 7 + buckets[0, mp]
    pos = lax.broadcasted_iota(jnp.int32, shape, axis)
    seq = lax.shift_right_logical(pos, shift)
    within = pos & (lax.shift_left(1, shift) - 1)
    n0, n1, n2, n3 = (lengths[0, mp, i] for i in range(4))
    live = jnp.where(seq == 0, n0, jnp.where(seq == 1, n1, jnp.where(seq == 2, n2, n3)))
    return seq, within < live


def mask_bias(info, key_axis):
    kshape = (T, 1) if key_axis == 0 else (1, T)
    qshape = (1, T) if key_axis == 0 else (T, 1)
    kseq, live = row_starts(info, kshape, key_axis)
    qseq, _ = row_starts(info, qshape, 1 - key_axis)
    kseq = jnp.where(live, kseq, -1)
    return jnp.where(kseq == qseq, 0.0, -1e30)


def attention_kernel(
    index, buckets, lengths, xr, qb, vb, others, p0, p1, p2, p3, p4, p5, p6, p7, p8, p9,
    q, k, v, ctx, lse, w_out, w, qkv, biases, mask, lcol, sem, sem2,
):
    pieces = (p0, p1, p2, p3, p4, p5, p6, p7, p8, p9)
    for m in range(2):
        start_weight(pieces, 0, 3 * HALF, w, m * 3 * HALF, m, sem)
    mask[...] = mask_bias((index, buckets, lengths), 1)
    wait_weight(w, 0, 6 * HALF, sem)
    keep = pltpu.make_async_copy(w, w_out, sem2)
    keep.start()
    zero = jnp.zeros((1, HALF), F32)
    for m in range(2):
        for i, own in enumerate((qb, None, vb)):
            if i == 1:
                b = zero
            elif m == 0:
                b = row_of(own)
            else:
                b = others[pl.ds((i >> 1) * HALF, HALF)].reshape(1, HALF)
            biases[m * 3 + i : m * 3 + i + 1, :] = b

    def project(i, _):
        a = nn(xr[...], weight(w, pl.multiple_of(i * HALF, HALF), HALF)) + biases[pl.ds(i, 1), :]
        scale = jnp.where((i == 0) | (i == 3), 0.125, 1.0)
        qkv[i] = (a.astype(BF).astype(F32) * scale).astype(BF)
        return 0

    lax.fori_loop(0, 6, project, 0, unroll=2)
    for i in range(6):
        (q, k, v)[i % 3][:, (i // 3) * HALF : (i // 3 + 1) * HALF] = qkv[i]
    lcol[...] = jnp.zeros_like(lcol)
    lane = lax.broadcasted_iota(jnp.int32, (1, 128), 1)

    def pair(i, _):
        cols = pl.ds(pl.multiple_of(i * 128, 128), 128)
        q2, k2, v2 = q[:, cols], k[:, cols], v[:, cols]
        total = None
        for half in range(2):
            mine = (lane < 64) if half == 0 else (lane >= 64)
            s = nt(jnp.where(mine, q2, BF(0)), k2) + mask[...]
            peak = jnp.max(s, axis=1, keepdims=True)
            e = jnp.exp(s - peak)
            z = jnp.sum(e, axis=1, keepdims=True)
            p = (e * (1.0 / z)).astype(BF)
            c = nn(p, jnp.where(mine, v2, BF(0)))
            total = c if total is None else total + c
            l = peak + jnp.log(z)
            lcol[...] = jnp.where(lane == i * 2 + half, l, lcol[...])
        ctx[:, cols] = total.astype(BF)
        return 0

    lax.fori_loop(0, 6, pair, 0, unroll=3)
    lse[...] = lcol[...].T[0:16, :]
    keep.wait()


def stats(a):
    mean = jnp.mean(a, axis=1, keepdims=True)
    a = a - mean
    r = lax.rsqrt(jnp.mean(a * a, axis=1, keepdims=True) + EPS)
    return a * r, r


def norm_back(dy, n, r, gain):
    a = dy * gain
    return r * (
        a - jnp.mean(a, axis=1, keepdims=True) - n * jnp.mean(a * n, axis=1, keepdims=True)
    )


def store_rows(own, other, value, cols):
    for core, dst in enumerate((own, other)):
        for g in range(3):
            for z in range(4):
                at = ((core * 3 + g) * 4 + z) * 32
                dst[z, g * 32 : (g + 1) * 32, cols] = value[at : at + 32]


def store_vectors(own, other, value):
    for dst in (own, other):
        for z in range(4):
            dst[z, 96:104, :] = value


def unit_source(f):
    return f < 2, (4 * HALF if f < 2 else 2 * FQ), f & 1


def up_kernel(
    ctx, xr, yr, vr, inb, others, order_b, swap,
    a0, a1, a2, a3, a4, a5, a6, a7, a8, a9, b0, b1, b2, b3, b4, b5, b6, b7, b8, b9,
    out, h1t_out, n1_out, r1, df, da, dinb, sums, slope_out, grads_out, grads1_out,
    wo, wi, wt, hs, hts, biases, n1, gact, slope, big, lowt, grads, grads1, sems, keeps, goes,
):
    ap = (a0, a1, a2, a3, a4, a5, a6, a7, a8, a9)
    bp = (b0, b1, b2, b3, b4, b5, b6, b7, b8, b9)
    for m in range(2):
        start_weight(ap, 3 * HALF, HALF, wo, m * HALF, m, sems.at[0])
    for f in range(4):
        first, col, m = unit_source(f)
        start_weight(ap if first else bp, col, FQ, wi, f * FQ, m, sems.at[1 + f])
        start_weight(bp, (f >> 1) * FQ, FQ, wt, f * FQ, m, sems.at[5 + f])
    wait_weight(wo, 0, D, sems.at[0])
    ob, g1, s1 = (vr[i : i + 1, :] for i in range(3))
    fb, g2, s2 = (vr[i : i + 1, :] for i in range(8, 11))
    nrm, r = stats(nt(ctx[...], weight(wo, 0, D)) + ob + xr[...].astype(F32))
    n1[...] = nrm
    keep = []

    def send(src, dst, sem):
        keep.append(pltpu.make_async_copy(src, dst, sem))
        keep[-1].start()

    send(n1, n1_out, keeps.at[2])
    r1[...] = jnp.broadcast_to(r, (T, 128))
    low = nrm * g1 + s1
    hs[0] = low.astype(BF)
    hts[0] = low.T.astype(BF)
    send(hts.at[0], h1t_out, keeps.at[3])
    low = nn(hs[0], swap[...])
    hs[1] = low.astype(BF)
    hts[1] = low.T.astype(BF)
    big[...] = hs[1].astype(F32) + fb
    for f in range(4):
        bias, at = (inb, 0) if f & 1 == 0 else (others, D)
        biases[f : f + 1, :] = bias[pl.ds(at + (f >> 1) * FQ, FQ)].reshape(1, FQ)

    def up(f, _):
        at = pl.multiple_of(f * FQ, FQ)
        wait_weight(wi, at, FQ, sems.at[1 + f])
        u = nn(hs[f >> 1], weight(wi, at, FQ)) + biases[pl.ds(f, 1), :]
        phi = 0.5 + 0.5 * lax.erf(u * INV_SQRT2)
        slope[f] = phi + u * (jnp.exp(-0.5 * u * u) * INV_SQRT2PI)

        @pl.when(f < 2)
        def _():
            pltpu.make_async_copy(slope.at[f], slope_out.at[f], keeps.at[f]).start()

        g = (u * phi).astype(BF)
        gact[:, pl.ds(at, FQ)] = g
        wait_weight(wt, at, FQ, sems.at[5 + f])
        big[...] += nt(g, weight(wt, at, FQ))
        return 0

    lax.fori_loop(0, 4, up, 0)
    keep += [pltpu.make_async_copy(slope.at[f], slope_out.at[f], keeps.at[f]) for f in range(2)]
    n2, r2 = stats(big[...])
    low = (n2 * g2 + s2).astype(BF)
    out[...] = nt(low, order_b[...]).astype(BF)
    y = yr[...].astype(F32)
    sums[1:2, :] = jnp.sum(y * n2, axis=0, keepdims=True)
    sums[2:3, :] = jnp.sum(y, axis=0, keepdims=True)
    d = norm_back(y, n2, r2, g2)
    big[...] = d
    low = d.astype(BF)
    df[...] = low
    sums[0:1, :] = jnp.sum(low.astype(F32), axis=0, keepdims=True)
    sums[3:8, :] = jnp.zeros((5, D), F32)
    lowt[...] = d.T.astype(BF)

    def go(first, width, sem):
        for k, (src, dst) in enumerate(((grads, grads_out), (grads1, grads1_out))):
            cols = pl.ds(first, width)
            yield pltpu.make_async_copy(src.at[:, :, cols], dst.at[:, :, cols], sem(k))

    def outer(f, _):
        g = nn(lowt[...], gact[:, pl.ds(pl.multiple_of(f * FQ, FQ), FQ)]).astype(BF)
        at = pl.multiple_of((f & 1) * CH + (f >> 1) * FQ, FQ)
        store_rows(grads, grads1, g, pl.ds(at, FQ))

        @pl.when(f >= 2)
        def _():
            for c in go(pl.multiple_of((f & 1) * CH, CH), FHALF, lambda k: goes.at[k, f & 1]):
                c.start()

        return 0

    lax.fori_loop(0, 4, outer, 0)

    def inner(m, _):
        f = m + 2
        at = pl.multiple_of(f * FQ, FQ)
        du = (nn(df[...], weight(wt, at, FQ)) * slope[f]).astype(BF)
        dinb[:, pl.ds(pl.multiple_of(m * FQ, FQ), FQ)] = jnp.sum(
            du.astype(F32), axis=0, keepdims=True
        )
        big[...] += nt(du, weight(wi, at, FQ))
        g = nn(hts[1], du).astype(BF)
        to = pl.multiple_of(m * CH + FHALF, FQ)
        store_rows(grads, grads1, g, pl.ds(to, FQ))
        for c in go(to, FQ, lambda k: goes.at[2 + k, m]):
            c.start()
        return 0

    lax.fori_loop(0, 2, inner, 0)
    for m in range(2):
        keep += list(go(m * CH, FHALF, lambda k, m=m: goes.at[k, m]))
        keep += list(go(m * CH + FHALF, FQ, lambda k, m=m: goes.at[2 + k, m]))
    d = big[...]
    hi = d.astype(BF)
    lo = (d - hi.astype(F32)).astype(BF)
    da[...] = nt(hi, swap[...]) + nt(lo, swap[...])
    for k in keep:
        k.wait()


def down_units(df, wi, wt, slope, big, h1t, dinb, grads, grads1, sems, keeps, slope_in):
    def down(f, _):
        at = pl.multiple_of(f * FQ, FQ)
        wait_weight(wt, at, FQ, sems.at[2 * f])
        pltpu.make_async_copy(slope_in.at[f], slope.at[f], keeps.at[f]).wait()
        du = (nn(df[...], weight(wt, at, FQ)) * slope[f]).astype(BF)
        dinb[pl.ds(f, 1), :] = jnp.sum(du.astype(F32), axis=0, keepdims=True)
        wait_weight(wi, at, FQ, sems.at[2 * f + 1])
        big[...] += nt(du, weight(wi, at, FQ))
        g = nn(h1t[...], du).astype(BF)
        store_rows(grads, grads1, g, pl.ds(pl.multiple_of(f * CQ + HALF, HALF), FQ))
        return 0

    lax.fori_loop(0, 2, down, 0, unroll=2)


def start_units(units, ap, bp, wi, wt, slope_in, slope, sems, keeps):
    for i, f in enumerate(units):
        first, col, m = unit_source(f)
        start_weight(bp, (f >> 1) * FQ, FQ, wt, i * FQ, m, sems.at[2 * i])
        pltpu.make_async_copy(slope_in.at[f], slope.at[i], keeps.at[i]).start()
        start_weight(ap if first else bp, col, FQ, wi, i * FQ, m, sems.at[2 * i + 1])


def down_kernel1(
    h1t, r1, df, dinb, sums, vr, ctx_all, n1_all, da_in, order_a_all, order_b_all, slope_in,
    a0, a1, a2, a3, a4, a5, a6, a7, a8, a9, b0, b1, b2, b3, b4, b5, b6, b7, b8, b9,
    dc, dr, grads, grads1,
    wo, wi, wt, slope, big, lowt, inner, ctx, n1, order_a, order_b, sems, keeps, loads,
):
    ap = (a0, a1, a2, a3, a4, a5, a6, a7, a8, a9)
    bp = (b0, b1, b2, b3, b4, b5, b6, b7, b8, b9)
    start_units((0, 1), ap, bp, wi, wt, slope_in, slope, sems, keeps)
    for m in range(2):
        start_weight(ap, 3 * HALF, HALF, wo, m * HALF, m, sems.at[4])
    copies = [
        pltpu.make_async_copy(src, dst, loads.at[i])
        for i, (src, dst) in enumerate(
            (
                (da_in, big),
                (n1_all, n1),
                (ctx_all, ctx),
                (order_a_all, order_a),
                (order_b_all, order_b),
            )
        )
    ]
    for c in copies:
        c.start()
    copies[0].wait()
    down_units(df, wi, wt, slope, big, h1t, inner, grads, grads1, sems, keeps, slope_in)
    for c in copies[1:]:
        c.wait()
    dh = big[...]
    nrm = n1[...]
    g1 = vr[1:2, :]
    dg1 = jnp.sum(dh * nrm, axis=0, keepdims=True)
    ds1 = jnp.sum(dh, axis=0, keepdims=True)
    d = norm_back(dh, nrm, r1[:, 0:1], g1)
    dr[...] = d
    da = d.astype(BF)
    dob = jnp.sum(da.astype(F32), axis=0, keepdims=True)
    wait_weight(wo, 0, D, sems.at[4])
    dc[...] = nn(da, weight(wo, 0, D)).astype(BF)
    lowt[...] = d.T.astype(BF)
    g = nn(lowt[...], ctx[...]).astype(BF)
    for m in range(2):
        store_rows(grads, grads1, g[:, m * HALF : (m + 1) * HALF], pl.ds(m * CQ, HALF))
    sa = exact(
        jnp.concatenate([dob, dg1, ds1, dob, dob, dob, dob, dob], axis=0),
        order_a[...].astype(F32),
        ((1,), (1,)),
    )
    sb = exact(sums[...], order_b[...].astype(F32), ((1,), (1,)))
    sides = []
    for m in range(2):
        line = jnp.concatenate(
            [inner[m : m + 1, :], dinb[:, m * FQ : (m + 1) * FQ]]
            + [sa[i : i + 1] for i in range(3)]
            + [sb[i : i + 1] for i in range(3)]
            + [jnp.zeros((1, 6 * CQ - 8 * FQ), F32)],
            axis=1,
        )
        rows = [line[:, i * CQ : (i + 1) * CQ] for i in range(6)]
        sides.append(jnp.concatenate(rows + [jnp.zeros((2, CQ), F32)], axis=0))
    store_vectors(grads, grads1, jnp.concatenate(sides, axis=1).astype(BF))


def back_half(
    m, index, buckets, lengths, q, k, v, dc, lse, xb_all, w_all, dr,
    grads, grads1, mask, dqkv, big, qb, vb, xt_ref, w, xb, sems,
):
    copies = [
        pltpu.make_async_copy(w_all.at[:, :, pl.ds(m * 3 * HALF, 3 * HALF)], w, sems.at[0]),
        pltpu.make_async_copy(xb_all, xb, sems.at[1]),
        pltpu.make_async_copy(dr, big, sems.at[2]),
    ]
    for c in copies:
        c.start()
    mask[...] = mask_bias((index, buckets, lengths), 0)
    lane = lax.broadcasted_iota(jnp.int32, (1, 128), 1)

    def pair(i, _):
        head = pl.ds(pl.multiple_of(m * HALF + i * 128, 128), 128)
        cols = pl.ds(pl.multiple_of(i * 128, 128), 128)
        q2, k2, v2, c2 = q[:, head], k[:, head], v[:, head], dc[:, head]
        k2t = k2.astype(F32).T.astype(BF)
        outs = []
        for half in range(2):
            mine = (lane < 64) if half == 0 else (lane >= 64)
            s = nt(jnp.where(mine, k2, BF(0)), q2) + mask[...]
            p = jnp.exp(s - lse[pl.ds(m * 6 + i * 2 + half, 1), :])
            dp = nt(jnp.where(mine, v2, BF(0)), c2)
            delta = jnp.sum(dp * p, axis=0, keepdims=True)
            ds = (p * (dp - delta)).astype(BF)
            outs.append((nn(k2t, ds), nn(ds, q2), nn(p.astype(BF), c2)))
        first = lane < 64
        (qa, ka, va), (qz, kz, vz) = outs
        dq2 = jnp.concatenate([qa[:64], qz[64:]], axis=0).T
        dk2, dv2 = jnp.where(first, ka, kz), jnp.where(first, va, vz)
        dq2 = (dq2 * 0.125).astype(BF)
        dk2 = dk2.astype(BF)
        dv2 = dv2.astype(BF)
        dqkv[0, :, cols] = dq2
        dqkv[1, :, cols] = dk2
        dqkv[2, :, cols] = dv2
        qb[:, cols] = jnp.sum(dq2.astype(F32), axis=0, keepdims=True)
        vb[:, cols] = jnp.sum(dv2.astype(F32), axis=0, keepdims=True)
        return 0

    lax.fori_loop(0, 3, pair, 0, unroll=3)
    for c in copies:
        c.wait()
    xt_ref[...] = xb[...].astype(F32).T.astype(BF)

    def weights(i, _):
        to = pl.multiple_of(i * HALF, HALF)
        a = dqkv[i]
        store_rows(grads, grads1, nn(xt_ref[...], a).astype(BF), pl.ds(to, HALF))
        big[...] += nt(a, weight(w, to, HALF))
        return 0

    lax.fori_loop(0, 3, weights, 0, unroll=3)
    line = jnp.concatenate([qb[...], vb[...], jnp.zeros((1, HALF), F32)], axis=1)
    line = jnp.concatenate([line, jnp.zeros((7, CQ), F32)], axis=0)
    store_vectors(grads, grads1, line.astype(BF))


def back_kernel0(
    index, buckets, lengths, q, k, v, dc, lse, xb, w, dr,
    grads, grads1, out, mask, dqkv, *scratch,
):
    ins = (index, buckets, lengths, q, k, v, dc, lse, xb, w, dr)
    big = scratch[0]
    back_half(0, *ins, grads, grads1, mask, dqkv, *scratch)
    out[...] = big[...]


def back_kernel1(
    index, buckets, lengths, q, k, v, dc, lse, xb, w, dr,
    grads, grads1, gin, mask, dqkv, *scratch,
):
    ins = (index, buckets, lengths, q, k, v, dc, lse, xb, w, dr)
    big = scratch[0]
    back_half(1, *ins, grads, grads1, mask, dqkv, *scratch)
    gin[...] = big[...].astype(BF)


def last_kernel(gin, order, out):
    out[...] = nt(gin[...], order[...]).astype(BF)


def call(kernel, outs, args, scratch=(), vmem=48, flops=0, smem=0, hbm=(), anyouts=()):
    specs = []
    for i in range(len(args)):
        if i < smem:
            specs.append(pl.BlockSpec(memory_space=pltpu.SMEM))
        elif i in hbm:
            specs.append(pl.BlockSpec(memory_space=pl.ANY))
        else:
            specs.append(pl.BlockSpec(memory_space=VMEM))
    return pl.pallas_call(
        kernel,
        out_shape=[jax.ShapeDtypeStruct(s, d) for s, d in outs],
        in_specs=specs,
        out_specs=[
            pl.BlockSpec(memory_space=pl.ANY if i in anyouts else VMEM) for i in range(len(outs))
        ],
        scratch_shapes=list(scratch),
        compiler_params=pltpu.CompilerParams(vmem_limit_bytes=vmem * 2**20),
        cost_estimate=pl.CostEstimate(flops=flops // 1000, bytes_accessed=1000, transcendentals=0),
    )(*args)


def body(
    hidden_in, buckets, lengths, query_weight, key_weight, value_weight, query_bias, value_bias,
    output_weight, output_bias, first_gain, first_shift, inner_weight, inner_bias, outer_weight,
    outer_bias, second_gain, second_shift, cotangent,
):
    mp = lax.axis_index("mp")
    index = lax.axis_index((*DP, "mp")).astype(jnp.int32).reshape(1)
    info = (index, buckets, lengths)
    (shard,) = call(
        pack_kernel,
        [((3, 4, 2 * CH), BF)],
        (query_weight, key_weight, value_weight, output_weight.T, inner_weight, outer_weight.T),
        vmem=60,
    )
    biases = jnp.concatenate([query_bias, value_bias, inner_bias])
    others = flip(biases, "mp", 1)
    def sides(mine, other):
        return jnp.where(
            mp == 0, jnp.concatenate([mine, other], axis=0), jnp.concatenate([other, mine], axis=0)
        )

    square = ((D, D), BF)
    tokens = ((T, D), BF)
    order_a, order_b, swap, xr, xb, yr, vr = call(
        order_kernel,
        [square, square, square, tokens, tokens, tokens, ((16, D), F32)],
        (
            index,
            hidden_in,
            cotangent,
            output_bias,
            first_gain,
            first_shift,
            outer_bias,
            second_gain,
            second_shift,
        ),
        [VMEM((T, D), BF), VMEM((T, D), BF), pltpu.SemaphoreType.DMA((2,))],
        smem=1,
        hbm=(1, 2),
        vmem=60,
        flops=2 * 10**9,
    )
    pa, pb, (xr, xb, yr, others) = gather(shard, (xr, xb, yr, others))
    pa = with_other_core(pa)
    q, k, v, ctx, lse, w = call(
        attention_kernel,
        [tokens, tokens, tokens, tokens, ((16, T), F32), ((6, 128, 6 * HALF), BF)],
        (*info, xr, query_bias, value_bias, others, *pa),
        [
            VMEM((6, 128, 6 * HALF), BF),
            VMEM((6, T, HALF), BF),
            VMEM((8, HALF), F32),
            VMEM((T, T), F32),
            VMEM((T, 128), F32),
            pltpu.SemaphoreType.DMA(()),
            pltpu.SemaphoreType.DMA(()),
        ],
        smem=3,
        hbm=range(7, 17),
        anyouts=(5,),
        vmem=60,
        flops=10 * 10**9,
    )
    ctx, pb[3], pb[4] = lax.optimization_barrier((ctx, pb[3], pb[4]))
    pb = with_other_core(pb)
    gb, ga = ((4, 96, 2 * CH), BF), ((4, 104, 2 * CQ), BF)
    wide = ((T, D), F32)
    out, h1t, n1, r1, df, da, dinb, sums, slope, grads_b, grads_b1 = call(
        up_kernel,
        [
            tokens,
            ((D, T), BF),
            wide,
            ((T, 128), F32),
            tokens,
            wide,
            ((1, 2 * FQ), F32),
            ((8, D), F32),
            ((2, T, FQ), F32),
            gb,
            gb,
        ],
        (ctx, xr, yr, vr, inner_bias, others, order_b, swap, *pa, *pb),
        [
            VMEM((6, 128, D), BF),
            VMEM((6, 128, FF), BF),
            VMEM((6, 128, FF), BF),
            VMEM((2, T, D), BF),
            VMEM((2, D, T), BF),
            VMEM((8, FQ), F32),
            VMEM((T, D), F32),
            VMEM((T, FF), BF),
            VMEM((4, T, FQ), F32),
            VMEM((T, D), F32),
            VMEM((D, T), BF),
            VMEM(*gb),
            VMEM(*gb),
            pltpu.SemaphoreType.DMA((9,)),
            pltpu.SemaphoreType.DMA((4,)),
            pltpu.SemaphoreType.DMA((4, 2)),
        ],
        hbm=range(8, 28),
        anyouts=(1, 2, 8, 9, 10),
        vmem=56,
        flops=8 * 10**9,
    )
    grads_b1 = flip(grads_b1, AC, 1)
    out_own, out = out, flip(out, "mp", 1)
    half = [VMEM((6, 128, 2 * FQ), BF)] * 2 + [VMEM((2, T, FQ), F32), VMEM((T, D), F32)]
    dc, dr, grads_a, grads_a1 = call(
        down_kernel1,
        [tokens, wide, ga, ga],
        (h1t, r1, df, dinb, sums, vr, ctx, n1, da, order_a, order_b, slope, *pa, *pb),
        [VMEM((6, 128, D), BF)]
        + half
        + [
            VMEM((D, T), BF),
            VMEM((8, FQ), F32),
            VMEM((T, D), BF),
            VMEM((T, D), F32),
            VMEM((D, D), BF),
            VMEM((D, D), BF),
            pltpu.SemaphoreType.DMA((5,)),
            pltpu.SemaphoreType.DMA((2,)),
            pltpu.SemaphoreType.DMA((5,)),
        ],
        hbm=range(6, 32),
        vmem=60,
        flops=4 * 10**9,
    )
    b0, b1, b3, bl, br = core_sums([(grads_b, grads_b1)], 96)
    grads_a1 = flip(grads_a1, AC, 1)
    b0, grads_a1 = lax.optimization_barrier((b0, grads_a1))
    a0, a1, a3, al, ar = core_sums([(grads_a, grads_a1)], 104)
    dc, b0, b1, b3, bl, br, a0, a1, a3, al, ar = lax.optimization_barrier(
        (dc, b0, b1, b3, bl, br, a0, a1, a3, al, ar)
    )
    bl, br = flip(bl, AY, 1), flip(br, AY, 3)
    al, ar = flip(al, AZ, 1), flip(ar, AZ, 3)
    gq = ((4, 104, CQ), BF)
    scratch = [
        VMEM((T, T), F32),
        VMEM((3, T, HALF), BF),
        VMEM((T, D), F32),
        VMEM((1, HALF), F32),
        VMEM((1, HALF), F32),
        VMEM((D, T), BF),
        VMEM((6, 128, 3 * HALF), BF),
        VMEM((T, D), BF),
        pltpu.SemaphoreType.DMA((3,)),
    ]
    q00, q01, big = call(
        back_kernel0,
        [gq, gq, wide],
        (*info, q, k, v, dc, lse, xb, w, dr),
        scratch,
        smem=3,
        hbm=(8, 9, 10),
        vmem=34,
        flops=7 * 10**9,
    )
    b1, b3 = relayed((2 * CH,), b1, b3, bl, br)
    a1, a3 = relayed((2 * CQ,), a1, a3, al, ar)
    big, b1, b3, a1, a3, out = lax.optimization_barrier((big, b1, b3, a1, a3, out))
    b1, b3 = flip(b1, AY, 1), flip(b3, AY, 3)
    a1, a3 = flip(a1, AZ, 1), flip(a3, AZ, 3)
    q10, q11, gin = call(
        back_kernel1,
        [gq, gq, tokens],
        (*info, q, k, v, dc, lse, xb, w, big),
        scratch,
        smem=3,
        hbm=(8, 9, 10),
        vmem=34,
        flops=7 * 10**9,
    )
    q01, q11, b1, b3, a1, a3 = lax.optimization_barrier((q01, q11, b1, b3, a1, a3))
    q01, q11 = flip(q01, AC, 1), flip(q11, AC, 1)
    whole, part = ((104, 2 * CQ), BF), ((104, CQ), BF)
    q0, q1, q3, left, right = call(
        pair_kernel, [whole, whole, whole, part, part], (q00, q01, q10, q11), vmem=24
    )
    left, right = flip(left, AY, 1), flip(right, AY, 3)
    q1, q3 = relayed((2 * CQ,), q1, q3, left, right)
    q1, q3 = flip(q1, AY, 1), flip(q3, AY, 3)
    (gin,) = call(last_kernel, [tokens], (gin, order_a), vmem=16)
    theirs = flip(gin, "mp", 1)
    q0, q1, q3, theirs = lax.optimization_barrier((q0, q1, q3, theirs))
    fa = sent(call(second_kernel, [((32, 2 * CQ), BF)] * 4, (a0, a1, a3), vmem=24), AY)
    fa = sent(call(third_kernel, [((20, CQ), BF)] * 4, fa, vmem=24), AX)
    (blocks,) = call(
        last_sums_kernel,
        [((16, 8, 14 * HALF), BF)],
        (index, b0, b1, b3, q0, q1, q3),
        smem=1,
        vmem=32,
    )
    blocks = exchanged(blocks, (*AX, AZ))
    small, inner, vector = ((12, HALF), F32), ((12, FHALF), F32), ((D,), F32)
    half = ((HALF,), F32)
    wq, wk, wv, wo, wi, wt, qb, vb, ib, *vecs = call(
        final_kernel,
        [small] * 4 + [inner] * 2 + [half] * 2 + [((FHALF,), F32)] + [vector] * 6,
        (*fa, blocks),
        vmem=24,
    )
    layer_out = sides(out_own, out)
    input_grad = sides(gin, theirs).astype(F32)
    dob, dg1, ds1, dfb, dg2, ds2 = vecs
    return (
        layer_out, input_grad, wq, wk, wv, qb, vb, wo.T, dob, dg1, ds1, wi, ib, wt.T, dfb, dg2, ds2
    )


def solution(mesh):
    torus = Mesh(
        mesh.devices.reshape(2, 4, 4, 2, mesh.shape["mp"]), ("dp_0", "dp_1", "dp_2", "dp_3", "mp")
    )
    row, col, half = P(DP, "mp"), P("mp", DP), P("mp")
    in_specs = (
        P(DP, None), P(DP, None), P(DP, None, None), row, row, row, half, half, col, P(), P(), P(),
        row, half, col, P(), P(), P(), P(DP, None),
    )
    out_specs = (
        P(DP, None), P(DP, None), row, row, row, half, half, col, P(), P(), P(), row, half, col,
        P(), P(), P(),
    )
    return jax.shard_map(body, mesh=torus, in_specs=in_specs, out_specs=out_specs, check_vma=False)
```
